32 devices in a mesh: seq: 8 (over z, x), batch: 4 (over y, core).
Axes of the slice: x: 2, y: 2, z: 4, core: 2. Of those that a mesh axis runs over, the one named last changes fastest.
Arguments:
- tokens: bfloat16 [8, 2048, 1024], P('batch', 'seq'), may hold values from -6 to 6
- cotangent: bfloat16 [8, 2048, 1024], P('batch', 'seq'), may hold values from -6 to 6
- gate_weight: bfloat16 [1024, 1536], replicated, may hold values from -0.1875 to 0.1875
- branch_weight: bfloat16 [1024, 1536], replicated, may hold values from -0.1875 to 0.1875
- out_weight: bfloat16 [1536, 1024], replicated, may hold values from -0.4375 to 0.4375
- conv_taps: float32 [4, 1536], replicated, may hold values from -3 to 3
- conv_offset: float32 [1536], replicated, may hold values from -3 to 3
- rate_weight: bfloat16 [16, 96, 96], replicated, may hold values from -0.625 to 0.625
- inlet_weight: bfloat16 [16, 96, 96], replicated, may hold values from -0.625 to 0.625
- rate_offset: float32 [1536], replicated, may hold values from -4 to 4
- inlet_offset: float32 [1536], replicated, may hold values from -4 to 4
- decay_param: float32 [1536], replicated, may hold values from -14 to -3.8, as said below
- mixer_gain: float32 [1024], replicated, may hold values from 0.5 to 1.5
- feed_gain: float32 [1024], replicated, may hold values from 0.5 to 1.5
- feed_gate: bfloat16 [1024, 3072], replicated, may hold values from -0.1875 to 0.1875
- feed_up: bfloat16 [1024, 3072], replicated, may hold values from -0.1875 to 0.1875
- feed_down: bfloat16 [3072, 1024], replicated, may hold values from -0.15625 to 0.15625
Outputs:
- block_out: bfloat16 [8, 2048, 1024], P('batch', 'seq')
- tokens_grad: float32 [8, 2048, 1024], P('batch', 'seq')
- gate_grad: float32 [1024, 1536], P('seq')
- branch_grad: float32 [1024, 1536], P('seq')
- out_grad: float32 [1536, 1024], P('seq')
- taps_grad: float32 [4, 1536], replicated
- offset_conv: float32 [1536], replicated
- rate_grad: float32 [16, 96, 96], replicated
- inlet_grad: float32 [16, 96, 96], replicated
- offset_rate: float32 [1536], replicated
- offset_inlet: float32 [1536], replicated
- decay_grad: float32 [1536], replicated
- gain_mixer: float32 [1024], replicated
- gain_feed: float32 [1024], replicated
- gate_feed: float32 [1024, 3072], P('seq')
- up_feed: float32 [1024, 3072], P('seq')
- down_feed: float32 [3072, 1024], P('seq')
The draws below stay inside these ranges and needn't reach their ends.
Inputs may be any that keep to these rules, and one draw needn't show every extreme that they name: `decay_param`: softplus of each entry lies between 0.05 / 2048 and 0.02.
All inputs are finite; a program needn't handle non-finite values.
Results may differ from the reference program's by a relative error of at most 0.012.
Values may be sent and summed in bfloat16 or wider, within the bound.
A program may use at most 256 MiB of HBM per device.

```python
import math
import jax
import jax.numpy as jnp
from jax import lax

D = 1024
R = 1536
F = 3072
BLOCKS = 16
BW = 96
SEQS = 8
LENGTH = 2048


def draw_decay_param(key, part):
    pick_key, position_key = jax.random.split(key)
    slow_share = 0.5
    slow_mask = jax.random.uniform(pick_key, (R,), jnp.float32) < slow_share
    position = jax.random.uniform(position_key, (R,), jnp.float32)
    low_end = jnp.log(0.05 / LENGTH)
    slow_rate = jnp.exp(low_end + position * jnp.log(10.0))
    fast_start = jnp.log(0.5 / LENGTH)
    fast_rate = jnp.exp(fast_start + position * (jnp.log(0.02) - fast_start))
    decay_rate = jnp.where(slow_mask, slow_rate, fast_rate)
    return jnp.log(jnp.expm1(decay_rate)).astype(jnp.float32)


def level_of(key, shape, cuts, least, largest):
    def one(dim, shards_of):
        draws = jax.random.uniform(jax.random.fold_in(jax.random.fold_in(key, 6), dim), (shards_of,), jnp.float32, least / len(cuts), largest / len(cuts))
        return jnp.repeat(jnp.exp(draws), shape[dim] // shards_of).reshape((-1,) + (1,) * (len(shape) - dim - 1))

    level = one(*cuts[0])
    for cut in cuts[1:]:
        level = level * one(*cut)
    return level


def bell_draw(key, extent, deviation, reach, cuts=(), held_as=jnp.bfloat16):
    entries = jax.random.normal(key, extent, jnp.float32) * deviation
    if len(cuts) > 0:
        entries = level_of(key, extent, cuts, -0.22, 0.18) * entries
    return jnp.clip(entries, min=-reach, max=reach).astype(held_as)


def setup_inputs(seed: int = 0) -> dict:
    key_of = jax.random.split(jax.random.key(seed), 18)
    return {
        "tokens": bell_draw(key_of[0], (SEQS, LENGTH, D), 1.0, 6.0, ((0, 4), (1, 8))),
        "cotangent": bell_draw(key_of[1], (SEQS, LENGTH, D), 1.0, 6.0, ((0, 4), (1, 8))),
        "gate_weight": bell_draw(key_of[2], (D, R), D ** -0.5, 0.1875),
        "branch_weight": bell_draw(key_of[3], (D, R), D ** -0.5, 0.1875),
        "out_weight": bell_draw(key_of[4], (R, D), (R // 8) ** -0.5, 0.4375),
        "conv_taps": bell_draw(key_of[5], (4, R), 0.5, 3.0, (), jnp.float32),
        "conv_offset": bell_draw(key_of[6], (R,), 0.5, 3.0, (), jnp.float32),
        "rate_weight": bell_draw(key_of[7], (BLOCKS, BW, BW), BW ** -0.5, 0.625),
        "inlet_weight": bell_draw(key_of[8], (BLOCKS, BW, BW), BW ** -0.5, 0.625),
        "rate_offset": bell_draw(key_of[9], (R,), 1.0, 4.0, (), jnp.float32),
        "inlet_offset": bell_draw(key_of[10], (R,), 1.0, 4.0, (), jnp.float32),
        "decay_param": draw_decay_param(jax.random.fold_in(key_of[17], 71), 0),
        "mixer_gain": jnp.clip(1.0 + 0.1 * jax.random.normal(key_of[12], (D,), jnp.float32), 0.5, 1.5),
        "feed_gain": jnp.clip(1.0 + 0.1 * jax.random.normal(key_of[13], (D,), jnp.float32), 0.5, 1.5),
        "feed_gate": bell_draw(key_of[14], (D, F), D ** -0.5, 0.1875),
        "feed_up": bell_draw(key_of[15], (D, F), D ** -0.5, 0.1875),
        "feed_down": bell_draw(key_of[16], (F, D), (F // 2) ** -0.5, 0.15625),
    }


@jax.custom_vjp
def low(v):
    return lax.optimization_barrier(v.astype(jnp.bfloat16)).astype(jnp.float32)

@jax.custom_vjp
def low_back(v):
    return v

def low_keep(v):
    return (low(v), None)

def low_pass(kept, grad):
    return (grad,)

def back_keep(v):
    return (v, None)

def back_low(kept, grad):
    return (low(grad),)
low.defvjp(low_keep, low_pass)
low_back.defvjp(back_keep, back_low)

def matmul(left, right):
    return jnp.dot(left, right, precision=lax.Precision.HIGHEST)

def rms_norm(values, gain):
    scale = lax.rsqrt(lax.optimization_barrier(jnp.mean(values * values, axis=-1, keepdims=True)) + 1e-06)
    return values * scale * gain

def blockdiag(values, weight):
    shaped = values.reshape(LENGTH, BLOCKS, BW)
    result = jnp.einsum('tbi,bio->tbo', shaped, weight, precision=lax.Precision.HIGHEST)
    return result.reshape(LENGTH, R)

def block_scan(state_now, pieces):

    def advance(state_prev, inputs):
        state_next = inputs[0] * state_prev + inputs[1]
        return (state_next, state_next)
    return lax.scan(advance, state_now, pieces)

def recurrence(decay, drive):
    block_len = math.gcd(LENGTH, 128)
    block_count = LENGTH // block_len
    shaped = (decay.reshape(block_count, block_len, R), drive.reshape(block_count, block_len, R))
    last_state, states = lax.scan(jax.checkpoint(block_scan), jnp.zeros((R,), jnp.float32), shaped)
    return states.reshape(LENGTH, R)

def block_forward(sequence, params):
    gate_weight, branch_weight, out_weight, conv_taps, conv_offset, rate_weight, inlet_weight, rate_offset, inlet_offset, decay_param, mixer_gain, feed_gain, feed_gate, feed_up, feed_down = params
    normed = low(rms_norm(sequence, mixer_gain))
    gate_pre = low_back(matmul(normed, gate_weight))
    branch = low(low_back(matmul(normed, branch_weight)))
    padded = jnp.concatenate([jnp.zeros((3, R), jnp.float32), branch], axis=0)
    convolved = conv_offset + conv_taps[0] * padded[3:]
    for tap_index in range(1, 4):
        convolved = convolved + conv_taps[tap_index] * padded[3 - tap_index:3 - tap_index + LENGTH]
    mixed = low(convolved)
    rate_pre = low_back(blockdiag(mixed, rate_weight)) + rate_offset
    inlet_pre = low_back(blockdiag(mixed, inlet_weight)) + inlet_offset
    rate = jax.nn.sigmoid(rate_pre)
    inlet = jax.nn.sigmoid(inlet_pre)
    log_decay = -8.0 * rate * jax.nn.softplus(decay_param)
    decay = jnp.exp(log_decay)
    drive = jnp.sqrt(-jnp.expm1(2.0 * log_decay)) * inlet * mixed
    states = recurrence(decay, drive)
    joined = low(jax.nn.gelu(gate_pre) * states)
    resid = sequence + low_back(matmul(joined, out_weight))
    normed_two = low(rms_norm(resid, feed_gain))
    up_gate = low_back(matmul(normed_two, feed_gate))
    up_value = low_back(matmul(normed_two, feed_up))
    hidden = low(jax.nn.gelu(up_gate) * up_value)
    return resid + low_back(matmul(hidden, feed_down))

def reference(tokens, cotangent, gate_weight, branch_weight, out_weight, conv_taps, conv_offset, rate_weight, inlet_weight, rate_offset, inlet_offset, decay_param, mixer_gain, feed_gain, feed_gate, feed_up, feed_down):
    params = tuple((value.astype(jnp.float32) for value in (gate_weight, branch_weight, out_weight, conv_taps, conv_offset, rate_weight, inlet_weight, rate_offset, inlet_offset, decay_param, mixer_gain, feed_gain, feed_gate, feed_up, feed_down)))

    def one_sequence(totals, pieces):
        sequence, seq_cotangent = pieces
        result, pullback = jax.vjp(block_forward, sequence.astype(jnp.float32), params)
        seq_grad, param_grads = pullback(seq_cotangent.astype(jnp.float32))
        totals = jax.tree.map(jnp.add, totals, param_grads)
        return (totals, (result.astype(jnp.bfloat16), seq_grad))
    zero_grads = jax.tree.map(jnp.zeros_like, params)
    totals, outputs = lax.scan(one_sequence, zero_grads, (tokens, cotangent))
    return (outputs[0], outputs[1], totals[0], totals[1], totals[2], totals[3], totals[4], totals[5], totals[6], totals[7], totals[8], totals[9], totals[10], totals[11], totals[12], totals[13], totals[14])
```

```python
import functools
import jax
import jax.numpy as jnp
from jax import lax
from jax.experimental import pallas as pl
from jax.experimental.pallas import tpu as pltpu
from jax.sharding import PartitionSpec as P

F32, BF16 = jnp.float32, jnp.bfloat16
VLIM = 56 * 2**20
GELU_A, GELU_B = 0.7978845608028654, 0.044715


def nn(a, b):
    return lax.dot_general(a, b, (((1,), (0,)), ((), ())), preferred_element_type=F32)


def nt(a, b):
    return lax.dot_general(a, b, (((1,), (1,)), ((), ())), preferred_element_type=F32)


def tn(a, b):
    return lax.dot_general(a, b, (((0,), (0,)), ((), ())), preferred_element_type=F32)


def sigmoid(v):
    return 1.0 / (1.0 + jnp.exp(-v))


def drop(u, decay):
    v = 2.0 * u
    series = 1.0 + v * (1.0 / 7.0)
    for k in (6.0, 5.0, 4.0, 3.0, 2.0):
        series = 1.0 + (v * (1.0 / k)) * series
    return jnp.where(v > -0.35, -v * series, 1.0 - decay * decay)


def gelu_parts(v):
    square = v * v
    inner = jnp.tanh(GELU_A * v * (1.0 + GELU_B * square))
    half = 0.5 + 0.5 * inner
    act = v * half
    slope = half + 0.5 * v * (1.0 - inner * inner) * (GELU_A + 3.0 * GELU_A * GELU_B * square)
    return act, slope


def gelu(v):
    inner = jnp.tanh(GELU_A * v * (1.0 + GELU_B * (v * v)))
    return v * (0.5 + 0.5 * inner)


def spread(dense, blocks, count, width):
    for a in range(count):
        parts = []
        if a > 0:
            parts.append(jnp.zeros((width, a * width), dense.dtype))
        parts.append(blocks[a])
        if a < count - 1:
            parts.append(jnp.zeros((width, (count - 1 - a) * width), dense.dtype))
        dense[a * width : (a + 1) * width, :] = jnp.concatenate(parts, axis=1)


def params(sem=("arbitrary",), **kw):
    return pltpu.CompilerParams(dimension_semantics=sem, vmem_limit_bytes=VLIM, **kw)


def whole(shape):
    return pl.BlockSpec(shape, lambda *_: (0,) * len(shape))


def front_kernel(
    seqs, length, tok, halo, gain, gw, bw, taps, coff, wr, wi, roff, ioff, sp,
    normed, gate, branch, edge, mixed, rate, inlet, h, p, carry,
    hn, ext, dr, di, rp, ip,
):
    rows, width = seqs * length, gw.shape[1]
    sub = dr.shape[-1]

    @pl.when(pl.program_id(0) == 0)
    def _():
        def norm(i, _):
            x = tok[pl.ds(i * 32, 32), :].astype(F32)
            r = lax.rsqrt(jnp.mean(x * x, axis=-1, keepdims=True) + 1e-06)
            normed[pl.ds(i * 32, 32), :] = (x * r * gain[...]).astype(BF16)
            return 0

        lax.fori_loop(0, rows // 32, norm, 0)
        x = halo[...].astype(F32)
        r = lax.rsqrt(jnp.mean(x * x, axis=-1, keepdims=True) + 1e-06)
        hn[...] = (x * r * gain[...]).astype(BF16)

    gate[...] = nn(normed[...], gw[...])
    b16 = nn(normed[...], bw[...]).astype(BF16)
    e16 = nn(hn[...], bw[...]).astype(BF16)
    branch[...] = b16
    edge[...] = e16
    for s in range(seqs):
        ext[s, 0:8, :] = e16[8 * s : 8 * s + 8].astype(F32)
        ext[s, 8 : 8 + length, :] = b16[length * s : length * (s + 1)].astype(F32)

    tap = [taps[k : k + 1, :] for k in range(4)]
    off = coff[...]
    for s in range(seqs):

        def conv(i, _):
            x = ext[s, pl.ds(pl.multiple_of(i * 16, 16), 24), :]
            total = off + tap[0] * x[8:24]
            for k in range(1, 4):
                total = total + tap[k] * x[8 - k : 24 - k]
            mixed[pl.ds(pl.multiple_of(s * length + i * 16, 16), 16), :] = total.astype(BF16)
            return 0

        lax.fori_loop(0, length // 16, conv, 0)

    for g in range(width // sub):
        cols = slice(g * sub, (g + 1) * sub)
        spread(dr.at[g], [wr[g * 4 + a] for a in range(4)], 4, wr.shape[-1])
        spread(di.at[g], [wi[g * 4 + a] for a in range(4)], 4, wi.shape[-1])
        rp[:, cols] = nn(mixed[:, cols], dr[g])
        ip[:, cols] = nn(mixed[:, cols], di[g])

    ro, io, slope = roff[...], ioff[...], -8.0 * sp[...]

    def gates(i, _):
        at = pl.ds(pl.multiple_of(i * 16, 16), 16)
        rt = sigmoid(rp[at, :] + ro)
        it = sigmoid(ip[at, :] + io)
        log_decay = rt * slope
        decay = jnp.exp(log_decay)
        rate[at, :] = rt
        inlet[at, :] = it
        p[at, :] = decay
        h[at, :] = jnp.sqrt(drop(log_decay, decay)) * it * mixed[at, :].astype(F32)
        return 0

    lax.fori_loop(0, rows // 16, gates, 0)

    row = lax.broadcasted_iota(jnp.int32, (8, width), 0)

    def scan(i, last):
        out = []
        for s in range(seqs):
            at = pl.ds(pl.multiple_of(s * length + i * 8, 8), 8)
            a, b = p[at, :], h[at, :]
            for d in (1, 2, 4):
                keep = row >= d
                b = b + a * jnp.where(keep, pltpu.roll(b, d, 0), 0.0)
                a = a * jnp.where(keep, pltpu.roll(a, d, 0), 1.0)
            ap, bp = last[s]
            b = b + a * bp
            a = a * ap
            p[at, :] = a
            h[at, :] = b
            out.append((a[7:8], b[7:8]))
        return tuple(out)

    init = tuple((jnp.ones((1, width), F32), jnp.zeros((1, width), F32)) for _ in range(seqs))
    last = lax.fori_loop(0, length // 8, scan, init)
    for s in range(seqs):
        carry[0, s : s + 1, :] = last[s][0]
        carry[1, s : s + 1, :] = last[s][1]


def front(tok, halo, gain, gw, bw, taps, coff, wr, wi, roff, ioff, sp, seqs, length):
    rows, model = tok.shape
    lru = gw.shape[1]
    bw_, per = wr.shape[-1], 8
    width = per * bw_
    sub = 4 * bw_
    n = lru // width
    col = lambda r: pl.BlockSpec((r, width), lambda j: (0, j))
    blk = pl.BlockSpec((per, bw_, bw_), lambda j: (j, 0, 0))
    f = lambda dt: jax.ShapeDtypeStruct((rows, lru), dt)
    return pl.pallas_call(
        functools.partial(front_kernel, seqs, length),
        grid=(n,),
        in_specs=[
            whole((rows, model)), whole(halo.shape), whole((1, model)),
            pl.BlockSpec((model, width), lambda j: (0, j)), pl.BlockSpec((model, width), lambda j: (0, j)),
            col(4), col(1), blk, blk, col(1), col(1), col(1),
        ],
        out_specs=[
            whole((rows, model)), col(rows), col(rows), col(halo.shape[0]), col(rows), col(rows), col(rows), col(rows), col(rows),
            pl.BlockSpec((2, seqs, width), lambda j: (0, 0, j)),
        ],
        out_shape=[
            jax.ShapeDtypeStruct((rows, model), BF16), f(F32), f(BF16),
            jax.ShapeDtypeStruct((halo.shape[0], lru), BF16), f(BF16), f(F32), f(F32), f(F32), f(F32),
            jax.ShapeDtypeStruct((2, seqs, lru), F32),
        ],
        scratch_shapes=[
            pltpu.VMEM(halo.shape, BF16), pltpu.VMEM((seqs, 8 + length, width), F32),
            pltpu.VMEM((2, sub, sub), BF16), pltpu.VMEM((2, sub, sub), BF16),
            pltpu.VMEM((rows, width), F32), pltpu.VMEM((rows, width), F32),
        ],
        compiler_params=params(),
        name="front",
    )(tok, halo, gain, gw, bw, taps, coff, wr, wi, roff, ioff, sp)


def join_kernel(tok, gate, h, p, entry, ow, gain, joined, resid, normed):
    rows = tok.shape[0]
    ent = entry[0]

    def join(i, _):
        at = pl.ds(pl.multiple_of(i * 16, 16), 16)
        state = h[at, :] + p[at, :] * ent
        joined[at, :] = (gelu(gate[at, :]) * state).astype(BF16)
        return 0

    lax.fori_loop(0, rows // 16, join, 0)
    resid[...] = nn(joined[...], ow[...])

    def norm(i, _):
        at = pl.ds(pl.multiple_of(i * 32, 32), 32)
        y = tok[at, :].astype(F32) + resid[at, :]
        resid[at, :] = y
        r = lax.rsqrt(jnp.mean(y * y, axis=-1, keepdims=True) + 1e-06)
        normed[at, :] = (y * r * gain[...]).astype(BF16)
        return 0

    lax.fori_loop(0, rows // 32, norm, 0)


def join(tok, gate, h, p, entry, ow, gain, seqs, length):
    rows, model = tok.shape
    lru = gate.shape[1]
    tile = 128
    per = length // tile
    row = lambda w: pl.BlockSpec((tile, w), lambda i: (i, 0))
    return pl.pallas_call(
        join_kernel,
        grid=(rows // tile,),
        in_specs=[row(model), row(lru), row(lru), row(lru), pl.BlockSpec((1, 1, lru), lambda i: (i // per, 0, 0)), whole((lru, model)), whole((1, model))],
        out_specs=[row(lru), row(model), row(model)],
        out_shape=[jax.ShapeDtypeStruct((rows, lru), BF16), jax.ShapeDtypeStruct((rows, model), F32), jax.ShapeDtypeStruct((rows, model), BF16)],
        compiler_params=params(),
        name="join",
    )(tok, gate, h, p, entry.reshape(seqs, 1, lru), ow, gain)


def feed_kernel(first, who, *refs):
    if first:
        n2, cot, fg, fu, fd, hid, gg, gu, acc, ug, uv, gh = refs
    else:
        n2, cot, fg, fu, fd, start, hid, gg, gu, acc, ug, uv, gh = refs
    rows = n2.shape[0]
    ug[...] = nn(n2[...], fg[...])
    uv[...] = nn(n2[...], fu[...])
    gh[...] = nt(cot[...], fd[...])

    def body(i, _):
        at = pl.ds(pl.multiple_of(i * 16, 16), 16)
        act, slope = gelu_parts(ug[at, :])
        v, g = uv[at, :], gh[at, :]
        hid[at, :] = (act * v).astype(BF16)
        gg[at, :] = (g * v * slope).astype(BF16)
        gu[at, :] = (g * act).astype(BF16)
        return 0

    lax.fori_loop(0, rows // 16, body, 0)

    @pl.when(pl.program_id(0) == 0)
    def _():
        if first:
            acc[...] = jnp.zeros_like(acc)
        else:
            acc[...] = start[...]

    acc[...] += nt(gg[...], fg[...]) + nt(gu[...], fu[...])


def feed(half, n2, cot, fg, fu, fd, start):
    rows, model = n2.shape
    units = fg.shape[1]
    tile = 512
    n = units // 2 // tile
    first = start is None
    out = lambda: pl.BlockSpec((rows, tile), lambda i, w: (0, i))
    ins = [
        whole((rows, model)), whole((rows, model)),
        pl.BlockSpec((model, tile), lambda i, w: (0, w[0] * n + i)), pl.BlockSpec((model, tile), lambda i, w: (0, w[0] * n + i)),
        pl.BlockSpec((tile, model), lambda i, w: (w[0] * n + i, 0)),
    ]
    args = [n2, cot, fg, fu, fd]
    if not first:
        ins.append(whole((rows, model)))
        args.append(start)
    return pl.pallas_call(
        functools.partial(feed_kernel, first),
        grid_spec=pltpu.PrefetchScalarGridSpec(
            num_scalar_prefetch=1, grid=(n,), in_specs=ins, out_specs=[out(), out(), out(), whole((rows, model))],
            scratch_shapes=[pltpu.VMEM((rows, tile), F32)] * 3,
        ),
        out_shape=[jax.ShapeDtypeStruct((rows, units // 2), BF16)] * 3 + [jax.ShapeDtypeStruct((rows, model), F32)],
        compiler_params=params(),
        name="feed_a" if first else "feed_b",
    )(half, *args)


def block_out(half, resid, hid_a, hid_b, fd):
    rows, model = resid.shape
    units = fd.shape[0]
    tile = 256

    def kernel(w, r, ha, hb, fa, fb, out):
        out[...] = (r[...] + nn(ha[...], fa[...]) + nn(hb[...], fb[...])).astype(BF16)

    col = lambda: pl.BlockSpec((rows, tile), lambda i, w: (0, i))
    return pl.pallas_call(
        kernel,
        grid_spec=pltpu.PrefetchScalarGridSpec(
            num_scalar_prefetch=1, grid=(model // tile,),
            in_specs=[
                col(), whole((rows, units // 2)), whole((rows, units // 2)),
                pl.BlockSpec((units // 2, tile), lambda i, w: (1 - w[0], i)), pl.BlockSpec((units // 2, tile), lambda i, w: (w[0], i)),
            ],
            out_specs=col(),
        ),
        out_shape=jax.ShapeDtypeStruct((rows, model), BF16),
        compiler_params=params(),
        name="block_out",
    )(half, resid, hid_a, hid_b, fd, fd)


def turn_kernel(
    seqs, length, who, gn, resid, cot, fgain, ow, gate, h, p, entry, rate, sp,
    gres, glow, gain_sum, gg_theirs, gg_mine, lc, q, carry,
    gj,
):
    step = pl.program_id(0)
    rows, width = gj.shape
    model = gn.shape[1]

    @pl.when(step == 0)
    def _():
        g = fgain[...]

        def norm(i, total):
            at = pl.ds(pl.multiple_of(i * 16, 16), 16)
            y, d = resid[at, :], gn[at, :]
            r = lax.rsqrt(jnp.mean(y * y, axis=-1, keepdims=True) + 1e-06)
            dg, yr = d * g, y * r
            dot = jnp.mean(dg * yr, axis=-1, keepdims=True)
            out = cot[at, :].astype(F32) + r * (dg - yr * dot)
            gres[at, :] = out
            glow[at, :] = out.astype(BF16)
            add = d * yr
            return total + add[0:8] + add[8:16]

        total = lax.fori_loop(0, rows // 16, norm, jnp.zeros((8, model), F32))
        gain_sum[...] = jnp.sum(total, axis=0, keepdims=True)

    gj[...] = nt(glow[...], ow[...])
    slope = -8.0 * sp[...]

    def act_part(store):
        for s in range(seqs):
            ent = entry[s]

            def body(i, _):
                at = pl.ds(pl.multiple_of(s * length + i * 16, 16), 16)
                act, der = gelu_parts(gate[at, :])
                state = h[at, :] + p[at, :] * ent
                d = gj[at, :]
                store[at, :] = (d * state * der).astype(BF16)
                gj[at, :] = d * act
                return 0

            lax.fori_loop(0, length // 16, body, 0)

    @pl.when(step == 0)
    def _():
        act_part(gg_theirs)

    @pl.when(step == 1)
    def _():
        act_part(gg_mine)

    row = lax.broadcasted_iota(jnp.int32, (8, width), 0)
    tiles = length // 8

    def scan(k, last):
        i = tiles - 1 - k
        out = []
        for s in range(seqs):
            at = pl.ds(pl.multiple_of(s * length + i * 8, 8), 8)
            g = gj[at, :]
            a = jnp.exp(rate[at, :] * slope)
            b = a * g
            for d in (1, 2, 4):
                keep = row < 8 - d
                b = b + a * jnp.where(keep, pltpu.roll(b, 8 - d, 0), 0.0)
                a = a * jnp.where(keep, pltpu.roll(a, 8 - d, 0), 1.0)
            ap, bp = last[s]
            b = b + a * bp
            a = a * ap
            lc[at, :] = g + jnp.where(row < 7, pltpu.roll(b, 7, 0), bp)
            q[at, :] = jnp.where(row < 7, pltpu.roll(a, 7, 0), ap)
            out.append((a[0:1], b[0:1]))
        return tuple(out)

    init = tuple((jnp.ones((1, width), F32), jnp.zeros((1, width), F32)) for _ in range(seqs))
    last = lax.fori_loop(0, tiles, scan, init)
    for s in range(seqs):
        carry[0, s : s + 1, :] = last[s][0]
        carry[1, s : s + 1, :] = last[s][1]


def turn(half, gn, resid, cot, fgain, ow, gate, h, p, entry, rate, sp, seqs, length):
    rows, model = gn.shape
    lru = gate.shape[1]
    width = lru // 2
    grp = lambda i, w: (1 - i) * (1 - w[0]) + i * w[0]
    col = lambda r: pl.BlockSpec((r, width), lambda i, w: (0, grp(i, w)))
    three = lambda a: pl.BlockSpec((a, seqs, width), lambda i, w: (0, 0, grp(i, w)))
    half_shape = jax.ShapeDtypeStruct((rows, width), BF16)
    f = lambda dt: jax.ShapeDtypeStruct((rows, lru), dt)
    return pl.pallas_call(
        functools.partial(turn_kernel, seqs, length),
        grid_spec=pltpu.PrefetchScalarGridSpec(
            num_scalar_prefetch=1, grid=(2,),
            in_specs=[
                whole((rows, model)), whole((rows, model)), whole((rows, model)), whole((1, model)),
                pl.BlockSpec((width, model), lambda i, w: (grp(i, w), 0)),
                col(rows), col(rows), col(rows), pl.BlockSpec((seqs, 1, width), lambda i, w: (0, 0, grp(i, w))), col(rows), col(1),
            ],
            out_specs=[
                whole((rows, model)), whole((rows, model)), whole((1, model)),
                whole((rows, width)), whole((rows, width)), col(rows), col(rows), three(2),
            ],
            scratch_shapes=[pltpu.VMEM((rows, width), F32)],
        ),
        out_shape=[
            jax.ShapeDtypeStruct((rows, model), F32), jax.ShapeDtypeStruct((rows, model), BF16), jax.ShapeDtypeStruct((1, model), F32),
            half_shape, half_shape, f(F32), f(F32), jax.ShapeDtypeStruct((2, seqs, lru), F32),
        ],
        compiler_params=params(),
        name="turn",
    )(half, gn, resid, cot, fgain, ow, gate, h, p, entry.reshape(seqs, 1, lru), rate, sp)


def gates_kernel(
    seqs, length, lc, q, cin, h, p, entry, rate, inlet, mixed, branch, edge, wr, wi, taps, sp, sg,
    gb, head, tail, rate_sum, inlet_sum, taps_sum, vec_sum,
    dr, di, gr, gi, gm, ext,
):
    rows, width = gm.shape[0] * 0 + seqs * length, wr.shape[0] * wr.shape[1]
    sub = dr.shape[-1]
    bw_ = wr.shape[-1]
    soft, sgm = sp[...], sg[...]
    slope = -8.0 * soft
    zero = jnp.zeros((8, width), F32)
    row = lax.broadcasted_iota(jnp.int32, (16, width), 0)

    sums = (zero, zero, zero)
    for s in range(seqs):
        c_in, ent = cin[s], entry[s]

        def body(i, carry):
            (before, t0, t1, t2) = carry
            at = pl.ds(pl.multiple_of(s * length + i * 16, 16), 16)
            state = h[at, :] + p[at, :] * ent
            prev = jnp.where(row > 0, pltpu.roll(state, 1, 0), before)
            carried = lc[at, :] + q[at, :] * c_in
            rt, it, mx = rate[at, :], inlet[at, :], mixed[at, :].astype(F32)
            log_decay = rt * slope
            decay = jnp.exp(log_decay)
            gap = drop(log_decay, decay)
            inv = lax.rsqrt(gap)
            nf = gap * inv
            im = it * mx
            g_log = carried * decay * (prev - im * decay * inv)
            cn = carried * nf
            g_rt = g_log * slope * (rt * (1.0 - rt))
            g_it = cn * im * (1.0 - it)
            gr[at, :] = g_rt.astype(BF16)
            gi[at, :] = g_it.astype(BF16)
            gm[s, pl.ds(pl.multiple_of(i * 16, 16), 16), :] = cn * it
            lr = g_log * rt
            return (state[15:16], t0 + lr[0:8] + lr[8:16], t1 + g_rt[0:8] + g_rt[8:16], t2 + g_it[0:8] + g_it[8:16])

        _, *sums = lax.fori_loop(0, length // 16, body, (ent, *sums))
        sums = tuple(sums)
    down = lambda v: jnp.sum(v, axis=0, keepdims=True)
    vec_sum[0:1, :] = down(sums[0]) * (-8.0 * sgm)
    vec_sum[1:2, :] = down(sums[1])
    vec_sum[2:3, :] = down(sums[2])

    for g in range(width // sub):
        cols = slice(g * sub, (g + 1) * sub)
        spread(dr.at[g], [wr[g * 4 + a] for a in range(4)], 4, bw_)
        spread(di.at[g], [wi[g * 4 + a] for a in range(4)], 4, bw_)
        back = nt(gr[:, cols], dr[g]) + nt(gi[:, cols], di[g])
        rs = tn(mixed[:, cols], gr[:, cols])
        is_ = tn(mixed[:, cols], gi[:, cols])
        for a in range(4):
            cut = slice(a * bw_, (a + 1) * bw_)
            rate_sum[g * 4 + a] = rs[cut, cut]
            inlet_sum[g * 4 + a] = is_[cut, cut]
        for s in range(seqs):
            gm[s, 0:length, cols] += back[s * length : (s + 1) * length]

    for s in range(seqs):
        gm[s, length : length + 8, :] = zero
        ext[s, 0:8, :] = edge[8 * s : 8 * s + 8].astype(F32)
        ext[s, 8 : 8 + length, :] = branch[s * length : (s + 1) * length].astype(F32)
        head[8 * s : 8 * s + 8, :] = gm[s, 0:8, :]

    tap = [taps[k : k + 1, :] for k in range(4)]
    acc = (zero,) * 5
    for s in range(seqs):

        def conv(i, acc):
            lo = pl.multiple_of(i * 16, 16)
            y = gm[s, pl.ds(lo, 24), :]
            x = ext[s, pl.ds(lo, 24), :]
            total = tap[0] * y[0:16]
            for k in range(1, 4):
                total = total + tap[k] * y[k : k + 16]
            gb[pl.ds(pl.multiple_of(s * length + i * 16, 16), 16), :] = total.astype(BF16)
            now = y[0:16]
            new = []
            for k in range(4):
                prod = now * x[8 - k : 24 - k]
                new.append(acc[k] + prod[0:8] + prod[8:16])
            new.append(acc[4] + now[0:8] + now[8:16])
            return tuple(new)

        acc = lax.fori_loop(0, length // 16, conv, acc)
        y = gm[s, length - 16 : length + 8, :]
        total = tap[0] * y[0:16]
        for k in range(1, 4):
            total = total + tap[k] * y[k : k + 16]
        tail[16 * s : 16 * s + 16, :] = total
    for k in range(4):
        taps_sum[k : k + 1, :] = down(acc[k])
    vec_sum[3:4, :] = down(acc[4])


def gates_back(lc, q, cin, h, p, entry, rate, inlet, mixed, branch, edge, wr, wi, taps, sp, sg, seqs, length):
    rows, lru = lc.shape
    bw_ = wr.shape[-1]
    per = 8
    width = per * bw_
    sub = 4 * bw_
    n = lru // width
    col = lambda r: pl.BlockSpec((r, width), lambda j: (0, j))
    vec = pl.BlockSpec((seqs, 1, width), lambda j: (0, 0, j))
    blk = pl.BlockSpec((per, bw_, bw_), lambda j: (j, 0, 0))
    out = lambda r, dt=F32: jax.ShapeDtypeStruct((r, lru), dt)
    return pl.pallas_call(
        functools.partial(gates_kernel, seqs, length),
        grid=(n,),
        in_specs=[
            col(rows), col(rows), vec, col(rows), col(rows), vec, col(rows), col(rows), col(rows), col(rows), col(edge.shape[0]),
            blk, blk, col(4), col(1), col(1),
        ],
        out_specs=[col(rows), col(8 * seqs), col(16 * seqs), blk, blk, col(4), col(4)],
        out_shape=[out(rows, BF16), out(8 * seqs), out(16 * seqs), jax.ShapeDtypeStruct(wr.shape, F32), jax.ShapeDtypeStruct(wi.shape, F32), out(4), out(4)],
        scratch_shapes=[
            pltpu.VMEM((2, sub, sub), BF16), pltpu.VMEM((2, sub, sub), BF16), pltpu.VMEM((rows, width), BF16), pltpu.VMEM((rows, width), BF16),
            pltpu.VMEM((seqs, length + 8, width), F32), pltpu.VMEM((seqs, length + 8, width), F32),
        ],
        compiler_params=params(),
        name="gates_back",
    )(lc, q, cin.reshape(seqs, 1, lru), h, p, entry.reshape(seqs, 1, lru), rate, inlet, mixed, branch, edge, wr, wi, taps, sp, sg)


def seam_kernel(seqs, length, who, gb, tail, ahead, taps, theirs, mine):
    step = pl.program_id(0)

    def write(out):
        out[...] = gb[...]
        for s in range(seqs):
            y = ahead[8 * s : 8 * s + 8, :]
            t = tail[16 * s : 16 * s + 16, :]
            grown = jnp.concatenate([jnp.zeros((16, t.shape[1]), F32), y], axis=0)
            for k in range(1, 4):
                t = t + taps[k : k + 1, :] * grown[k : k + 16]
            out[(s + 1) * length - 16 : (s + 1) * length, :] = t.astype(BF16)

    @pl.when(step == 0)
    def _():
        write(theirs)

    @pl.when(step == 1)
    def _():
        write(mine)


def seam(half, gb, tail, ahead, taps, seqs, length):
    rows, lru = gb.shape
    width = lru // 2
    grp = lambda i, w: (1 - i) * (1 - w[0]) + i * w[0]
    col = lambda r: pl.BlockSpec((r, width), lambda i, w: (0, grp(i, w)))
    out = jax.ShapeDtypeStruct((rows, width), BF16)
    return pl.pallas_call(
        functools.partial(seam_kernel, seqs, length),
        grid_spec=pltpu.PrefetchScalarGridSpec(
            num_scalar_prefetch=1, grid=(2,), in_specs=[col(rows), col(16 * seqs), col(8 * seqs), col(4)],
            out_specs=[whole((rows, width)), whole((rows, width))],
        ),
        out_shape=[out, out],
        compiler_params=params(),
        name="seam",
    )(half, gb, tail, ahead, taps)


def input_grad(half, gg_theirs, gg_mine, gb_theirs, gb_mine, gw, bw, tok, gres, gain):
    rows, model = tok.shape
    width = gg_mine.shape[1]
    tile = 128

    def kernel(w, gt, gm, bt, bm, gwt, gwm, bwt, bwm, x_ref, gr, g_ref, out, gain_sum):
        d = nt(gt[...], gwt[...]) + nt(gm[...], gwm[...]) + nt(bt[...], bwt[...]) + nt(bm[...], bwm[...])
        x = x_ref[...].astype(F32)
        r = lax.rsqrt(jnp.mean(x * x, axis=-1, keepdims=True) + 1e-06)
        xr, dg = x * r, d * g_ref[...]
        out[...] = gr[...] + r * (dg - xr * jnp.mean(dg * xr, axis=-1, keepdims=True))
        part = jnp.sum(d * xr, axis=0, keepdims=True)

        @pl.when(pl.program_id(0) == 0)
        def _():
            gain_sum[...] = part

        @pl.when(pl.program_id(0) > 0)
        def _():
            gain_sum[...] += part

    row = lambda c: pl.BlockSpec((tile, c), lambda i, w: (i, 0))
    theirs = pl.BlockSpec((model, width), lambda i, w: (0, 1 - w[0]))
    mine = pl.BlockSpec((model, width), lambda i, w: (0, w[0]))
    return pl.pallas_call(
        kernel,
        grid_spec=pltpu.PrefetchScalarGridSpec(
            num_scalar_prefetch=1, grid=(rows // tile,),
            in_specs=[row(width), row(width), row(width), row(width), theirs, mine, theirs, mine, row(model), row(model), whole((1, model))],
            out_specs=[row(model), whole((1, model))],
        ),
        out_shape=[jax.ShapeDtypeStruct((rows, model), F32), jax.ShapeDtypeStruct((1, model), F32)],
        compiler_params=params(),
        name="input_grad",
    )(half, gg_theirs, gg_mine, gb_theirs, gb_mine, gw, gw, bw, bw, tok, gres, gain)


def place_of(core, s, y):
    x, high, low = s % 2, s // 4, (s // 2) % 2
    return (1 - core) * (x * 8 + high * 4 + y * 2 + low) + core * (y * 8 + x * 4 + high * 2 + low)


def put_pieces(out, acc, core, y, first, count):
    part, cols = acc.shape[0] // count, acc.shape[1]
    for j in range(count):
        at = place_of(core, first + j, y)
        for t in range(cols // 128):
            out[at, t * part : (t + 1) * part, :] = acc[j * part : (j + 1) * part, t * 128 : (t + 1) * 128].astype(BF16)


def wgrad(half, lhs, lhs_far, rhs, rhs_far, own_columns, name):
    rows, deep = lhs.shape
    wide = rhs.shape[1] if own_columns else rhs.shape[1] // 2
    tile = wide // 2

    def kernel(w, a, b, c, d, out):
        acc = tn(a[...], c[...]) + tn(b[...], d[...])
        put_pieces(out, acc, w[0], pl.program_id(0), 0, 8)

    base = (lambda w: 0) if own_columns else (lambda w: 2 * w[0])
    right = lambda: pl.BlockSpec((rows, tile), lambda y, w: (0, base(w) + y))
    shape = (16, deep // 8 * (tile // 128), 128)
    return pl.pallas_call(
        kernel,
        grid_spec=pltpu.PrefetchScalarGridSpec(
            num_scalar_prefetch=1, grid=(2,), in_specs=[whole(lhs.shape), whole(lhs.shape), right(), right()], out_specs=whole(shape),
        ),
        out_shape=jax.ShapeDtypeStruct(shape, BF16),
        compiler_params=params(),
        name=name,
    )(half, lhs, lhs_far, rhs, rhs_far)


def wgrad_down(half, theirs, mine, far_theirs, far_mine, cot, cot_far):
    rows, units = mine.shape
    tile = cot.shape[1] // 4

    def kernel(w, ht, hm, ft, fm, c, d, out):
        i, y = pl.program_id(0), pl.program_id(1)

        @pl.when(i == 0)
        def _():
            put_pieces(out, tn(ht[...], c[...]) + tn(fm[...], d[...]), w[0], y, 4 * (1 - w[0]), 4)

        @pl.when(i == 1)
        def _():
            put_pieces(out, tn(hm[...], c[...]) + tn(ft[...], d[...]), w[0], y, 4 * w[0], 4)

    right = lambda: pl.BlockSpec((rows, tile), lambda i, y, w: (0, 2 * w[0] + y))
    shape = (16, units // 4 * (tile // 128), 128)
    return pl.pallas_call(
        kernel,
        grid_spec=pltpu.PrefetchScalarGridSpec(
            num_scalar_prefetch=1, grid=(2, 2), in_specs=[whole(mine.shape)] * 4 + [right(), right()], out_specs=whole(shape),
        ),
        out_shape=jax.ShapeDtypeStruct(shape, BF16),
        compiler_params=params(("arbitrary", "arbitrary")),
        name="wgrad_down",
    )(half, theirs, mine, far_theirs, far_mine, cot, cot_far)


MESH = pl.DeviceIdType.MESH


def meet(peers):
    barrier = pltpu.get_barrier_semaphore()
    for peer in peers:
        pl.semaphore_signal(barrier, inc=1, device_id=peer, device_id_type=MESH)
    pl.semaphore_wait(barrier, len(peers))


def entry_state(part, n, reverse, collective_id):
    _, seqs, lru = part.shape

    def kernel(mine, out, got, send, recv):
        me, b = lax.axis_index("seq"), lax.axis_index("batch")
        peers = [(lax.rem(me + k, n), b) for k in range(1, n)]
        meet(peers)
        copies = []
        for k in range(1, n):
            copy = pltpu.make_async_remote_copy(
                src_ref=mine, dst_ref=got.at[me], send_sem=send.at[k], recv_sem=recv.at[k],
                device_id=peers[k - 1], device_id_type=MESH,
            )
            copy.start()
            copies.append(copy)
        got[me] = mine[...]
        for copy in copies:
            copy.wait()

        def one(k, state):
            j = n - 1 - k if reverse else k
            before = (j > me) if reverse else (j < me)
            return jnp.where(before, got[j, 0] * state + got[j, 1], state)

        out[...] = lax.fori_loop(0, n, one, jnp.zeros((seqs, lru), F32))

    return pl.pallas_call(
        kernel,
        in_specs=[pl.BlockSpec(memory_space=pltpu.VMEM)],
        out_specs=pl.BlockSpec(memory_space=pltpu.VMEM),
        out_shape=jax.ShapeDtypeStruct((seqs, lru), F32),
        scratch_shapes=[pltpu.VMEM((n, 2, seqs, lru), F32), pltpu.SemaphoreType.DMA((n,)), pltpu.SemaphoreType.DMA((n,))],
        compiler_params=pltpu.CompilerParams(collective_id=collective_id, has_side_effects=True, vmem_limit_bytes=VLIM),
        name="entry_back" if reverse else "entry",
    )(part)


def flip(index, bit):
    return index + bit - 2 * bit * (lax.rem(index // bit, 2))


def sum_all(value, seq, batch, collective_id):
    rows = value.shape[0]
    steps = [("batch", 1 << k) for k in range(batch.bit_length() - 1)] + [("seq", 1 << k) for k in range(seq.bit_length() - 1)]

    def kernel(v, out, got, send, recv):
        s, b = lax.axis_index("seq"), lax.axis_index("batch")
        peers = [(flip(s, bit), b) if axis == "seq" else (s, flip(b, bit)) for axis, bit in steps]
        meet(peers)
        copies = []
        got[0] = v[...]
        for k, peer in enumerate(peers):
            copy = pltpu.make_async_remote_copy(
                src_ref=got.at[2 * k], dst_ref=got.at[2 * k + 1], send_sem=send.at[k], recv_sem=recv.at[k], device_id=peer, device_id_type=MESH,
            )
            copy.start()
            copy.wait()
            got[2 * k + 2] = got[2 * k] + got[2 * k + 1]
        out[...] = got[2 * len(steps)]

    n = len(steps)
    return pl.pallas_call(
        kernel,
        in_specs=[pl.BlockSpec(memory_space=pltpu.VMEM)],
        out_specs=pl.BlockSpec(memory_space=pltpu.VMEM),
        out_shape=jax.ShapeDtypeStruct(value.shape, F32),
        scratch_shapes=[pltpu.VMEM((2 * n + 1, rows, 128), F32), pltpu.SemaphoreType.DMA((n,)), pltpu.SemaphoreType.DMA((n,))],
        compiler_params=pltpu.CompilerParams(collective_id=collective_id, has_side_effects=True, vmem_limit_bytes=VLIM),
        name="sum_all",
    )(value)


def scatter_sum(pieces, cut, collective_id, name):
    count, rows = len(pieces), pieces[0].shape[1]
    part = rows // cut
    chunks = count * cut

    def kernel(*refs):
        ins, out = refs[:count], refs[count]
        keep, r1, r2, r3, r4, send, recv, local, back = refs[count + 1 :]
        seq, bat = lax.axis_index("seq"), lax.axis_index("batch")
        core, y = lax.rem(bat, 2), bat // 2
        x, low, high = lax.rem(seq, 2), lax.rem(seq // 2, 2), seq // 4
        pick = lambda a, b: (1 - core) * a + core * b
        ex, elow, ehigh, ey = 1 - 2 * x, 2 - 4 * low, 4 - 8 * high, 2 - 4 * y
        bits = [pick(x, y), pick(high, x), pick(y, high), low]
        peers = [
            (seq + (1 - core) * ex, bat + core * ey),
            (seq + pick(ehigh, ex), bat),
            (seq + core * ehigh, bat + (1 - core) * ey),
            (seq + elow, bat),
            (seq, bat + ey),
            (seq, bat + 1 - 2 * core),
        ]
        meet([(seq + ex, bat), (seq + ehigh, bat), (seq + elow, bat), (seq, bat + ey), (seq, bat + 1 - 2 * core)])
        got = [r1, r2, r3, r4]

        def where(q):
            return q // cut, slice((q % cut) * part, (q % cut + 1) * part)

        def remote(k, q, src, dst):
            return pltpu.make_async_remote_copy(
                src_ref=src, dst_ref=dst, send_sem=send.at[k, q], recv_sem=recv.at[k, q], device_id=peers[k], device_id_type=MESH,
            )

        def copy_of(k, q):
            m, at = where(q)
            if k == 0:
                return remote(0, q, ins[m].at[pl.ds((1 - bits[0]) * 8, 8), at], r1.at[q])
            if k < 4:
                size = 8 >> k
                return remote(k, q, got[k - 1].at[q, pl.ds((1 - bits[k]) * size, size)], got[k].at[q])
            if k == 4:
                slot = out.at[m, core, y, at]
                return remote(4, q, slot, slot)
            slot = out.at[m, core, :, at]
            return remote(5, q, slot, slot)

        def keep_copy(q):
            m, at = where(q)
            return pltpu.make_async_copy(ins[m].at[pl.ds(bits[0] * 8, 8), at], keep.at[q], local.at[q])

        def add(dst, q, base, src, sbase, size):
            for j in range(size):

                def body(i, _):
                    a = pl.ds(pl.multiple_of(i * 64, 64), 64)
                    dst[q, base + j, a, :] = (dst[q, base + j, a, :].astype(F32) + src[q, sbase + j, a, :].astype(F32)).astype(BF16)
                    return 0

                lax.fori_loop(0, part // 64, body, 0)

        def stage(k, q):
            if k < 4:
                size = 8 >> k
                if k == 0:
                    keep_copy(q).wait()
                    src, sbase = keep, 0
                else:
                    src, sbase = got[k - 1], bits[k] * size
                copy_of(k, q).wait_recv()
                if k < 3:
                    half = size // 2
                    far, near = (1 - bits[k + 1]) * half, bits[k + 1] * half
                    add(got[k], q, far, src, sbase + far, half)
                    copy_of(k + 1, q).start()
                    add(got[k], q, near, src, sbase + near, half)
                else:
                    m, at = where(q)

                    def body(i, _):
                        a = pl.ds(pl.multiple_of(i * 64, 64), 64)
                        o = pl.ds(pl.multiple_of(at.start + i * 64, 64), 64)
                        out[m, core, y, o, :] = (r4[q, 0, a, :].astype(F32) + r3[q, sbase, a, :].astype(F32)).astype(BF16)
                        return 0

                    lax.fori_loop(0, part // 64, body, 0)
                    copy_of(4, q).start()
            elif k == 4:
                copy_of(4, q).wait()
                copy_of(5, q).start()
            else:
                copy_of(5, q).wait()

        for t in range(chunks + 8):
            for k in range(5, -1, -1):
                q = t - 2 - k
                if 0 <= q < chunks:
                    stage(k, q)
            if t < chunks:
                copy_of(0, t).start()
                keep_copy(t).start()
        for q in range(chunks):
            for k in range(4):
                copy_of(k, q).wait_send()

    hbm = pl.BlockSpec(memory_space=pl.ANY)
    buf = lambda n: pltpu.VMEM((chunks, n, part, 128), BF16)
    return pl.pallas_call(
        kernel,
        in_specs=[hbm] * count,
        out_specs=pl.BlockSpec(memory_space=pltpu.VMEM),
        out_shape=jax.ShapeDtypeStruct((count, 2, 2, rows, 128), BF16),
        scratch_shapes=[
            buf(8), buf(8), buf(4), buf(2), buf(1),
            pltpu.SemaphoreType.DMA((6, chunks)), pltpu.SemaphoreType.DMA((6, chunks)), pltpu.SemaphoreType.DMA((chunks,)), pltpu.SemaphoreType.DMA((1,)),
        ],
        compiler_params=pltpu.CompilerParams(collective_id=collective_id, has_side_effects=True, vmem_limit_bytes=VLIM),
        name=name,
    )(*pieces)


def shifted(value, axis, steps):
    count = lax.axis_size(axis)
    return lax.ppermute(value, axis, [(i, i + steps) for i in range(count) if 0 <= i + steps < count])


def swap(value):
    count = lax.axis_size("batch")
    return lax.ppermute(value, "batch", [(i, i ^ 1) for i in range(count)])


def local(
    tokens, cotangent, gate_weight, branch_weight, out_weight, conv_taps, conv_offset, rate_weight, inlet_weight,
    rate_offset, inlet_offset, decay_param, mixer_gain, feed_gain, feed_gate, feed_up, feed_down,
):
    seqs, length, model = tokens.shape
    lru, units = gate_weight.shape[1], feed_gate.shape[1]
    rows = seqs * length
    seq_n, batch_n = lax.axis_size("seq"), lax.axis_size("batch")
    core = lax.rem(lax.axis_index("batch"), 2)
    half = jnp.full((1,), core, jnp.int32)

    halo = shifted(tokens[:, length - 8 :, :], "seq", 1).reshape(8 * seqs, model)
    tok, cot = tokens.reshape(rows, model), cotangent.reshape(rows, model)
    cot_far = swap(cot)
    soft, sgm = jax.nn.softplus(decay_param)[None], jax.nn.sigmoid(decay_param)[None]
    gain1, gain2 = mixer_gain[None], feed_gain[None]

    normed, gate, branch, edge, mixed, rate, inlet, h, p, carry = front(
        tok, halo, gain1, gate_weight, branch_weight, conv_taps, conv_offset[None], rate_weight, inlet_weight,
        rate_offset[None], inlet_offset[None], soft, seqs, length,
    )
    normed_far = swap(normed)
    entry = entry_state(carry, seq_n, False, 0)
    joined, resid, normed_two = join(tok, gate, h, p, entry, out_weight, gain2, seqs, length)
    joined_far, normed_two_far = swap(joined), swap(normed_two)
    hid_t, gg_t, gu_t, acc = feed(1 - half, normed_two, cot, feed_gate, feed_up, feed_down, None)
    hid_t_far, gg_far, gu_far = swap(hid_t), swap(gg_t), swap(gu_t)
    hid_m, gg_m, gu_m, grad_two = feed(half, normed_two, cot, feed_gate, feed_up, feed_down, acc)
    hid_m_far = swap(hid_m)
    out = block_out(half, resid, hid_t, hid_m, feed_down)

    grad_resid, grad_low, feed_gain_sum, ggate_t, ggate_m, lc, q, back = turn(
        half, grad_two, resid, cot, gain2, out_weight, gate, h, p, entry, rate, soft, seqs, length
    )
    grad_low_far, ggate_far = swap(grad_low), swap(ggate_t)
    arriving = entry_state(back, seq_n, True, 1)
    gb, head, tail, rate_sum, inlet_sum, taps_sum, vec_sum = gates_back(
        lc, q, arriving, h, p, entry, rate, inlet, mixed, branch, edge, rate_weight, inlet_weight, conv_taps, soft, sgm, seqs, length
    )
    ahead = shifted(head, "seq", -1)
    gb_t, gb_m = seam(half, gb, tail, ahead, conv_taps, seqs, length)
    gb_far = swap(gb_t)
    tokens_grad, mixer_gain_sum = input_grad(half, ggate_t, ggate_m, gb_t, gb_m, gate_weight, branch_weight, tok, grad_resid, gain1)

    small = jnp.concatenate([v.reshape(-1) for v in (taps_sum, vec_sum, mixer_gain_sum, feed_gain_sum)]).reshape(-1, 128)
    small = sum_all(small, seq_n, batch_n, 2).reshape(-1)
    taps_all, vec_all = small[: 4 * lru].reshape(4, lru), small[4 * lru : 8 * lru].reshape(4, lru)
    mixer_gain_all, feed_gain_all = small[8 * lru : 8 * lru + model], small[8 * lru + model :]
    rate_all, inlet_all = lax.psum((rate_sum, inlet_sum), ("seq", "batch"))

    if (seq_n, batch_n) == (8, 4):
        feed_pieces = [
            wgrad_down(half, hid_t, hid_m, hid_t_far, hid_m_far, cot, cot_far),
            wgrad(half, normed_two, normed_two_far, gg_m, gg_far, True, "wgrad_feed_gate"),
            wgrad(half, normed_two, normed_two_far, gu_m, gu_far, True, "wgrad_feed_up"),
        ]
        mixer_pieces = [
            wgrad(half, joined, joined_far, grad_low, grad_low_far, False, "wgrad_out"),
            wgrad(half, normed, normed_far, ggate_m, ggate_far, True, "wgrad_gate"),
            wgrad(half, normed, normed_far, gb_m, gb_far, True, "wgrad_branch"),
        ]
        feed_sums = scatter_sum(feed_pieces, 2, 3, "scatter_feed")
        mixer_sums = scatter_sum(mixer_pieces, 1, 4, "scatter_mixer")

        def laid(sums, part):
            t = sums.shape[2] // part
            return sums.reshape(2, 2, t, part, 128).transpose(3, 0, 1, 2, 4).reshape(part, 4 * t * 128).astype(F32)

        down_all, gate_feed_all, up_feed_all = (
            laid(feed_sums[0], units // 8), laid(feed_sums[1], model // 8), laid(feed_sums[2], model // 8)
        )
        out_all, gate_all, branch_all = (
            laid(mixer_sums[0], lru // 8), laid(mixer_sums[1], model // 8), laid(mixer_sums[2], model // 8)
        )
    else:

        def full(theirs, mine):
            a, b = jnp.where(core == 0, mine, theirs), jnp.where(core == 0, theirs, mine)
            return jnp.concatenate([a, b], axis=1)

        def total(left, right):
            return lax.psum(lax.psum_scatter(tn(left, right), "seq", scatter_dimension=0, tiled=True), "batch")

        down_all = total(full(hid_t, hid_m), cot)
        gate_feed_all = total(normed_two, full(gg_t, gg_m))
        up_feed_all = total(normed_two, full(gu_t, gu_m))
        out_all = total(joined, grad_low)
        gate_all = total(normed, full(ggate_t, ggate_m))
        branch_all = total(normed, full(gb_t, gb_m))

    return (
        out.reshape(seqs, length, model), tokens_grad.reshape(seqs, length, model), gate_all, branch_all, out_all,
        taps_all, vec_all[3], rate_all, inlet_all, vec_all[1], vec_all[2], vec_all[0], mixer_gain_all, feed_gain_all,
        gate_feed_all, up_feed_all, down_all,
    )


def solution(mesh):
    big = P("batch", "seq", None)
    in_specs = (big, big) + (P(),) * 15
    out_specs = (big, big) + (P("seq", None),) * 3 + (P(),) * 9 + (P("seq", None),) * 3
    return jax.shard_map(local, mesh=mesh, in_specs=in_specs, out_specs=out_specs, check_vma=False)
```

```python
import functools
import jax
import jax.numpy as jnp
from jax import lax
from jax.experimental import pallas as pl
from jax.experimental.pallas import tpu as pltpu
from jax.sharding import PartitionSpec as P

F32, BF16 = jnp.float32, jnp.bfloat16
VLIM = 56 * 2**20
GELU_A, GELU_B = 0.7978845608028654, 0.044715


def nn(a, b):
    return lax.dot_general(a, b, (((1,), (0,)), ((), ())), preferred_element_type=F32)


def nt(a, b):
    return lax.dot_general(a, b, (((1,), (1,)), ((), ())), preferred_element_type=F32)


def tn(a, b):
    return lax.dot_general(a, b, (((0,), (0,)), ((), ())), preferred_element_type=F32)


def sigmoid(v):
    return 1.0 / (1.0 + jnp.exp(-v))


def drop(u, decay):
    v = 2.0 * u
    series = 1.0 + v * (1.0 / 7.0)
    for k in (6.0, 5.0, 4.0, 3.0, 2.0):
        series = 1.0 + (v * (1.0 / k)) * series
    return jnp.where(v > -0.35, -v * series, 1.0 - decay * decay)


def gelu_parts(v):
    square = v * v
    inner = jnp.tanh(GELU_A * v * (1.0 + GELU_B * square))
    half = 0.5 + 0.5 * inner
    act = v * half
    slope = half + 0.5 * v * (1.0 - inner * inner) * (GELU_A + 3.0 * GELU_A * GELU_B * square)
    return act, slope


def gelu(v):
    inner = jnp.tanh(GELU_A * v * (1.0 + GELU_B * (v * v)))
    return v * (0.5 + 0.5 * inner)


def spread(dense, blocks, count, width):
    for a in range(count):
        parts = []
        if a > 0:
            parts.append(jnp.zeros((width, a * width), dense.dtype))
        parts.append(blocks[a])
        if a < count - 1:
            parts.append(jnp.zeros((width, (count - 1 - a) * width), dense.dtype))
        dense[a * width : (a + 1) * width, :] = jnp.concatenate(parts, axis=1)


def params(sem=("arbitrary",), **kw):
    return pltpu.CompilerParams(dimension_semantics=sem, vmem_limit_bytes=VLIM, **kw)


def whole(shape):
    return pl.BlockSpec(shape, lambda *_: (0,) * len(shape))


def front_kernel(
    seqs, length, tok, halo, gain, gw, bw, taps, coff, wr, wi, roff, ioff, sp,
    normed, gate, branch, edge, mixed, rate, inlet, h, p, carry,
    hn, ext, dr, di, rp, ip,
):
    rows, width = seqs * length, gw.shape[1]
    sub = dr.shape[-1]

    @pl.when(pl.program_id(0) == 0)
    def _():
        def norm(i, _):
            x = tok[pl.ds(i * 32, 32), :].astype(F32)
            r = lax.rsqrt(jnp.mean(x * x, axis=-1, keepdims=True) + 1e-06)
            normed[pl.ds(i * 32, 32), :] = (x * r * gain[...]).astype(BF16)
            return 0

        lax.fori_loop(0, rows // 32, norm, 0)
        x = halo[...].astype(F32)
        r = lax.rsqrt(jnp.mean(x * x, axis=-1, keepdims=True) + 1e-06)
        hn[...] = (x * r * gain[...]).astype(BF16)

    gate[...] = nn(normed[...], gw[...])
    b16 = nn(normed[...], bw[...]).astype(BF16)
    e16 = nn(hn[...], bw[...]).astype(BF16)
    branch[...] = b16
    edge[...] = e16
    for s in range(seqs):
        ext[s, 0:8, :] = e16[8 * s : 8 * s + 8].astype(F32)
        ext[s, 8 : 8 + length, :] = b16[length * s : length * (s + 1)].astype(F32)

    tap = [taps[k : k + 1, :] for k in range(4)]
    off = coff[...]
    for s in range(seqs):

        def conv(i, _):
            x = ext[s, pl.ds(pl.multiple_of(i * 16, 16), 24), :]
            total = off + tap[0] * x[8:24]
            for k in range(1, 4):
                total = total + tap[k] * x[8 - k : 24 - k]
            mixed[pl.ds(pl.multiple_of(s * length + i * 16, 16), 16), :] = total.astype(BF16)
            return 0

        lax.fori_loop(0, length // 16, conv, 0)

    for g in range(width // sub):
        cols = slice(g * sub, (g + 1) * sub)
        spread(dr.at[g], [wr[g * 4 + a] for a in range(4)], 4, wr.shape[-1])
        spread(di.at[g], [wi[g * 4 + a] for a in range(4)], 4, wi.shape[-1])
        rp[:, cols] = nn(mixed[:, cols], dr[g])
        ip[:, cols] = nn(mixed[:, cols], di[g])

    ro, io, slope = roff[...], ioff[...], -8.0 * sp[...]

    def gates(i, _):
        at = pl.ds(pl.multiple_of(i * 16, 16), 16)
        rt = sigmoid(rp[at, :] + ro)
        it = sigmoid(ip[at, :] + io)
        log_decay = rt * slope
        decay = jnp.exp(log_decay)
        rate[at, :] = rt
        inlet[at, :] = it
        p[at, :] = decay
        h[at, :] = jnp.sqrt(drop(log_decay, decay)) * it * mixed[at, :].astype(F32)
        return 0

    lax.fori_loop(0, rows // 16, gates, 0)

    row = lax.broadcasted_iota(jnp.int32, (8, width), 0)

    def scan(i, last):
        out = []
        for s in range(seqs):
            at = pl.ds(pl.multiple_of(s * length + i * 8, 8), 8)
            a, b = p[at, :], h[at, :]
            for d in (1, 2, 4):
                keep = row >= d
                b = b + a * jnp.where(keep, pltpu.roll(b, d, 0), 0.0)
                a = a * jnp.where(keep, pltpu.roll(a, d, 0), 1.0)
            ap, bp = last[s]
            b = b + a * bp
            a = a * ap
            p[at, :] = a
            h[at, :] = b
            out.append((a[7:8], b[7:8]))
        return tuple(out)

    init = tuple((jnp.ones((1, width), F32), jnp.zeros((1, width), F32)) for _ in range(seqs))
    last = lax.fori_loop(0, length // 8, scan, init)
    for s in range(seqs):
        carry[0, s : s + 1, :] = last[s][0]
        carry[1, s : s + 1, :] = last[s][1]


def front(tok, halo, gain, gw, bw, taps, coff, wr, wi, roff, ioff, sp, seqs, length):
    rows, model = tok.shape
    lru = gw.shape[1]
    bw_, per = wr.shape[-1], 8
    width = per * bw_
    sub = 4 * bw_
    n = lru // width
    col = lambda r: pl.BlockSpec((r, width), lambda j: (0, j))
    blk = pl.BlockSpec((per, bw_, bw_), lambda j: (j, 0, 0))
    f = lambda dt: jax.ShapeDtypeStruct((rows, lru), dt)
    return pl.pallas_call(
        functools.partial(front_kernel, seqs, length),
        grid=(n,),
        in_specs=[
            whole((rows, model)), whole(halo.shape), whole((1, model)),
            pl.BlockSpec((model, width), lambda j: (0, j)), pl.BlockSpec((model, width), lambda j: (0, j)),
            col(4), col(1), blk, blk, col(1), col(1), col(1),
        ],
        out_specs=[
            whole((rows, model)), col(rows), col(rows), col(halo.shape[0]), col(rows), col(rows), col(rows), col(rows), col(rows),
            pl.BlockSpec((2, seqs, width), lambda j: (0, 0, j)),
        ],
        out_shape=[
            jax.ShapeDtypeStruct((rows, model), BF16), f(F32), f(BF16),
            jax.ShapeDtypeStruct((halo.shape[0], lru), BF16), f(BF16), f(F32), f(F32), f(F32), f(F32),
            jax.ShapeDtypeStruct((2, seqs, lru), F32),
        ],
        scratch_shapes=[
            pltpu.VMEM(halo.shape, BF16), pltpu.VMEM((seqs, 8 + length, width), F32),
            pltpu.VMEM((2, sub, sub), BF16), pltpu.VMEM((2, sub, sub), BF16),
            pltpu.VMEM((rows, width), F32), pltpu.VMEM((rows, width), F32),
        ],
        compiler_params=params(),
        name="front",
    )(tok, halo, gain, gw, bw, taps, coff, wr, wi, roff, ioff, sp)


def join_kernel(tok, gate, h, p, entry, ow, gain, joined, resid, normed):
    rows = tok.shape[0]
    ent = entry[0]

    def join(i, _):
        at = pl.ds(pl.multiple_of(i * 16, 16), 16)
        state = h[at, :] + p[at, :] * ent
        joined[at, :] = (gelu(gate[at, :]) * state).astype(BF16)
        return 0

    lax.fori_loop(0, rows // 16, join, 0)
    resid[...] = nn(joined[...], ow[...])

    def norm(i, _):
        at = pl.ds(pl.multiple_of(i * 32, 32), 32)
        y = tok[at, :].astype(F32) + resid[at, :]
        resid[at, :] = y
        r = lax.rsqrt(jnp.mean(y * y, axis=-1, keepdims=True) + 1e-06)
        normed[at, :] = (y * r * gain[...]).astype(BF16)
        return 0

    lax.fori_loop(0, rows // 32, norm, 0)


def join(tok, gate, h, p, entry, ow, gain, seqs, length):
    rows, model = tok.shape
    lru = gate.shape[1]
    tile = 128
    per = length // tile
    row = lambda w: pl.BlockSpec((tile, w), lambda i: (i, 0))
    return pl.pallas_call(
        join_kernel,
        grid=(rows // tile,),
        in_specs=[row(model), row(lru), row(lru), row(lru), pl.BlockSpec((1, 1, lru), lambda i: (i // per, 0, 0)), whole((lru, model)), whole((1, model))],
        out_specs=[row(lru), row(model), row(model)],
        out_shape=[jax.ShapeDtypeStruct((rows, lru), BF16), jax.ShapeDtypeStruct((rows, model), F32), jax.ShapeDtypeStruct((rows, model), BF16)],
        compiler_params=params(),
        name="join",
    )(tok, gate, h, p, entry.reshape(seqs, 1, lru), ow, gain)


def feed_kernel(first, who, *refs):
    if first:
        n2, cot, fg, fu, fd, hid, gg, gu, acc, ug, uv, gh = refs
    else:
        n2, cot, fg, fu, fd, start, hid, gg, gu, acc, ug, uv, gh = refs
    rows = n2.shape[0]
    ug[...] = nn(n2[...], fg[...])
    uv[...] = nn(n2[...], fu[...])
    gh[...] = nt(cot[...], fd[...])

    def body(i, _):
        at = pl.ds(pl.multiple_of(i * 16, 16), 16)
        act, slope = gelu_parts(ug[at, :])
        v, g = uv[at, :], gh[at, :]
        hid[at, :] = (act * v).astype(BF16)
        gg[at, :] = (g * v * slope).astype(BF16)
        gu[at, :] = (g * act).astype(BF16)
        return 0

    lax.fori_loop(0, rows // 16, body, 0)

    @pl.when(pl.program_id(0) == 0)
    def _():
        if first:
            acc[...] = jnp.zeros_like(acc)
        else:
            acc[...] = start[...]

    acc[...] += nt(gg[...], fg[...]) + nt(gu[...], fu[...])


def feed(half, n2, cot, fg, fu, fd, start):
    rows, model = n2.shape
    units = fg.shape[1]
    tile = 512
    n = units // 2 // tile
    first = start is None
    out = lambda: pl.BlockSpec((rows, tile), lambda i, w: (0, i))
    ins = [
        whole((rows, model)), whole((rows, model)),
        pl.BlockSpec((model, tile), lambda i, w: (0, w[0] * n + i)), pl.BlockSpec((model, tile), lambda i, w: (0, w[0] * n + i)),
        pl.BlockSpec((tile, model), lambda i, w: (w[0] * n + i, 0)),
    ]
    args = [n2, cot, fg, fu, fd]
    if not first:
        ins.append(whole((rows, model)))
        args.append(start)
    return pl.pallas_call(
        functools.partial(feed_kernel, first),
        grid_spec=pltpu.PrefetchScalarGridSpec(
            num_scalar_prefetch=1, grid=(n,), in_specs=ins, out_specs=[out(), out(), out(), whole((rows, model))],
            scratch_shapes=[pltpu.VMEM((rows, tile), F32)] * 3,
        ),
        out_shape=[jax.ShapeDtypeStruct((rows, units // 2), BF16)] * 3 + [jax.ShapeDtypeStruct((rows, model), F32)],
        compiler_params=params(),
        name="feed_a" if first else "feed_b",
    )(half, *args)


MESH = pl.DeviceIdType.MESH


def meet(peers):
    barrier = pltpu.get_barrier_semaphore()
    for peer in peers:
        pl.semaphore_signal(barrier, inc=1, device_id=peer, device_id_type=MESH)
    pl.semaphore_wait(barrier, len(peers))


def entry_state(part, n, reverse, collective_id):
    _, seqs, lru = part.shape

    def kernel(mine, out, got, send, recv):
        me, b = lax.axis_index("seq"), lax.axis_index("batch")
        peers = [(lax.rem(me + k, n), b) for k in range(1, n)]
        meet(peers)
        copies = []
        for k in range(1, n):
            copy = pltpu.make_async_remote_copy(
                src_ref=mine, dst_ref=got.at[me], send_sem=send.at[k], recv_sem=recv.at[k],
                device_id=peers[k - 1], device_id_type=MESH,
            )
            copy.start()
            copies.append(copy)
        got[me] = mine[...]
        for copy in copies:
            copy.wait()

        def one(k, state):
            j = n - 1 - k if reverse else k
            before = (j > me) if reverse else (j < me)
            return jnp.where(before, got[j, 0] * state + got[j, 1], state)

        out[...] = lax.fori_loop(0, n, one, jnp.zeros((seqs, lru), F32))

    return pl.pallas_call(
        kernel,
        in_specs=[pl.BlockSpec(memory_space=pltpu.VMEM)],
        out_specs=pl.BlockSpec(memory_space=pltpu.VMEM),
        out_shape=jax.ShapeDtypeStruct((seqs, lru), F32),
        scratch_shapes=[pltpu.VMEM((n, 2, seqs, lru), F32), pltpu.SemaphoreType.DMA((n,)), pltpu.SemaphoreType.DMA((n,))],
        compiler_params=pltpu.CompilerParams(collective_id=collective_id, has_side_effects=True, vmem_limit_bytes=VLIM),
        name="entry_back" if reverse else "entry",
    )(part)


def flip(index, bit):
    return index + bit - 2 * bit * (lax.rem(index // bit, 2))


ORDERS = {"D": ("xlyh", "ylxh"), "E": ("xlhy", "yxlh")}


class Exchange:
    def __init__(self, chunks, part, bufs, fin, send, recv):
        self.chunks, self.part, self.bufs, self.fin, self.sems = chunks, part, bufs, fin, (send, recv)
        seq, bat = lax.axis_index("seq"), lax.axis_index("batch")
        core, y = lax.rem(bat, 2), bat // 2
        x, low, high = lax.rem(seq, 2), lax.rem(seq // 2, 2), seq // 4
        bit = {"x": x, "y": y, "l": low, "h": high}
        move = {"x": (1 - 2 * x, 0), "y": (0, 2 - 4 * y), "l": (2 - 4 * low, 0), "h": (4 - 8 * high, 0)}
        pick = lambda a, b: a if a is b else (1 - core) * a + core * b
        self.core, self.y = core, y
        self.other, self.across = (seq, bat + 1 - 2 * core), (seq, bat + 2 - 4 * y)
        self.bits, self.peers = {}, {}
        for kind, (first, second) in ORDERS.items():
            self.bits[kind] = [pick(bit[a], bit[b]) for a, b in zip(first, second)]
            self.peers[kind] = [
                (seq + pick(move[a][0], move[b][0]), bat + pick(move[a][1], move[b][1])) for a, b in zip(first, second)
            ] + [self.across, self.other]
        self.greet = [(seq + move[a][0], bat) for a in "xlh"] + [self.across, self.other]
        self.freed, self.further = set(), {}

    def at(self, place):
        for k, q in PLAN.get(place, ()):
            self.step(k, q)

    def free(self, q):
        self.copy(0, q).wait_send()
        self.freed.add(q)

    def drain(self):
        self.at("drain")
        for q in range(len(self.chunks)):
            for k in range(4):
                if k > 0 or q not in self.freed:
                    self.copy(k, q).wait_send()

    def copy(self, k, q):
        grad, row, kind = self.chunks[q]
        size, bits = 8 >> k, self.bits[kind]
        if k == 0:
            src, dst = grad.at[pl.ds((1 - bits[0]) * 8, 8), row : row + self.part], self.bufs[0].at[q]
        elif k < 4:
            src, dst = self.bufs[k - 1].at[q, pl.ds((1 - bits[k]) * size, size)], self.bufs[k].at[q]
        elif k == 4:
            src = dst = self.fin.at[q, self.core, self.y]
        else:
            src = dst = self.fin.at[q, self.core]
        return pltpu.make_async_remote_copy(
            src_ref=src, dst_ref=dst, send_sem=self.sems[0].at[k, q], recv_sem=self.sems[1].at[k, q],
            device_id=self.peers[kind][k], device_id_type=MESH,
        )

    def add(self, k, q, base, size):
        grad, row, kind = self.chunks[q]
        dst = self.bufs[k]
        bits = self.bits[kind]
        for j in range(size):

            def body(i, _):
                a = pl.ds(pl.multiple_of(i * 128, 128), 128)
                if k == 0:
                    own = grad[bits[0] * 8 + base + j, pl.ds(pl.multiple_of(row + i * 128, 128), 128), :]
                else:
                    own = self.bufs[k - 1][q, bits[k] * (8 >> k) + base + j, a, :]
                dst[q, base + j, a, :] = dst[q, base + j, a, :] + own
                return 0

            lax.fori_loop(0, self.part // 128, body, 0)

    def step(self, k, q):
        if k > 5:
            self.further[k][q]()
        elif k < 0:
            self.copy(0, q).start()
        elif k < 3:
            half, bits = 4 >> k, self.bits[self.chunks[q][2]]
            self.copy(k, q).wait_recv()
            self.add(k, q, (1 - bits[k + 1]) * half, half)
            self.copy(k + 1, q).start()
            self.add(k, q, bits[k + 1] * half, half)
        elif k == 3:
            bits = self.bits[self.chunks[q][2]]
            self.copy(3, q).wait_recv()

            def body(i, _):
                a = pl.ds(pl.multiple_of(i * 128, 128), 128)
                self.fin[q, self.core, self.y, a, :] = self.bufs[3][q, 0, a, :] + self.bufs[2][q, bits[3], a, :]
                return 0

            lax.fori_loop(0, self.part // 128, body, 0)
            self.copy(4, q).start()
        elif k == 4:
            self.copy(4, q).wait()
            self.copy(5, q).start()
        else:
            self.copy(5, q).wait()

    @staticmethod
    def scratch(chunks, part):
        return [pltpu.VMEM((chunks, 8 >> k, part, 128), BF16) for k in range(4)] + [pltpu.SemaphoreType.DMA((6, chunks))] * 2


class BlockSums:
    def __init__(self, value, bufs, out, send, recv):
        self.value, self.bufs, self.out, self.sems = value, bufs, out, (send, recv)
        seq, bat = lax.axis_index("seq"), lax.axis_index("batch")
        core, y = lax.rem(bat, 2), bat // 2
        x, low, high = lax.rem(seq, 2), lax.rem(seq // 2, 2), seq // 4
        self.bits = [core, low, high, x, y]
        self.peers = [(seq, bat + 1 - 2 * core), (seq + 2 - 4 * low, bat), (seq + 4 - 8 * high, bat), (seq + 1 - 2 * x, bat), (seq, bat + 2 - 4 * y)]
        self.base = [0]
        for k in range(5):
            self.base.append(self.base[-1] + self.bits[k] * (16 >> k))

    def halve(self, k):
        size = 16 >> k
        return pltpu.make_async_remote_copy(
            src_ref=self.value.at[pl.ds(self.base[k] + (1 - self.bits[k]) * size, size)], dst_ref=self.bufs[k],
            send_sem=self.sems[0].at[k], recv_sem=self.sems[1].at[k], device_id=self.peers[k], device_id_type=MESH,
        )

    def hand(self, k):
        at = pl.ds(self.base[k + 1], 16 >> k)
        return pltpu.make_async_remote_copy(
            src_ref=self.out.at[at], dst_ref=self.out.at[at],
            send_sem=self.sems[0].at[5 + k], recv_sem=self.sems[1].at[5 + k], device_id=self.peers[k], device_id_type=MESH,
        )

    def events(self):
        def took(k):
            size = 16 >> k
            self.halve(k).wait()

            def body(j, _):
                at = self.base[k + 1] + j
                total = (self.value[at].astype(F32) + self.bufs[k][j].astype(F32)).astype(BF16)
                if k < 4:
                    self.value[at] = total
                else:
                    self.out[at] = total
                return 0

            lax.fori_loop(0, size, body, 0)
            if k < 4:
                self.halve(k + 1).start()
            else:
                self.hand(4).start()

        def got(k):
            self.hand(k).wait()
            if k > 0:
                self.hand(k - 1).start()

        first = [lambda: self.halve(0).start()]
        return first + [functools.partial(took, k) for k in range(5)] + [functools.partial(got, k) for k in range(4, -1, -1)]

    @staticmethod
    def scratch(width):
        return [pltpu.VMEM((16 >> k, width, 128), BF16) for k in range(5)] + [pltpu.SemaphoreType.DMA((10,))] * 2


def core_of():
    return lax.rem(lax.axis_index("batch"), 2)


def group(core):
    i = pl.program_id(0)
    return (1 - i) * (1 - core) + i * core


def put_pieces(chunks, acc, core, y, first, count):
    part, cols = acc.shape[0] // count, acc.shape[1]
    for j in range(count):
        for t in range(cols // 128):
            ref, row, kind = chunks[t * part // 384]
            at = place_of(core, first + j, y, kind)
            row = row + t * part % 384
            ref[at, row : row + part, :] = acc[j * part : (j + 1) * part, t * 128 : (t + 1) * 128].astype(BF16)


def place_of(core, s, y, kind):
    bit = {"x": s % 2, "l": (s // 2) % 2, "h": s // 4, "y": y}
    place = lambda order: sum(bit[a] * (8 >> k) for k, a in enumerate(order))
    first, second = ORDERS[kind]
    return place(first) if first == second else (1 - core) * place(first) + core * place(second)


def wgrad(core, chunks, lhs, lhs_far, rhs, rhs_far, own_columns):
    rows = lhs.shape[0]
    tile = rhs.shape[1] // (2 if own_columns else 4)
    base = 0 if own_columns else 2 * core

    def body(a, b, c, d):
        put_pieces(chunks, tn(a[...], c[...]) + tn(b[...], d[...]), core, pl.program_id(0), 0, 8)

    left = pl.BlockSpec(lhs.shape, lambda y: (0, 0), pipeline_mode=pl.Buffered(1))
    right = pl.BlockSpec((rows, tile), lambda y: (0, base + y))
    pltpu.emit_pipeline(body, grid=(2,), in_specs=[left, left, right, right])(lhs, lhs_far, rhs, rhs_far)


def wgrad_down(core, chunks, theirs, mine, far_theirs, far_mine, cot, cot_far, between):
    rows, units = mine.shape
    tile = cot.shape[1] // 4
    for a, b, first in ((theirs, far_mine, 4 * (1 - core)), (mine, far_theirs, 4 * core)):

        def body(l, m, c, d):
            put_pieces(chunks, tn(l[...], c[...]) + tn(m[...], d[...]), core, pl.program_id(0), first, 4)

        left = pl.BlockSpec((rows, units), lambda y: (0, 0), pipeline_mode=pl.Buffered(1))
        right = pl.BlockSpec((rows, tile), lambda y: (0, 2 * core + y))
        pltpu.emit_pipeline(body, grid=(2,), in_specs=[left, left, right, right])(a, b, cot, cot_far)
        between()
        between = lambda: None


def norm_back(core, gn, resid, cot, fgain, gres, low, gain_sum):
    rows, model = gn.shape
    tile = 128
    gain_sum[...] = jnp.zeros_like(gain_sum)

    def body(d_ref, y_ref, c_ref, out_ref):
        g = fgain[...]

        def norm(i, total):
            at = pl.ds(pl.multiple_of(i * 16, 16), 16)
            y, d = y_ref[at, :], d_ref[at, :]
            r = lax.rsqrt(jnp.mean(y * y, axis=-1, keepdims=True) + 1e-06)
            dg, yr = d * g, y * r
            dot = jnp.mean(dg * yr, axis=-1, keepdims=True)
            out = c_ref[at, :].astype(F32) + r * (dg - yr * dot)
            out_ref[at, :] = out
            low[pl.ds(pl.multiple_of(pl.program_id(0) * tile + i * 16, 16), 16), :] = out.astype(BF16)
            add = d * yr
            return total + add[0:8] + add[8:16]

        total = lax.fori_loop(0, tile // 16, norm, jnp.zeros((8, model), F32))
        gain_sum[...] += jnp.sum(total, axis=0, keepdims=True)

    row = pl.BlockSpec((tile, model), lambda i: (i, 0))
    pltpu.emit_pipeline(body, grid=(rows // tile,), in_specs=[row, row, row], out_specs=[row])(gn, resid, cot, gres)


def turn(core, seqs, length, low, ow, gate, h, p, entry, rate, sp, ggate, lc, q, carry, gj, begin):
    rows, lru = gate.shape
    width = lru // 2

    def body(ow_ref, gate_ref, h_ref, p_ref, e_ref, rate_ref, sp_ref, gg_ref, lc_ref, q_ref):
        pump = begin()
        for s in range(seqs):
            gj[s, 0:length, :] = nt(low[s * length : (s + 1) * length, :], ow_ref[...])
        pump()
        slope = -8.0 * sp_ref[...]
        for s in range(seqs):
            ent = e_ref[s]

            def act(i, _):
                at = pl.ds(pl.multiple_of(s * length + i * 16, 16), 16)
                here = pl.ds(pl.multiple_of(i * 16, 16), 16)
                value, der = gelu_parts(gate_ref[at, :])
                state = h_ref[at, :] + p_ref[at, :] * ent
                d = gj[s, here, :]
                gg_ref[0, at, :] = (d * state * der).astype(BF16)
                gj[s, here, :] = d * value
                return 0

            lax.fori_loop(0, length // 16, act, 0)
            pump()

        row = lax.broadcasted_iota(jnp.int32, (8, width), 0)
        tiles = length // 8

        def scan(k, last):
            i = tiles - 1 - k
            out = []
            for s in range(seqs):
                at = pl.ds(pl.multiple_of(s * length + i * 8, 8), 8)
                g = gj[s, pl.ds(pl.multiple_of(i * 8, 8), 8), :]
                a = jnp.exp(rate_ref[at, :] * slope)
                b = a * g
                for d in (1, 2, 4):
                    keep = row < 8 - d
                    b = b + a * jnp.where(keep, pltpu.roll(b, 8 - d, 0), 0.0)
                    a = a * jnp.where(keep, pltpu.roll(a, 8 - d, 0), 1.0)
                ap, bp = last[s]
                b = b + a * bp
                a = a * ap
                lc_ref[at, :] = g + jnp.where(row < 7, pltpu.roll(b, 7, 0), bp)
                q_ref[at, :] = jnp.where(row < 7, pltpu.roll(a, 7, 0), ap)
                out.append((a[0:1], b[0:1]))
            return tuple(out)

        init = tuple((jnp.ones((1, width), F32), jnp.zeros((1, width), F32)) for _ in range(seqs))
        last = lax.fori_loop(0, tiles, scan, init)
        for s in range(seqs):
            carry[group(core), 0, s : s + 1, :] = last[s][0]
            carry[group(core), 1, s : s + 1, :] = last[s][1]
        pump()

    grp = lambda i: (1 - i) * (1 - core) + i * core
    col = lambda r: pl.BlockSpec((r, width), lambda i: (0, grp(i)))
    pltpu.emit_pipeline(
        body, grid=(2,),
        in_specs=[
            pl.BlockSpec((width, ow.shape[1]), lambda i: (grp(i), 0)), col(rows), col(rows), col(rows),
            pl.BlockSpec((seqs, 1, width), lambda i: (0, 0, grp(i))), col(rows), col(1),
        ],
        out_specs=[pl.BlockSpec((1, rows, width), lambda i: (i, 0, 0)), col(rows), col(rows)],
    )(ow, gate, h, p, entry, rate, sp, ggate, lc, q)


def gates_back(
    own, core, seqs, length, lc, q, cin, h, p, entry, rate, inlet, mixed, branch, edge, wr, wi, taps, sp, sg,
    gb, head, tail, blocks, rate_sum, inlet_sum, sums_out, dr, di, gr, gi, gm, ext, begin,
):
    rows, lru = lc.shape
    width, bw_ = lru // 2, wr.shape[-1]
    per, sub = width // bw_, dr.shape[-1]

    def body(
        lc_ref, q_ref, h_ref, p_ref, e_ref, rate_ref, inlet_ref, mixed_ref, branch_ref, edge_ref, wr_ref, wi_ref, taps_ref, sp_ref, sg_ref,
        gb_ref,
    ):
        pump = begin()
        mine = group(core)
        slope = -8.0 * sp_ref[...]
        zero = jnp.zeros((8, width), F32)
        row = lax.broadcasted_iota(jnp.int32, (16, width), 0)

        sums = (zero, zero, zero)
        for s in range(seqs):
            c_in, ent = cin[mine, s : s + 1, :], e_ref[s]

            def gates(i, carry):
                (before, t0, t1, t2) = carry
                at = pl.ds(pl.multiple_of(s * length + i * 16, 16), 16)
                state = h_ref[at, :] + p_ref[at, :] * ent
                prev = jnp.where(row > 0, pltpu.roll(state, 1, 0), before)
                carried = lc_ref[at, :] + q_ref[at, :] * c_in
                rt, it, mx = rate_ref[at, :], inlet_ref[at, :], mixed_ref[at, :].astype(F32)
                log_decay = rt * slope
                decay = jnp.exp(log_decay)
                gap = drop(log_decay, decay)
                inv = lax.rsqrt(gap)
                nf = gap * inv
                im = it * mx
                g_log = carried * decay * (prev - im * decay * inv)
                cn = carried * nf
                g_rt = g_log * slope * (rt * (1.0 - rt))
                g_it = cn * im * (1.0 - it)
                gr[at, :] = g_rt.astype(BF16)
                gi[at, :] = g_it.astype(BF16)
                gm[s, pl.ds(pl.multiple_of(i * 16, 16), 16), :] = cn * it
                lr = g_log * rt
                return (state[15:16], t0 + lr[0:8] + lr[8:16], t1 + g_rt[0:8] + g_rt[8:16], t2 + g_it[0:8] + g_it[8:16])

            _, *sums = lax.fori_loop(0, length // 16, gates, (ent, *sums))
            pump()
        down = lambda v: jnp.sum(v, axis=0, keepdims=True)
        lanes = pl.ds(pl.multiple_of(mine * width, 128), width)
        sums_out[4:5, lanes] = down(sums[0]) * (-8.0 * sg_ref[...])
        sums_out[5:6, lanes] = down(sums[1])
        sums_out[6:7, lanes] = down(sums[2])

        for g in range(width // sub):
            cols = slice(g * sub, (g + 1) * sub)
            spread(dr, [wr_ref[g * 4 + a] for a in range(4)], 4, bw_)
            spread(di, [wi_ref[g * 4 + a] for a in range(4)], 4, bw_)
            back = nt(gr[:, cols], dr[...]) + nt(gi[:, cols], di[...])
            rs = tn(mixed_ref[:, cols], gr[:, cols])
            is_ = tn(mixed_ref[:, cols], gi[:, cols])
            for a in range(4):
                block = slice(a * bw_, (a + 1) * bw_)
                if own:
                    blocks[mine * per + g * 4 + a, :, 0:bw_] = rs[block, block].astype(BF16)
                    blocks[2 * per + mine * per + g * 4 + a, :, 0:bw_] = is_[block, block].astype(BF16)
                else:
                    rate_sum[mine * per + g * 4 + a] = rs[block, block]
                    inlet_sum[mine * per + g * 4 + a] = is_[block, block]
            for s in range(seqs):
                gm[s, 0:length, cols] += back[s * length : (s + 1) * length]
        pump()

        for s in range(seqs):
            gm[s, length : length + 8, :] = zero
            ext[s, 0:8, :] = edge_ref[8 * s : 8 * s + 8].astype(F32)
            ext[s, 8 : 8 + length, :] = branch_ref[s * length : (s + 1) * length].astype(F32)
            head[mine, 8 * s : 8 * s + 8, :] = gm[s, 0:8, :]

        tap = [taps_ref[k : k + 1, :] for k in range(4)]
        acc = (zero,) * 5
        for s in range(seqs):

            def conv(i, acc):
                lo = pl.multiple_of(i * 16, 16)
                y = gm[s, pl.ds(lo, 24), :]
                x = ext[s, pl.ds(lo, 24), :]
                total = tap[0] * y[0:16]
                for k in range(1, 4):
                    total = total + tap[k] * y[k : k + 16]
                gb_ref[0, pl.ds(pl.multiple_of(s * length + i * 16, 16), 16), :] = total.astype(BF16)
                now = y[0:16]
                new = []
                for k in range(4):
                    prod = now * x[8 - k : 24 - k]
                    new.append(acc[k] + prod[0:8] + prod[8:16])
                new.append(acc[4] + now[0:8] + now[8:16])
                return tuple(new)

            acc = lax.fori_loop(0, length // 16, conv, acc)
            y = gm[s, length - 16 : length + 8, :]
            total = tap[0] * y[0:16]
            for k in range(1, 4):
                total = total + tap[k] * y[k : k + 16]
            tail[mine, 16 * s : 16 * s + 16, :] = total
            pump()
        for k in range(4):
            sums_out[k : k + 1, lanes] = down(acc[k])
        sums_out[7:8, lanes] = down(acc[4])

    grp = lambda i: (1 - i) * (1 - core) + i * core
    col = lambda r: pl.BlockSpec((r, width), lambda i: (0, grp(i)))
    blk = pl.BlockSpec((per, bw_, bw_), lambda i: (grp(i), 0, 0))
    pltpu.emit_pipeline(
        body, grid=(2,),
        in_specs=[
            col(rows), col(rows), col(rows), col(rows), pl.BlockSpec((seqs, 1, width), lambda i: (0, 0, grp(i))),
            col(rows), col(rows), col(rows), col(rows), col(edge.shape[0]), blk, blk, col(4), col(1), col(1),
        ],
        out_specs=[pl.BlockSpec((1, rows, width), lambda i: (i, 0, 0))],
    )(lc, q, h, p, entry, rate, inlet, mixed, branch, edge, wr, wi, taps, sp, sg, gb)


class Entry:
    def __init__(self, part, got, n, send, recv):
        self.part, self.got, self.n = part, got, n
        self.me = lax.axis_index("seq")
        self.copies = [
            pltpu.make_async_remote_copy(
                src_ref=part, dst_ref=got.at[self.me], send_sem=send.at[k], recv_sem=recv.at[k],
                device_id=(lax.rem(self.me + k, n), lax.axis_index("batch")), device_id_type=MESH,
            )
            for k in range(1, n)
        ]

    def start(self):
        for copy in self.copies:
            copy.start()
        self.got[self.me] = self.part[...]

    def finish(self, out, reverse):
        for copy in self.copies:
            copy.wait()

        def one(k, state):
            j = self.n - 1 - k if reverse else k
            before = (j > self.me) if reverse else (j < self.me)
            return jnp.where(before, self.got[j, :, 0] * state + self.got[j, :, 1], state)

        out[...] = lax.fori_loop(0, self.n, one, jnp.zeros(out.shape, F32))


def spaced(exchange, name, steps):
    def begin():
        place = iter(range(64))

        def pump():
            j = next(place)
            for i in range(steps):
                if PLAN.get(f"{name}{i}{j}"):

                    @pl.when(pl.program_id(0) == i)
                    def _():
                        exchange.at(f"{name}{i}{j}")

        return pump

    return begin


def no_pump():
    return lambda: None


ANY = pl.BlockSpec(memory_space=pl.ANY)
INSIDE = pl.BlockSpec(memory_space=pltpu.VMEM)


KINDS = "DDEDDEDDE"
PLAN = {
    "a0": [(-1, 0), (-1, 1)],
    "a1": [(-1, 2), (-1, 3)],
    "t01": [(0, 0), (-1, 4), (0, 1), (-1, 5)],
    "t12": [(0, 2), (0, 3)],
    "b1": [(1, 0), (-1, 6), (1, 1)],
    "g00": [(1, 2), (1, 3), (0, 4), (0, 5), (2, 0), (2, 1)],
    "g03": [(2, 3)],
    "g11": [(3, 0), (0, 6), (3, 1), (2, 2)],
    "g13": [(4, 0), (3, 3)],
    "g14": [(5, 0), (4, 1)],
    "c1": [(-1, 7), (5, 1), (3, 2), (4, 3), (6, 0)],
    "c2": [(5, 3), (1, 4), (1, 5), (6, 1)],
    "c3": [(4, 2)],
    "c4": [(-1, 8), (5, 2), (2, 4), (1, 6)],
    "i00": [(2, 5), (6, 2)],
    "i10": [(0, 7), (3, 4), (2, 6)],
    "i30": [(4, 4), (3, 5), (6, 3)],
    "o00": [(5, 4), (3, 6), (0, 8), (6, 4), (4, 5), (7, 0)],
    "o10": [(5, 5)],
    "o20": [(4, 6), (6, 5)],
    "o30": [(5, 6), (1, 7), (6, 6), (7, 1)],
    "drain": [(1, 8), (6, 7), (7, 2), (2, 7), (2, 8), (6, 8), (7, 3), (3, 7), (3, 8), (4, 7), (7, 4), (4, 8), (5, 7), (6, 9), (5, 8), (6, 10)],
}


PART = 384


def backward(own, seqs, length, seq_n, batch_n, grads_in, values, collective_id):
    (
        gn, resid, cot, fgain, ow, gate, h, p, entry, rate, sp, inlet, mixed, branch, edge, wr, wi, taps, sg, gw, bw, tok, mgain, ht, hm, fd
    ) = values
    rows, model = gn.shape
    lru, units = gate.shape[1], fd.shape[0]
    width, bw_ = lru // 2, wr.shape[-1]
    per, sub = width // bw_, 4 * bw_
    steps = [("batch", 1 << k) for k in range(batch_n.bit_length() - 1)] + [("seq", 1 << k) for k in range(seq_n.bit_length() - 1)]
    n_steps = len(steps)
    if not own:
        grads_in = []

    def kernel(*refs):
        refs = list(refs)
        cut = lambda n: [refs.pop(0) for _ in range(n)]
        far_in = cut(len(grads_in))
        (
            gn, resid, cot, fgain, ow, gate, h, p, entry, rate, sp, inlet, mixed, branch, edge, wr, wi, taps, sg, gw, bw, tok, mgain, ht, hm, fd
        ) = cut(26)
        tokens_grad, block_out, totals, gres, low_out, low_far, ggate, ggate_far, lc, q, gb, gb_far = cut(12)
        fin, block_total = cut(2) if own else (None, None)
        rate_sum, inlet_sum = (None, None) if own else cut(2)
        low, carry, got, cin, dr, di, gr, gi, gm, ext, head, tail, ahead, fixed, gain_sum, acc, small = cut(17)
        send, recv, swap_send, swap_recv, one, local, s_send, s_recv = cut(8)

        core = core_of()
        seq, bat = lax.axis_index("seq"), lax.axis_index("batch")
        other = (seq, bat + 1 - 2 * core)
        peers = [(flip(seq, bit), bat) if axis == "seq" else (seq, flip(bat, bit)) for axis, bit in steps]
        exchange, blocks = None, None
        if own:
            g0, g1, g2, *bufs, x_send, x_recv = cut(9)
            blocks, *block_bufs, b_send, b_recv = cut(8)
            places = [(g0, 0), (g0, PART), (g1, 0), (g1, PART), (g2, 0), (g2, PART), (g0, 0), (g0, PART), (g1, 0)]
            chunks = [(ref, row, kind) for (ref, row), kind in zip(places, KINDS)]
            exchange = Exchange(chunks, PART, bufs, fin, x_send, x_recv)
            exchange.further[6] = BlockSums(blocks, block_bufs, block_total, b_send, b_recv).events()
            blocks[...] = jnp.zeros_like(blocks)
        small[0] = jnp.zeros((16, lru), F32)
        greet = [(lax.rem(seq + k, seq_n), bat) for k in range(1, seq_n)] + [peer for peer, step in zip(peers, steps) if step[0] == "batch"]
        meet(greet)

        def swap(j, src, dst):
            return pltpu.make_async_remote_copy(
                src_ref=src, dst_ref=dst, send_sem=swap_send.at[j], recv_sem=swap_recv.at[j], device_id=other, device_id_type=MESH
            )

        at = exchange.at if own else (lambda place: None)
        if own:
            n2, n2_far, gg, gg_far, gu, gu_far, ht_far, hm_far, cot_far, joined, joined_far, normed, normed_far = far_in
            wgrad(core, chunks[0:2], n2, n2_far, gg, gg_far, True)
            at("a0")
            wgrad(core, chunks[2:4], n2, n2_far, gu, gu_far, True)
            at("a1")
            wgrad_down(core, chunks[4:6], ht, hm, ht_far, hm_far, cot, cot_far, lambda: at("a2"))
            at("a3")
        norm_back(core, gn, resid, cot, fgain, gres, low, gain_sum)
        at("a4")
        keep = pltpu.make_async_copy(low, low_out, one)
        keep.start()
        low_swap = swap(0, low, low_far)
        low_swap.start()
        turn(
            core, seqs, length, low, ow, gate, h, p, entry, rate, sp, ggate, lc, q, carry, gm,
            spaced(exchange, "t", 2) if own else no_pump,
        )
        gate_swap = swap(1, ggate.at[0], ggate_far)
        gate_swap.start()
        arriving = Entry(carry, got, seq_n, send, recv)
        arriving.start()
        keep.wait()
        low_swap.wait()
        if own:
            at("b0")
            exchange.free(0)
            wgrad(core, chunks[6:7], joined, joined_far, low_out, low_far, False)
            at("b1")
        arriving.finish(cin, True)
        gate_swap.wait()
        at("b2")
        gates_back(
            own, core, seqs, length, lc, q, cin, h, p, entry, rate, inlet, mixed, branch, edge, wr, wi, taps, sp, sg,
            gb, head, tail, blocks, rate_sum, inlet_sum, small.at[0], dr, di, gr, gi, gm, ext,
            spaced(exchange, "g", 2) if own else no_pump,
        )

        to_left = pltpu.make_async_remote_copy(
            src_ref=head, dst_ref=ahead, send_sem=swap_send.at[2], recv_sem=swap_recv.at[2],
            device_id=(lax.rem(seq + seq_n - 1, seq_n), bat), device_id_type=MESH,
        )
        to_left.start()
        if own:
            at("c0")
            exchange.free(1)
            wgrad(core, chunks[7:8], normed, normed_far, ggate.at[1], ggate_far, True)
            at("c1")
        to_left.wait()
        weight = (seq < seq_n - 1).astype(F32)
        copies = []
        for i in range(2):
            mine = (1 - i) * (1 - core) + i * core
            for s in range(seqs):
                y = ahead[mine, 8 * s : 8 * s + 8, :] * weight
                t = tail[mine, 16 * s : 16 * s + 16, :]
                grown = jnp.concatenate([jnp.zeros((16, width), F32), y], axis=0)
                for k in range(1, 4):
                    t = t + taps[k : k + 1, pl.ds(pl.multiple_of(mine * width, 128), width)] * grown[k : k + 16]
                fixed[i, 16 * s : 16 * s + 16, :] = t.astype(BF16)
                copy = pltpu.make_async_copy(
                    fixed.at[i, 16 * s : 16 * s + 16], gb.at[i, (s + 1) * length - 16 : (s + 1) * length], local.at[i, s]
                )
                copy.start()
                copies.append(copy)
        for copy in copies:
            copy.wait()
        branch_swap = swap(3, gb.at[0], gb_far)
        branch_swap.start()
        at("c2")
        branch_swap.wait()
        at("c3")
        if own:
            exchange.free(2)
            wgrad(core, chunks[8:9], normed, normed_far, gb.at[1], gb_far, True)
            at("c4")

        begin = spaced(exchange, "i", 4) if own else no_pump
        tile = 128
        acc[...] = jnp.zeros_like(acc)

        def input_grad(gg_ref, gb_ref, gwt, gwm, bwt, bwm, x_ref, gr_ref, out):
            pump = begin()
            d = nt(gg_ref[0], gwt[...]) + nt(gg_ref[1], gwm[...]) + nt(gb_ref[0], bwt[...]) + nt(gb_ref[1], bwm[...])
            x = x_ref[...].astype(F32)
            r = lax.rsqrt(jnp.mean(x * x, axis=-1, keepdims=True) + 1e-06)
            xr, dg = x * r, d * mgain[...]
            out[...] = gr_ref[...] + r * (dg - xr * jnp.mean(dg * xr, axis=-1, keepdims=True))
            acc[...] += jnp.sum(d * xr, axis=0, keepdims=True)
            pump()

        row = pl.BlockSpec((tile, model), lambda i: (i, 0))
        pair = pl.BlockSpec((2, tile, width), lambda i: (0, i, 0))
        side = lambda c: pl.BlockSpec((model, width), lambda i: (0, c), pipeline_mode=pl.Buffered(1))
        pltpu.emit_pipeline(
            input_grad, grid=(rows // tile,), in_specs=[pair, pair, side(1 - core), side(core), side(1 - core), side(core), row, row], out_specs=[row]
        )(ggate, gb, gw, gw, bw, bw, tok, gres, tokens_grad)

        small[0, 8:9, 0:model] = acc[...]
        small[0, 9:10, 0:model] = gain_sum[...]

        def small_step(k):
            return pltpu.make_async_remote_copy(
                src_ref=small.at[0], dst_ref=small.at[k + 1], send_sem=s_send.at[k], recv_sem=s_recv.at[k],
                device_id=peers[k], device_id_type=MESH,
            )

        def small_event(k):
            small_step(k).wait()
            small[0] = small[0] + small[k + 1]
            if k + 1 < n_steps:
                small_step(k + 1).start()

        small_events = [functools.partial(small_event, k) for k in range(n_steps)]
        small_step(0).start()
        if own:
            exchange.further[7] = small_events
        begin_out = spaced(exchange, "o", 4) if own else no_pump
        tile_out = 256

        def last(r, ha, hb, fa, fb, out):
            pump = begin_out()
            out[...] = (r[...] + nn(ha[...], fa[...]) + nn(hb[...], fb[...])).astype(BF16)
            pump()

        col = pl.BlockSpec((rows, tile_out), lambda i: (0, i))
        hid = pl.BlockSpec((rows, units // 2), lambda i: (0, 0), pipeline_mode=pl.Buffered(1))
        down = lambda c: pl.BlockSpec((units // 2, tile_out), lambda i: (c, i))
        pltpu.emit_pipeline(last, grid=(model // tile_out,), in_specs=[col, hid, hid, down(1 - core), down(core)], out_specs=[col])(
            resid, ht, hm, fd, fd, block_out
        )
        if own:
            exchange.drain()
        else:
            for event in small_events:
                event()
        totals[...] = small[0]

    f = lambda *shape: jax.ShapeDtypeStruct(shape, F32)
    b = lambda *shape: jax.ShapeDtypeStruct(shape, BF16)
    vm, dma = pltpu.VMEM, lambda *shape: pltpu.SemaphoreType.DMA(shape)
    out_shape = [
        f(rows, model), b(rows, model), f(16, lru),
        f(rows, model), b(rows, model), b(rows, model), b(2, rows, width), b(rows, width), f(rows, lru), f(rows, lru), b(2, rows, width), b(rows, width),
    ]
    out_specs = [ANY, ANY, INSIDE] + [ANY] * 9
    scratch = [
        vm((rows, model), BF16), vm((2, 2, seqs, width), F32), vm((seq_n, 2, 2, seqs, width), F32), vm((2, seqs, width), F32),
        vm((sub, sub), BF16), vm((sub, sub), BF16), vm((rows, width), BF16), vm((rows, width), BF16),
        vm((seqs, length + 8, width), F32), vm((seqs, length + 8, width), F32), vm((2, 8 * seqs, width), F32), vm((2, 16 * seqs, width), F32),
        vm((2, 8 * seqs, width), F32), vm((2, 16 * seqs, width), BF16), vm((1, model), F32), vm((1, model), F32), vm((n_steps + 1, 16, lru), F32),
        dma(seq_n), dma(seq_n), dma(4), dma(4), pltpu.SemaphoreType.DMA, dma(2, seqs), dma(n_steps), dma(n_steps),
    ]
    if own:
        out_shape += [b(9, 2, 2, PART, 128), b(4 * per, bw_, 128)]
        out_specs += [INSIDE, INSIDE]
        scratch += [vm((16, 2 * PART, 128), BF16)] * 3 + Exchange.scratch(9, PART)
        scratch += [vm((4 * per, bw_, 128), BF16)] + BlockSums.scratch(bw_)
    else:
        out_shape += [f(*wr.shape), f(*wi.shape)]
        out_specs += [INSIDE, INSIDE]
    ins = [ANY] * (len(grads_in) + len(values))
    for j in (3, 17, 22):
        ins[len(grads_in) + j] = INSIDE
    return pl.pallas_call(
        kernel,
        in_specs=ins,
        out_specs=out_specs,
        out_shape=out_shape,
        scratch_shapes=scratch,
        compiler_params=pltpu.CompilerParams(collective_id=collective_id, has_side_effects=True, vmem_limit_bytes=60 * 2**20),
        name="backward",
    )(*grads_in, *values)


def lay(sums, model, lru, units, n):
    shapes = [(model // n, units), (model // n, units), (units // n, model), (lru // n, model), (model // n, lru), (model // n, lru)]

    def kernel(v, *outs):
        first = 0
        for out in outs:
            part, wide = out.shape
            for t in range(wide // 128):
                at = t * part
                out[:, t * 128 : (t + 1) * 128] = v[first + at // PART, 0, 0, at % PART : at % PART + part, :].astype(F32)
            first += part * wide // 128 // PART

    return pl.pallas_call(
        kernel,
        grid=(4,),
        in_specs=[pl.BlockSpec((9, 1, 1, PART, 128), lambda i: (0, i // 2, i % 2, 0, 0))],
        out_specs=[pl.BlockSpec((part, wide // 4), lambda i: (0, i)) for part, wide in shapes],
        out_shape=[jax.ShapeDtypeStruct(shape, F32) for shape in shapes],
        compiler_params=params(),
        name="lay",
    )(sums)


def shifted(value, axis, steps):
    count = lax.axis_size(axis)
    return lax.ppermute(value, axis, [(i, i + steps) for i in range(count) if 0 <= i + steps < count])


def swap(value):
    count = lax.axis_size("batch")
    return lax.ppermute(value, "batch", [(i, i ^ 1) for i in range(count)])


def local(
    tokens, cotangent, gate_weight, branch_weight, out_weight, conv_taps, conv_offset, rate_weight, inlet_weight,
    rate_offset, inlet_offset, decay_param, mixer_gain, feed_gain, feed_gate, feed_up, feed_down,
):
    seqs, length, model = tokens.shape
    lru, units = gate_weight.shape[1], feed_gate.shape[1]
    rows = seqs * length
    seq_n, batch_n = lax.axis_size("seq"), lax.axis_size("batch")
    core = lax.rem(lax.axis_index("batch"), 2)
    half = jnp.full((1,), core, jnp.int32)

    halo = shifted(tokens[:, length - 8 :, :], "seq", 1).reshape(8 * seqs, model)
    tok, cot = tokens.reshape(rows, model), cotangent.reshape(rows, model)
    cot_far = swap(cot)
    soft, sgm = jax.nn.softplus(decay_param)[None], jax.nn.sigmoid(decay_param)[None]
    gain1, gain2 = mixer_gain[None], feed_gain[None]

    normed, gate, branch, edge, mixed, rate, inlet, h, p, carry = front(
        tok, halo, gain1, gate_weight, branch_weight, conv_taps, conv_offset[None], rate_weight, inlet_weight,
        rate_offset[None], inlet_offset[None], soft, seqs, length,
    )
    normed_far = swap(normed)
    entry = entry_state(carry, seq_n, False, 0)
    joined, resid, normed_two = join(tok, gate, h, p, entry, out_weight, gain2, seqs, length)
    joined_far, normed_two_far = swap(joined), swap(normed_two)
    hid_t, gg_t, gu_t, acc = feed(1 - half, normed_two, cot, feed_gate, feed_up, feed_down, None)
    hid_t_far, gg_far, gu_far = swap(hid_t), swap(gg_t), swap(gu_t)
    hid_m, gg_m, gu_m, grad_two = feed(half, normed_two, cot, feed_gate, feed_up, feed_down, acc)
    hid_m_far = swap(hid_m)

    own = (seq_n, batch_n) == (8, 4)
    grads_in = [normed_two, normed_two_far, gg_m, gg_far, gu_m, gu_far, hid_t_far, hid_m_far, cot_far, joined, joined_far, normed, normed_far]
    tokens_grad, out, totals, _, grad_low, _, ggate, _, _, _, gb, _, *sums = backward(
        own, seqs, length, seq_n, batch_n, grads_in,
        [
            grad_two, resid, cot, gain2, out_weight, gate, h, p, entry.reshape(seqs, 1, lru), rate, soft, inlet, mixed, branch, edge,
            rate_weight, inlet_weight, conv_taps, sgm, gate_weight, branch_weight, tok, gain1, hid_t, hid_m, feed_down,
        ],
        1,
    )
    if own:
        gate_feed_all, up_feed_all, down_all, out_all, gate_all, branch_all = lay(sums[0], model, lru, units, seq_n)
        count, wide = rate_weight.shape[0], rate_weight.shape[2]
        rate_all, inlet_all = sums[1][:count, :, :wide].astype(F32), sums[1][count:, :, :wide].astype(F32)
    else:
        rate_all, inlet_all = lax.psum((sums[0], sums[1]), ("seq", "batch"))

        def full(theirs, mine):
            a, b = jnp.where(core == 0, mine, theirs), jnp.where(core == 0, theirs, mine)
            return jnp.concatenate([a, b], axis=1)

        def total(left, right):
            return lax.psum(lax.psum_scatter(tn(left, right), "seq", scatter_dimension=0, tiled=True), "batch")

        down_all = total(full(hid_t, hid_m), cot)
        gate_feed_all = total(normed_two, full(gg_t, gg_m))
        up_feed_all = total(normed_two, full(gu_t, gu_m))
        out_all = total(joined, grad_low)
        gate_all = total(normed, full(ggate[0], ggate[1]))
        branch_all = total(normed, full(gb[0], gb[1]))

    return (
        out.reshape(seqs, length, model), tokens_grad.reshape(seqs, length, model), gate_all, branch_all, out_all,
        totals[0:4], totals[7], rate_all, inlet_all, totals[5], totals[6], totals[4], totals[8, :model], totals[9, :model],
        gate_feed_all, up_feed_all, down_all,
    )


def solution(mesh):
    big = P("batch", "seq", None)
    in_specs = (big, big) + (P(),) * 15
    out_specs = (big, big) + (P("seq", None),) * 3 + (P(),) * 9 + (P("seq", None),) * 3
    return jax.shard_map(local, mesh=mesh, in_specs=in_specs, out_specs=out_specs, check_vma=False)
```

```python
import functools
import jax
import jax.numpy as jnp
from jax import lax
from jax.experimental import pallas as pl
from jax.experimental.pallas import tpu as pltpu
from jax.sharding import PartitionSpec as P

F32, BF16 = jnp.float32, jnp.bfloat16
VLIM = 56 * 2**20
GELU_A, GELU_B = 0.7978845608028654, 0.044715


def nn(a, b):
    return lax.dot_general(a, b, (((1,), (0,)), ((), ())), preferred_element_type=F32)


def nt(a, b):
    return lax.dot_general(a, b, (((1,), (1,)), ((), ())), preferred_element_type=F32)


def tn(a, b):
    return lax.dot_general(a, b, (((0,), (0,)), ((), ())), preferred_element_type=F32)


def sigmoid(v):
    return 1.0 / (1.0 + jnp.exp(-v))


def drop(u, decay):
    v = 2.0 * u
    series = 1.0 + v * (1.0 / 7.0)
    for k in (6.0, 5.0, 4.0, 3.0, 2.0):
        series = 1.0 + (v * (1.0 / k)) * series
    return jnp.where(v > -0.35, -v * series, 1.0 - decay * decay)


def gelu_parts(v):
    square = v * v
    inner = jnp.tanh(GELU_A * v * (1.0 + GELU_B * square))
    half = 0.5 + 0.5 * inner
    act = v * half
    slope = half + 0.5 * v * (1.0 - inner * inner) * (GELU_A + 3.0 * GELU_A * GELU_B * square)
    return act, slope


def gelu(v):
    inner = jnp.tanh(GELU_A * v * (1.0 + GELU_B * (v * v)))
    return v * (0.5 + 0.5 * inner)


def spread(dense, blocks, count, width):
    for a in range(count):
        parts = []
        if a > 0:
            parts.append(jnp.zeros((width, a * width), dense.dtype))
        parts.append(blocks[a])
        if a < count - 1:
            parts.append(jnp.zeros((width, (count - 1 - a) * width), dense.dtype))
        dense[a * width : (a + 1) * width, :] = jnp.concatenate(parts, axis=1)


def params(sem=("arbitrary",), **kw):
    return pltpu.CompilerParams(dimension_semantics=sem, vmem_limit_bytes=VLIM, **kw)


def whole(shape):
    return pl.BlockSpec(shape, lambda *_: (0,) * len(shape))


MESH = pl.DeviceIdType.MESH


def meet(peers):
    barrier = pltpu.get_barrier_semaphore()
    for peer in peers:
        pl.semaphore_signal(barrier, inc=1, device_id=peer, device_id_type=MESH)
    pl.semaphore_wait(barrier, len(peers))


def flip(index, bit):
    return index + bit - 2 * bit * (lax.rem(index // bit, 2))


class Entry:
    def __init__(self, part, got, n, send, recv):
        self.part, self.got, self.n = part, got, n
        self.me = lax.axis_index("seq")
        self.copies = [
            pltpu.make_async_remote_copy(
                src_ref=part, dst_ref=got.at[self.me], send_sem=send.at[k], recv_sem=recv.at[k],
                device_id=(lax.rem(self.me + k, n), lax.axis_index("batch")), device_id_type=MESH,
            )
            for k in range(1, n)
        ]

    def start(self):
        for copy in self.copies:
            copy.start()
        self.got[self.me] = self.part[...]

    def finish(self, out, reverse):
        for copy in self.copies:
            copy.wait()

        def one(k, state):
            j = self.n - 1 - k if reverse else k
            before = (j > self.me) if reverse else (j < self.me)
            return jnp.where(before, self.got[j, :, 0] * state + self.got[j, :, 1], state)

        out[...] = lax.fori_loop(0, self.n, one, jnp.zeros(out.shape, F32))


def front_kernel(
    seqs, length, seq_n, tok, gain, gw, bw, taps, vec, wr, wi,
    normed, gate, branch, edge, mixed, rate, inlet, h, p, entry,
    halo, hn, ext, dr, di, rp, ip, carry, got, state, h_send, h_recv, send, recv,
):
    rows, width = seqs * length, gw.shape[1]
    sub = dr.shape[-1]

    seq, bat = lax.axis_index("seq"), lax.axis_index("batch")

    @pl.when(pl.program_id(0) == 0)
    def _():
        meet([(lax.rem(seq + k, seq_n), bat) for k in range(1, seq_n)])
        copies = [
            pltpu.make_async_remote_copy(
                src_ref=tok.at[(s + 1) * length - 16 : (s + 1) * length], dst_ref=halo.at[s], send_sem=h_send.at[s], recv_sem=h_recv.at[s],
                device_id=(lax.rem(seq + 1, seq_n), bat), device_id_type=MESH,
            )
            for s in range(seqs)
        ]
        for copy in copies:
            copy.start()

        def norm(i, _):
            x = tok[pl.ds(i * 32, 32), :].astype(F32)
            r = lax.rsqrt(jnp.mean(x * x, axis=-1, keepdims=True) + 1e-06)
            normed[pl.ds(i * 32, 32), :] = (x * r * gain[...]).astype(BF16)
            return 0

        lax.fori_loop(0, rows // 32, norm, 0)
        for s in range(seqs):
            copies[s].wait()
            x = halo[s].astype(F32)
            r = lax.rsqrt(jnp.mean(x * x, axis=-1, keepdims=True) + 1e-06)
            hn[16 * s : 16 * s + 16, :] = (x * r * gain[...]).astype(BF16)

    gate[...] = nn(normed[...], gw[...])
    b16 = nn(normed[...], bw[...]).astype(BF16)
    e16 = (nn(hn[...], bw[...]) * (seq > 0).astype(F32)).astype(BF16)
    branch[...] = b16
    edge[...] = e16
    e32 = e16.astype(F32)
    for s in range(seqs):
        ext[s, 0:8, :] = e32[16 * s + 8 : 16 * s + 16]
        ext[s, 8 : 8 + length, :] = b16[length * s : length * (s + 1)].astype(F32)

    tap = [taps[k : k + 1, :] for k in range(4)]
    off = vec[0:1, :]
    for s in range(seqs):

        def conv(i, _):
            x = ext[s, pl.ds(pl.multiple_of(i * 16, 16), 24), :]
            total = off + tap[0] * x[8:24]
            for k in range(1, 4):
                total = total + tap[k] * x[8 - k : 24 - k]
            mixed[pl.ds(pl.multiple_of(s * length + i * 16, 16), 16), :] = total.astype(BF16)
            return 0

        lax.fori_loop(0, length // 16, conv, 0)

    for g in range(width // sub):
        cols = slice(g * sub, (g + 1) * sub)
        spread(dr.at[g], [wr[g * 4 + a] for a in range(4)], 4, wr.shape[-1])
        spread(di.at[g], [wi[g * 4 + a] for a in range(4)], 4, wi.shape[-1])
        rp[:, cols] = nn(mixed[:, cols], dr[g])
        ip[:, cols] = nn(mixed[:, cols], di[g])

    ro, io, slope = vec[1:2, :], vec[2:3, :], -8.0 * vec[3:4, :]

    def gates(i, _):
        at = pl.ds(pl.multiple_of(i * 16, 16), 16)
        rt = sigmoid(rp[at, :] + ro)
        it = sigmoid(ip[at, :] + io)
        log_decay = rt * slope
        decay = jnp.exp(log_decay)
        rate[at, :] = rt
        inlet[at, :] = it
        p[at, :] = decay
        h[at, :] = jnp.sqrt(drop(log_decay, decay)) * it * mixed[at, :].astype(F32)
        return 0

    lax.fori_loop(0, rows // 16, gates, 0)

    row = lax.broadcasted_iota(jnp.int32, (8, width), 0)

    def scan(i, last):
        out = []
        for s in range(seqs):
            at = pl.ds(pl.multiple_of(s * length + i * 8, 8), 8)
            a, b = p[at, :], h[at, :]
            for d in (1, 2, 4):
                keep = row >= d
                b = b + a * jnp.where(keep, pltpu.roll(b, d, 0), 0.0)
                a = a * jnp.where(keep, pltpu.roll(a, d, 0), 1.0)
            ap, bp = last[s]
            b = b + a * bp
            a = a * ap
            p[at, :] = a
            h[at, :] = b
            out.append((a[7:8], b[7:8]))
        return tuple(out)

    init = tuple((jnp.ones((1, width), F32), jnp.zeros((1, width), F32)) for _ in range(seqs))
    last = lax.fori_loop(0, length // 8, scan, init)
    for s in range(seqs):
        carry[pl.program_id(0), 0, s : s + 1, :] = last[s][0]
        carry[pl.program_id(0), 1, s : s + 1, :] = last[s][1]

    @pl.when(pl.program_id(0) == 1)
    def _():
        arriving = Entry(carry, got, seq_n, send, recv)
        arriving.start()
        arriving.finish(state, False)
        for g in range(2):
            for s in range(seqs):
                entry[s, :, g * width : (g + 1) * width] = state[g, s : s + 1, :]


def front(tok, gain, gw, bw, taps, vec, wr, wi, seqs, length, seq_n, collective_id):
    rows, model = tok.shape
    lru, bw_ = gw.shape[1], wr.shape[-1]
    width, sub, per = lru // 2, 4 * bw_, lru // 2 // bw_
    col = lambda r: pl.BlockSpec((r, width), lambda j: (0, j))
    blk = pl.BlockSpec((per, bw_, bw_), lambda j: (j, 0, 0))
    f = lambda dt: jax.ShapeDtypeStruct((rows, lru), dt)
    vm, dma = pltpu.VMEM, lambda n: pltpu.SemaphoreType.DMA((n,))
    return pl.pallas_call(
        functools.partial(front_kernel, seqs, length, seq_n),
        grid=(2,),
        in_specs=[
            whole((rows, model)), whole((1, model)),
            pl.BlockSpec((model, width), lambda j: (0, j)), pl.BlockSpec((model, width), lambda j: (0, j)), col(4), col(8), blk, blk,
        ],
        out_specs=[
            whole((rows, model)), col(rows), col(rows), col(16 * seqs), col(rows), col(rows), col(rows), col(rows), col(rows),
            whole((seqs, 1, lru)),
        ],
        out_shape=[
            jax.ShapeDtypeStruct((rows, model), BF16), f(F32), f(BF16),
            jax.ShapeDtypeStruct((16 * seqs, lru), BF16), f(BF16), f(F32), f(F32), f(F32), f(F32),
            jax.ShapeDtypeStruct((seqs, 1, lru), F32),
        ],
        scratch_shapes=[
            vm((seqs, 16, model), BF16), vm((16 * seqs, model), BF16), vm((seqs, 8 + length, width), F32),
            vm((2, sub, sub), BF16), vm((2, sub, sub), BF16), vm((rows, width), F32), vm((rows, width), F32),
            vm((2, 2, seqs, width), F32), vm((seq_n, 2, 2, seqs, width), F32), vm((2, seqs, width), F32),
            dma(seqs), dma(seqs), dma(seq_n), dma(seq_n),
        ],
        compiler_params=params(collective_id=collective_id, has_side_effects=True),
        name="front",
    )(tok, gain, gw, bw, taps, vec, wr, wi)


def join_kernel(tok, gate, h, p, entry, ow, gain, joined, resid, normed, state_ref):
    rows = tok.shape[0]
    ent = entry[0]

    def join(i, _):
        at = pl.ds(pl.multiple_of(i * 16, 16), 16)
        state = h[at, :] + p[at, :] * ent
        state_ref[at, :] = state
        joined[at, :] = (gelu(gate[at, :]) * state).astype(BF16)
        return 0

    lax.fori_loop(0, rows // 16, join, 0)
    resid[...] = nn(joined[...], ow[...])

    def norm(i, _):
        at = pl.ds(pl.multiple_of(i * 32, 32), 32)
        y = tok[at, :].astype(F32) + resid[at, :]
        resid[at, :] = y
        r = lax.rsqrt(jnp.mean(y * y, axis=-1, keepdims=True) + 1e-06)
        normed[at, :] = (y * r * gain[...]).astype(BF16)
        return 0

    lax.fori_loop(0, rows // 32, norm, 0)


def join(tok, gate, h, p, entry, ow, gain, seqs, length):
    rows, model = tok.shape
    lru = gate.shape[1]
    tile = 128
    per = length // tile
    row = lambda w: pl.BlockSpec((tile, w), lambda i: (i, 0))
    return pl.pallas_call(
        join_kernel,
        grid=(rows // tile,),
        in_specs=[row(model), row(lru), row(lru), row(lru), pl.BlockSpec((1, 1, lru), lambda i: (i // per, 0, 0)), whole((lru, model)), whole((1, model))],
        out_specs=[row(lru), row(model), row(model), row(lru)],
        out_shape=[jax.ShapeDtypeStruct((rows, lru), BF16), jax.ShapeDtypeStruct((rows, model), F32), jax.ShapeDtypeStruct((rows, model), BF16), jax.ShapeDtypeStruct((rows, lru), F32)],
        compiler_params=params(),
        name="join",
    )(tok, gate, h, p, entry, ow, gain)


ORDERS = {"A": ("xhyl", "yxhl"), "E": ("xlhy", "yxlh"), "F": ("xylh", "yxlh")}


class Exchange:
    def __init__(self, chunks, bufs, fin, send, recv):
        self.chunks, self.bufs, self.fin, self.sems = chunks, bufs, fin, (send, recv)
        self.first = [sum(c[2] for c in chunks[:q]) for q in range(len(chunks))]
        seq, bat = lax.axis_index("seq"), lax.axis_index("batch")
        core, y = lax.rem(bat, 2), bat // 2
        x, low, high = lax.rem(seq, 2), lax.rem(seq // 2, 2), seq // 4
        bit = {"x": x, "y": y, "l": low, "h": high}
        move = {"x": (1 - 2 * x, 0), "y": (0, 2 - 4 * y), "l": (2 - 4 * low, 0), "h": (4 - 8 * high, 0)}
        pick = lambda a, b: a if a is b else (1 - core) * a + core * b
        self.core, self.y = core, y
        self.other, self.across = (seq, bat + 1 - 2 * core), (seq, bat + 2 - 4 * y)
        self.bits, self.peers = {}, {}
        for kind, (first, second) in ORDERS.items():
            self.bits[kind] = [pick(bit[a], bit[b]) for a, b in zip(first, second)]
            self.peers[kind] = [
                (seq + pick(move[a][0], move[b][0]), bat + pick(move[a][1], move[b][1])) for a, b in zip(first, second)
            ] + [self.across, self.other]
        self.greet = [(seq + move[a][0], bat) for a in "xlh"] + [self.across, self.other]
        self.freed, self.further = set(), {}

    def at(self, place):
        for k, q in PLAN.get(place, ()):
            self.step(k, q)

    def free(self, q):
        self.copy(0, q).wait_send()
        self.freed.add(q)

    def drain(self):
        self.at("drain")
        for q in range(len(self.chunks)):
            for k in range(4):
                if k > 0 or q not in self.freed:
                    self.copy(k, q).wait_send()

    def copy(self, k, q):
        grad, row, part, kind = self.chunks[q]
        size, bits = 8 >> k, self.bits[kind]
        at = slice(self.first[q], self.first[q] + part)
        if k == 0:
            src, dst = grad.at[pl.ds((1 - bits[0]) * 8, 8), row : row + part], self.bufs[0].at[:, at]
        elif k < 4:
            src, dst = self.bufs[k - 1].at[pl.ds((1 - bits[k]) * size, size), at], self.bufs[k].at[:, at]
        elif k == 4:
            src = dst = self.fin.at[self.core, self.y, at]
        else:
            src = dst = self.fin.at[self.core, :, at]
        return pltpu.make_async_remote_copy(
            src_ref=src, dst_ref=dst, send_sem=self.sems[0].at[k, q], recv_sem=self.sems[1].at[k, q],
            device_id=self.peers[kind][k], device_id_type=MESH,
        )

    def add(self, k, q, base, size):
        grad, row, part, kind = self.chunks[q]
        dst, bits = self.bufs[k], self.bits[kind]
        for j in range(size):

            def body(i, _):
                a = pl.ds(pl.multiple_of(self.first[q] + i * 128, 128), 128)
                if k == 0:
                    own = grad[bits[0] * 8 + base + j, pl.ds(pl.multiple_of(row + i * 128, 128), 128), :]
                else:
                    own = self.bufs[k - 1][bits[k] * (8 >> k) + base + j, a, :]
                dst[base + j, a, :] = dst[base + j, a, :] + own
                return 0

            lax.fori_loop(0, part // 128, body, 0)

    def step(self, k, q):
        if k > 5:
            self.further[k][q]()
        elif k < 0:
            self.copy(0, q).start()
        elif k < 3:
            half, bits = 4 >> k, self.bits[self.chunks[q][3]]
            self.copy(k, q).wait_recv()
            self.add(k, q, (1 - bits[k + 1]) * half, half)
            self.copy(k + 1, q).start()
            self.add(k, q, bits[k + 1] * half, half)
        elif k == 3:
            bits = self.bits[self.chunks[q][3]]
            self.copy(3, q).wait_recv()

            def body(i, _):
                a = pl.ds(pl.multiple_of(self.first[q] + i * 128, 128), 128)
                self.fin[self.core, self.y, a, :] = self.bufs[3][0, a, :] + self.bufs[2][bits[3], a, :]
                return 0

            lax.fori_loop(0, self.chunks[q][2] // 128, body, 0)
            self.copy(4, q).start()
        elif k == 4:
            self.copy(4, q).wait()
            self.copy(5, q).start()
        else:
            self.copy(5, q).wait()

    @staticmethod
    def scratch(chunks, rows):
        return [pltpu.VMEM((8 >> k, rows, 128), BF16) for k in range(4)] + [pltpu.SemaphoreType.DMA((6, chunks))] * 2


class BlockSums:
    def __init__(self, value, bufs, out, send, recv):
        self.value, self.bufs, self.out, self.sems = value, bufs, out, (send, recv)
        seq, bat = lax.axis_index("seq"), lax.axis_index("batch")
        core, y = lax.rem(bat, 2), bat // 2
        x, low, high = lax.rem(seq, 2), lax.rem(seq // 2, 2), seq // 4
        self.bits = [core, low, high, x, y]
        self.peers = [(seq, bat + 1 - 2 * core), (seq + 2 - 4 * low, bat), (seq + 4 - 8 * high, bat), (seq + 1 - 2 * x, bat), (seq, bat + 2 - 4 * y)]
        self.base = [0]
        for k in range(5):
            self.base.append(self.base[-1] + self.bits[k] * (16 >> k))

    def halve(self, k):
        size = 16 >> k
        return pltpu.make_async_remote_copy(
            src_ref=self.value.at[pl.ds(self.base[k] + (1 - self.bits[k]) * size, size)], dst_ref=self.bufs[k],
            send_sem=self.sems[0].at[k], recv_sem=self.sems[1].at[k], device_id=self.peers[k], device_id_type=MESH,
        )

    def hand(self, k):
        at = pl.ds(self.base[k + 1], 16 >> k)
        return pltpu.make_async_remote_copy(
            src_ref=self.out.at[at], dst_ref=self.out.at[at],
            send_sem=self.sems[0].at[5 + k], recv_sem=self.sems[1].at[5 + k], device_id=self.peers[k], device_id_type=MESH,
        )

    def events(self):
        def took(k):
            size = 16 >> k
            self.halve(k).wait()

            def body(j, _):
                at = self.base[k + 1] + j
                total = (self.value[at].astype(F32) + self.bufs[k][j].astype(F32)).astype(BF16)
                if k < 4:
                    self.value[at] = total
                else:
                    self.out[at] = total
                return 0

            lax.fori_loop(0, size, body, 0)
            if k < 4:
                self.halve(k + 1).start()
            else:
                self.hand(4).start()

        def got(k):
            self.hand(k).wait()
            if k > 0:
                self.hand(k - 1).start()

        first = [lambda: self.halve(0).start()]
        return first + [functools.partial(took, k) for k in range(5)] + [functools.partial(got, k) for k in range(4, -1, -1)]

    @staticmethod
    def scratch(width):
        return [pltpu.VMEM((16 >> k, width, 128), BF16) for k in range(5)] + [pltpu.SemaphoreType.DMA((10,))] * 2


def core_of():
    return lax.rem(lax.axis_index("batch"), 2)


def group(core):
    i = pl.program_id(0)
    return (1 - i) * (1 - core) + i * core


def put_pieces(chunks, row, acc, core, y, s):
    part, cols = acc.shape
    for t in range(cols // 128):
        at = row[t] if isinstance(row, (list, tuple)) else row + t * part
        base = 0
        for ref, first, rows, kind in chunks:
            low, high = max(at, base), min(at + part, base + rows)
            if low < high:
                ref[place_of(core, s, y, kind), first + low - base : first + high - base, :] = acc[
                    low - at : high - at, t * 128 : (t + 1) * 128
                ].astype(BF16)
            base += rows


def place_of(core, s, y, kind):
    bit = {"x": s % 2, "l": (s // 2) % 2, "h": s // 4, "y": y}
    place = lambda order: sum(bit[a] * (8 >> k) for k, a in enumerate(order))
    first, second = ORDERS[kind]
    return place(first) if first == second else (1 - core) * place(first) + core * place(second)


def wgrad(core, chunks, lhs, lhs_far, rhs, rhs_far, own_columns):
    rows, deep = lhs.shape
    tile = rhs.shape[1] // (2 if own_columns else 4)
    base, part = 0 if own_columns else 2 * core, deep // 8

    def body(a, b, c, d):
        acc = tn(a[...], c[...]) + tn(b[...], d[...])
        for s in range(8):
            put_pieces(chunks, 0, acc[s * part : (s + 1) * part], core, pl.program_id(0), s)

    left = pl.BlockSpec(lhs.shape, lambda y: (0, 0), pipeline_mode=pl.Buffered(1))
    right = pl.BlockSpec((rows, tile), lambda y: (0, base + y))
    pltpu.emit_pipeline(body, grid=(2,), in_specs=[left, left, right, right])(lhs, lhs_far, rhs, rhs_far)


def wgrad_up(core, gate_chunk, up_chunk, lhs, lhs_far, rhs, rhs_far, begin):
    rows, deep = lhs.shape
    tile, part = rhs.shape[2], deep // 8

    def body(a, b, c, d):
        pump = begin()
        acc = tn(a[...], c[0]) + tn(b[...], d[0])
        for j, chunk in enumerate((gate_chunk, up_chunk)):

            @pl.when(pl.program_id(0) == j)
            def _():
                for s in range(8):
                    for y in range(2):
                        put_pieces([chunk], 0, acc[s * part : (s + 1) * part, y * tile // 2 : (y + 1) * tile // 2], core, y, s)

        pump()

    left = pl.BlockSpec(lhs.shape, lambda i: (0, 0), pipeline_mode=pl.Buffered(1))
    right = pl.BlockSpec((1, rows, tile), lambda i: (i, 0, 0))
    pltpu.emit_pipeline(body, grid=(2,), in_specs=[left, left, right, right])(lhs, lhs_far, rhs, rhs_far)


def wgrad_down(core, chunks, hid, hid_far, cot, cot_far, begin):
    _, parts, rows, units = hid.shape
    half_cols = cot.shape[1] // 2
    block = 2 * parts * units // 8

    def body(l, m, c, d):
        pump = begin()
        i = pl.program_id(0)
        acc = tn(l[0, 0], c[...]) + tn(m[0, 0], d[...])
        for side in range(2):
            for p in range(parts):

                @pl.when(i == side * parts + p)
                def _():
                    half = core if side else 1 - core
                    for j in range(units // 128):
                        unit = p * units + j * 128
                        s = 4 * half + unit // block
                        row = unit % block
                        for y in range(2):
                            cut = acc[j * 128 : (j + 1) * 128, y * half_cols // 2 : (y + 1) * half_cols // 2]
                            put_pieces(chunks, [row, block + row], cut, core, y, s)

        pump()

    mine = pl.BlockSpec((1, 1, rows, units), lambda i: (i // parts, i % parts, 0, 0))
    theirs = pl.BlockSpec((1, 1, rows, units), lambda i: (1 - i // parts, i % parts, 0, 0))
    right = pl.BlockSpec((rows, half_cols), lambda i: (0, core), pipeline_mode=pl.Buffered(1))
    pltpu.emit_pipeline(body, grid=(2 * parts,), in_specs=[mine, theirs, right, right])(hid, hid_far, cot, cot_far)


def feed(core, part, n2, cot, fg, fu, fd, hid, ups, acc, begin):
    rows, model = n2.shape
    parts, tile = hid.shape[1], hid.shape[3]
    block = rows // 2

    def body(n2_ref, cot_ref, fg_ref, fu_ref, fd_ref, hid_ref, gg_ref, gu_ref):
        pump = begin()
        for r in range(2):
            at = slice(r * block, (r + 1) * block)
            gate, up = nn(n2_ref[at, :], fg_ref[...]), nn(n2_ref[at, :], fu_ref[...])
            g = nt(cot_ref[at, :], fd_ref[...])
            act, slope = gelu_parts(gate)
            hid_ref[0, 0, at, :] = (act * up).astype(BF16)
            gg_ref[0, 0, at, :] = (g * up * slope).astype(BF16)
            gu_ref[0, 0, at, :] = (g * act).astype(BF16)
        total = nt(gg_ref[0, 0], fg_ref[...]) + nt(gu_ref[0, 0], fu_ref[...])
        if part == 0:

            @pl.when(pl.program_id(0) == 0)
            def _():
                acc[...] = total

            @pl.when(pl.program_id(0) > 0)
            def _():
                acc[...] += total

        else:
            acc[...] += total
        pump()

    unit = lambda i: ((1 - i) * (1 - core) + i * core) * parts + part
    flat = pl.BlockSpec((rows, model), lambda i: (0, 0), pipeline_mode=pl.Buffered(1))
    col = pl.BlockSpec((model, tile), lambda i: (0, unit(i)))
    out = pl.BlockSpec((1, 1, rows, tile), lambda i: (i, part, 0, 0))
    pltpu.emit_pipeline(
        body, grid=(2,), in_specs=[flat, flat, col, col, pl.BlockSpec((tile, model), lambda i: (unit(i), 0))], out_specs=[out, out, out]
    )(n2, cot, fg, fu, fd, hid, ups.at[0], ups.at[1])


def norm_back(core, gn, resid, cot, fgain, gres, low, gain_sum):
    rows, model = gn.shape
    tile = 128
    gain_sum[...] = jnp.zeros_like(gain_sum)

    def body(y_ref, c_ref, out_ref):
        g = fgain[...]

        def norm(i, total):
            at = pl.ds(pl.multiple_of(i * 16, 16), 16)
            place = pl.ds(pl.multiple_of(pl.program_id(0) * tile + i * 16, 16), 16)
            y, d = y_ref[at, :], gn[place, :]
            r = lax.rsqrt(jnp.mean(y * y, axis=-1, keepdims=True) + 1e-06)
            dg, yr = d * g, y * r
            dot = jnp.mean(dg * yr, axis=-1, keepdims=True)
            out = c_ref[at, :].astype(F32) + r * (dg - yr * dot)
            out_ref[at, :] = out
            low[place, :] = out.astype(BF16)
            add = d * yr
            return total + add[0:8] + add[8:16]

        total = lax.fori_loop(0, tile // 16, norm, jnp.zeros((8, model), F32))
        gain_sum[...] += jnp.sum(total, axis=0, keepdims=True)

    row = pl.BlockSpec((tile, model), lambda i: (i, 0))
    pltpu.emit_pipeline(body, grid=(rows // tile,), in_specs=[row, row], out_specs=[row])(resid, cot, gres)


def turn(core, seqs, length, low, ow, gate, state, rate, vec, ggate, lc, q, carry, gj, begin):
    rows, lru = gate.shape
    width = lru // 2

    def body(ow_ref, gate_ref, state_ref, rate_ref, vec_ref, gg_ref, lc_ref, q_ref):
        pump = begin()
        for s in range(seqs):
            gj[s, 0:length, :] = nt(low[s * length : (s + 1) * length, :], ow_ref[...])
        pump()
        slope = -8.0 * vec_ref[3:4, :]
        for s in range(seqs):

            def act(i, _):
                at = pl.ds(pl.multiple_of(s * length + i * 16, 16), 16)
                here = pl.ds(pl.multiple_of(i * 16, 16), 16)
                value, der = gelu_parts(gate_ref[at, :])
                d = gj[s, here, :]
                gg_ref[0, at, :] = (d * state_ref[at, :] * der).astype(BF16)
                gj[s, here, :] = d * value
                return 0

            lax.fori_loop(0, length // 16, act, 0)
            pump()

        row = lax.broadcasted_iota(jnp.int32, (8, width), 0)
        tiles = length // 8

        def scan(k, last):
            i = tiles - 1 - k
            out = []
            for s in range(seqs):
                at = pl.ds(pl.multiple_of(s * length + i * 8, 8), 8)
                g = gj[s, pl.ds(pl.multiple_of(i * 8, 8), 8), :]
                a = jnp.exp(rate_ref[at, :] * slope)
                b = a * g
                for d in (1, 2, 4):
                    keep = row < 8 - d
                    b = b + a * jnp.where(keep, pltpu.roll(b, 8 - d, 0), 0.0)
                    a = a * jnp.where(keep, pltpu.roll(a, 8 - d, 0), 1.0)
                ap, bp = last[s]
                b = b + a * bp
                a = a * ap
                lc_ref[at, :] = g + jnp.where(row < 7, pltpu.roll(b, 7, 0), bp)
                q_ref[at, :] = jnp.where(row < 7, pltpu.roll(a, 7, 0), ap)
                out.append((a[0:1], b[0:1]))
            return tuple(out)

        init = tuple((jnp.ones((1, width), F32), jnp.zeros((1, width), F32)) for _ in range(seqs))
        last = lax.fori_loop(0, tiles, scan, init)
        for s in range(seqs):
            carry[group(core), 0, s : s + 1, :] = last[s][0]
            carry[group(core), 1, s : s + 1, :] = last[s][1]
        pump()

    grp = lambda i: (1 - i) * (1 - core) + i * core
    col = lambda r: pl.BlockSpec((r, width), lambda i: (0, grp(i)))
    pltpu.emit_pipeline(
        body, grid=(2,),
        in_specs=[
            pl.BlockSpec((width, ow.shape[1]), lambda i: (grp(i), 0)), col(rows), col(rows), col(rows), col(8),
        ],
        out_specs=[pl.BlockSpec((1, rows, width), lambda i: (i, 0, 0)), col(rows), col(rows)],
    )(ow, gate, state, rate, vec, ggate, lc, q)


def gates_back(
    own, core, seqs, length, lc, q, cin, states, entry, rate, inlet, mixed, branch, edge, wr, wi, taps, vec,
    gb, head, tail, blocks, rate_sum, inlet_sum, sums_out, dr, di, gr, gi, gm, ext, begin,
):
    rows, lru = lc.shape
    width, bw_ = lru // 2, wr.shape[-1]
    per, sub = width // bw_, dr.shape[-1]

    def body(
        lc_ref, q_ref, state_ref, e_ref, rate_ref, inlet_ref, mixed_ref, branch_ref, edge_ref, wr_ref, wi_ref, taps_ref, vec_ref,
        gb_ref,
    ):
        pump = begin()
        mine = group(core)
        slope = -8.0 * vec_ref[3:4, :]
        zero = jnp.zeros((8, width), F32)
        row = lax.broadcasted_iota(jnp.int32, (16, width), 0)

        sums = (zero, zero, zero)
        for s in range(seqs):
            c_in, ent = cin[mine, s : s + 1, :], e_ref[s]

            def gates(i, carry):
                (before, t0, t1, t2) = carry
                at = pl.ds(pl.multiple_of(s * length + i * 16, 16), 16)
                state = state_ref[at, :]
                prev = jnp.where(row > 0, pltpu.roll(state, 1, 0), before)
                carried = lc_ref[at, :] + q_ref[at, :] * c_in
                rt, it, mx = rate_ref[at, :], inlet_ref[at, :], mixed_ref[at, :].astype(F32)
                log_decay = rt * slope
                decay = jnp.exp(log_decay)
                gap = drop(log_decay, decay)
                inv = lax.rsqrt(gap)
                nf = gap * inv
                im = it * mx
                g_log = carried * decay * (prev - im * decay * inv)
                cn = carried * nf
                g_rt = g_log * slope * (rt * (1.0 - rt))
                g_it = cn * im * (1.0 - it)
                gr[at, :] = g_rt.astype(BF16)
                gi[at, :] = g_it.astype(BF16)
                gm[s, pl.ds(pl.multiple_of(i * 16, 16), 16), :] = cn * it
                lr = g_log * rt
                return (state[15:16], t0 + lr[0:8] + lr[8:16], t1 + g_rt[0:8] + g_rt[8:16], t2 + g_it[0:8] + g_it[8:16])

            _, *sums = lax.fori_loop(0, length // 16, gates, (ent, *sums))
            pump()
        down = lambda v: jnp.sum(v, axis=0, keepdims=True)
        lanes = pl.ds(pl.multiple_of(mine * width, 128), width)
        sums_out[4:5, lanes] = down(sums[0]) * (-8.0 * vec_ref[4:5, :])
        sums_out[5:6, lanes] = down(sums[1])
        sums_out[6:7, lanes] = down(sums[2])

        for g in range(width // sub):
            cols = slice(g * sub, (g + 1) * sub)
            spread(dr, [wr_ref[g * 4 + a] for a in range(4)], 4, bw_)
            spread(di, [wi_ref[g * 4 + a] for a in range(4)], 4, bw_)
            back = nt(gr[:, cols], dr[...]) + nt(gi[:, cols], di[...])
            rs = tn(mixed_ref[:, cols], gr[:, cols])
            is_ = tn(mixed_ref[:, cols], gi[:, cols])
            for a in range(4):
                block = slice(a * bw_, (a + 1) * bw_)
                if own:
                    blocks[mine * per + g * 4 + a, :, 0:bw_] = rs[block, block].astype(BF16)
                    blocks[2 * per + mine * per + g * 4 + a, :, 0:bw_] = is_[block, block].astype(BF16)
                else:
                    rate_sum[mine * per + g * 4 + a] = rs[block, block]
                    inlet_sum[mine * per + g * 4 + a] = is_[block, block]
            for s in range(seqs):
                gm[s, 0:length, cols] += back[s * length : (s + 1) * length]
        pump()

        for s in range(seqs):
            gm[s, length : length + 8, :] = zero
            ext[s, 0:8, :] = edge_ref[16 * s : 16 * s + 16].astype(F32)[8:16]
            ext[s, 8 : 8 + length, :] = branch_ref[s * length : (s + 1) * length].astype(F32)
            head[mine, 8 * s : 8 * s + 8, :] = gm[s, 0:8, :]

        tap = [taps_ref[k : k + 1, :] for k in range(4)]
        acc = (zero,) * 5
        for s in range(seqs):

            def conv(i, acc):
                lo = pl.multiple_of(i * 16, 16)
                y = gm[s, pl.ds(lo, 24), :]
                x = ext[s, pl.ds(lo, 24), :]
                total = tap[0] * y[0:16]
                for k in range(1, 4):
                    total = total + tap[k] * y[k : k + 16]
                gb_ref[0, pl.ds(pl.multiple_of(s * length + i * 16, 16), 16), :] = total.astype(BF16)
                now = y[0:16]
                new = []
                for k in range(4):
                    prod = now * x[8 - k : 24 - k]
                    new.append(acc[k] + prod[0:8] + prod[8:16])
                new.append(acc[4] + now[0:8] + now[8:16])
                return tuple(new)

            acc = lax.fori_loop(0, length // 16, conv, acc)
            y = gm[s, length - 16 : length + 8, :]
            total = tap[0] * y[0:16]
            for k in range(1, 4):
                total = total + tap[k] * y[k : k + 16]
            tail[mine, 16 * s : 16 * s + 16, :] = total
            pump()
        for k in range(4):
            sums_out[k : k + 1, lanes] = down(acc[k])
        sums_out[7:8, lanes] = down(acc[4])

    grp = lambda i: (1 - i) * (1 - core) + i * core
    col = lambda r: pl.BlockSpec((r, width), lambda i: (0, grp(i)))
    blk = pl.BlockSpec((per, bw_, bw_), lambda i: (grp(i), 0, 0))
    pltpu.emit_pipeline(
        body, grid=(2,),
        in_specs=[
            col(rows), col(rows), col(rows), pl.BlockSpec((seqs, 1, width), lambda i: (0, 0, grp(i))),
            col(rows), col(rows), col(rows), col(rows), col(edge.shape[0]), blk, blk, col(4), col(8),
        ],
        out_specs=[pl.BlockSpec((1, rows, width), lambda i: (i, 0, 0))],
    )(lc, q, states, entry, rate, inlet, mixed, branch, edge, wr, wi, taps, vec, gb)


def spaced(exchange, name, steps):
    def begin():
        place = iter(range(64))

        def pump():
            j = next(place)
            for i in range(steps):
                if PLAN.get(f"{name}{i}{j}"):

                    @pl.when(pl.program_id(0) == i)
                    def _():
                        exchange.at(f"{name}{i}{j}")

        return pump

    return begin


def no_pump():
    return lambda: None


ANY = pl.BlockSpec(memory_space=pl.ANY)
INSIDE = pl.BlockSpec(memory_space=pltpu.VMEM)


KINDS = "AFEAFEAFEAFE"
PLAN = {
    "u000": [(-1, 0)],
    "u010": [(-1, 1)],
    "f200": [(0, 0), (0, 1)],
    "u100": [(-1, 2)],
    "u110": [(1, 0), (-1, 3), (1, 1)],
    "u200": [(-1, 4)],
    "d00": [(2, 0), (2, 1)],
    "d40": [(3, 0), (3, 1), (0, 2), (-1, 5)],
    "t00": [(4, 0), (4, 1), (0, 3), (-1, 6)],
    "t01": [(1, 2)],
    "t02": [(5, 0), (5, 1), (0, 4), (-1, 7)],
    "t12": [(2, 2)],
    "b1": [(3, 2), (1, 3), (0, 5), (-1, 8)],
    "b2": [(1, 4)],
    "g01": [(4, 2), (0, 6), (-1, 9)],
    "g02": [(2, 3), (2, 4)],
    "g03": [(5, 2), (0, 7)],
    "g10": [(1, 5)],
    "g11": [(3, 3), (3, 4)],
    "c1": [(-1, 10), (4, 3), (4, 4), (2, 5), (1, 6), (1, 7), (0, 8), (6, 0)],
    "c3": [(5, 3), (5, 4), (6, 1)],
    "c4": [(-1, 11), (3, 5)],
    "i00": [(2, 6), (2, 7), (0, 9)],
    "i10": [(4, 5)],
    "i30": [(5, 5)],
    "o00": [(3, 6), (3, 7), (1, 8), (6, 2)],
    "o10": [(7, 0)],
    "drain": [(4, 6), (4, 7), (0, 10), (7, 1), (5, 6), (5, 7), (6, 3), (2, 8), (0, 11), (1, 9), (7, 2), (3, 8), (6, 4), (6, 5), (4, 8), (1, 10), (7, 3), (6, 6), (2, 9), (5, 8), (6, 7), (1, 11), (7, 4), (3, 9), (6, 8), (2, 10), (4, 9), (5, 9), (2, 11), (3, 10), (6, 9), (3, 11), (4, 10), (6, 10), (5, 10), (4, 11), (5, 11)],
}

PARTS = [256] * 9 + [384] * 3
SWAPS = 10


def backward(own, seqs, length, seq_n, batch_n, grads_in, values, collective_id):
    (
        n2, resid, cot, fgain, ow, gate, state, entry, rate, vec, inlet, mixed, branch, edge, wr, wi, taps, gw, bw, tok, mgain,
        fg, fu, fd, joined, normed,
    ) = values
    rows, model = n2.shape
    lru, units = gate.shape[1], fd.shape[0]
    width, bw_ = lru // 2, wr.shape[-1]
    per, sub = width // bw_, 4 * bw_
    steps = [("batch", 1 << k) for k in range(batch_n.bit_length() - 1)] + [("seq", 1 << k) for k in range(seq_n.bit_length() - 1)]
    n_steps = len(steps)
    parts, unit = 3, units // 6
    if not own:
        grads_in = []

    def kernel(*refs):
        refs = list(refs)
        cut = lambda n: [refs.pop(0) for _ in range(n)]
        far_in = cut(len(grads_in))
        (
            n2, resid, cot, fgain, ow, gate, state, entry, rate, vec, inlet, mixed, branch, edge, wr, wi, taps, gw, bw, tok, mgain,
            fg, fu, fd, joined, normed,
        ) = cut(26)
        tokens_grad, block_out, totals, gres, low_out, low_far, ggate, ggate_far, lc, q, gb, gb_far, hid, hid_far, ups, ups_far, n2_far, joined_far = cut(18)
        fin, block_total = cut(2) if own else (None, None)
        rate_sum, inlet_sum = (None, None) if own else cut(2)
        low, carry, got, cin, dr, di, gr, gi, gm, ext, head, tail, ahead, fixed, gain_sum, acc, small, gn = cut(18)
        send, recv, swap_send, swap_recv, one, local, s_send, s_recv = cut(8)

        core = core_of()
        seq, bat = lax.axis_index("seq"), lax.axis_index("batch")
        other = (seq, bat + 1 - 2 * core)
        peers = [(flip(seq, bit), bat) if axis == "seq" else (seq, flip(bat, bit)) for axis, bit in steps]
        exchange, blocks = None, None
        if own:
            g0, g1, g2, *bufs, x_send, x_recv = cut(9)
            blocks, *block_bufs, b_send, b_recv = cut(8)
            places = [(ref, row) for row in (0, 256, 512) for ref in (g0, g1)] + [(g2, 0), (g2, 256), (g2, 512), (g0, 0), (g0, 384), (g1, 0)]
            chunks = [(ref, row, part, kind) for (ref, row), part, kind in zip(places, PARTS, KINDS)]
            exchange = Exchange(chunks, bufs, fin, x_send, x_recv)
            exchange.further[6] = BlockSums(blocks, block_bufs, block_total, b_send, b_recv).events()
            blocks[...] = jnp.zeros_like(blocks)
        small[0] = jnp.zeros((16, lru), F32)
        greet = [(lax.rem(seq + k, seq_n), bat) for k in range(1, seq_n)] + [peer for peer, step in zip(peers, steps) if step[0] == "batch"]
        meet(greet)

        def swap(j, src, dst):
            return pltpu.make_async_remote_copy(
                src_ref=src, dst_ref=dst, send_sem=swap_send.at[j], recv_sem=swap_recv.at[j], device_id=other, device_id_type=MESH
            )

        at = exchange.at if own else (lambda place: None)
        plan = lambda name, steps: spaced(exchange, name, steps) if own else no_pump
        run_feed = lambda p: feed(core, p, n2, cot, fg, fu, fd, hid, ups, gn, plan(f"f{p}", 2))
        if own:
            cot_far, normed_far = far_in
            n2_swap, joined_swap = swap(4, n2, n2_far), swap(5, joined, joined_far)
            ups_swaps = [swap(6 + p, ups.at[:, 0, p], ups_far.at[:, p]) for p in range(parts)]
            hid_swap = swap(9, hid, hid_far)
            run_up = lambda p: wgrad_up(core, chunks[2 * p], chunks[2 * p + 1], n2, n2_far, ups.at[:, 1, p], ups_far.at[:, p], plan(f"u{p}", 2))
            n2_swap.start()
            run_feed(0)
            ups_swaps[0].start()
            joined_swap.start()
            n2_swap.wait()
            ups_swaps[0].wait()
            run_up(0)
            run_feed(1)
            ups_swaps[1].start()
            run_feed(2)
            ups_swaps[2].start()
            hid_swap.start()
            ups_swaps[1].wait()
            run_up(1)
            ups_swaps[2].wait()
            run_up(2)
            joined_swap.wait()
            hid_swap.wait()
            wgrad_down(core, chunks[6:9], hid, hid_far, cot, cot_far, plan("d", 2 * parts))
        else:
            for p in range(parts):
                run_feed(p)
        norm_back(core, gn, resid, cot, fgain, gres, low, gain_sum)
        at("a4")
        keep = pltpu.make_async_copy(low, low_out, one)
        keep.start()
        low_swap = swap(0, low, low_far)
        low_swap.start()
        turn(
            core, seqs, length, low, ow, gate, state, rate, vec, ggate, lc, q, carry, gm,
            plan("t", 2),
        )
        gate_swap = swap(1, ggate.at[0], ggate_far)
        gate_swap.start()
        arriving = Entry(carry, got, seq_n, send, recv)
        arriving.start()
        keep.wait()
        low_swap.wait()
        if own:
            at("b0")
            exchange.free(0)
            exchange.free(2)
            wgrad(core, chunks[9:10], joined, joined_far, low_out, low_far, False)
            at("b1")
        arriving.finish(cin, True)
        gate_swap.wait()
        at("b2")
        gates_back(
            own, core, seqs, length, lc, q, cin, state, entry, rate, inlet, mixed, branch, edge, wr, wi, taps, vec,
            gb, head, tail, blocks, rate_sum, inlet_sum, small.at[0], dr, di, gr, gi, gm, ext,
            plan("g", 2),
        )

        to_left = pltpu.make_async_remote_copy(
            src_ref=head, dst_ref=ahead, send_sem=swap_send.at[2], recv_sem=swap_recv.at[2],
            device_id=(lax.rem(seq + seq_n - 1, seq_n), bat), device_id_type=MESH,
        )
        to_left.start()
        if own:
            at("c0")
            exchange.free(4)
            wgrad(core, chunks[10:11], normed, normed_far, ggate.at[1], ggate_far, True)
            at("c1")
        to_left.wait()
        weight = (seq < seq_n - 1).astype(F32)
        copies = []
        for i in range(2):
            mine = (1 - i) * (1 - core) + i * core
            for s in range(seqs):
                y = ahead[mine, 8 * s : 8 * s + 8, :] * weight
                t = tail[mine, 16 * s : 16 * s + 16, :]
                grown = jnp.concatenate([jnp.zeros((16, width), F32), y], axis=0)
                for k in range(1, 4):
                    t = t + taps[k : k + 1, pl.ds(pl.multiple_of(mine * width, 128), width)] * grown[k : k + 16]
                fixed[i, 16 * s : 16 * s + 16, :] = t.astype(BF16)
                copy = pltpu.make_async_copy(
                    fixed.at[i, 16 * s : 16 * s + 16], gb.at[i, (s + 1) * length - 16 : (s + 1) * length], local.at[i, s]
                )
                copy.start()
                copies.append(copy)
        for copy in copies:
            copy.wait()
        branch_swap = swap(3, gb.at[0], gb_far)
        branch_swap.start()
        at("c2")
        branch_swap.wait()
        at("c3")
        if own:
            exchange.free(1)
            exchange.free(3)
            wgrad(core, chunks[11:12], normed, normed_far, gb.at[1], gb_far, True)
            at("c4")

        begin = plan("i", 4)
        tile = 128
        acc[...] = jnp.zeros_like(acc)

        def input_grad(gg_ref, gb_ref, gwt, gwm, bwt, bwm, x_ref, gr_ref, out):
            pump = begin()
            d = nt(gg_ref[0], gwt[...]) + nt(gg_ref[1], gwm[...]) + nt(gb_ref[0], bwt[...]) + nt(gb_ref[1], bwm[...])
            x = x_ref[...].astype(F32)
            r = lax.rsqrt(jnp.mean(x * x, axis=-1, keepdims=True) + 1e-06)
            xr, dg = x * r, d * mgain[...]
            out[...] = gr_ref[...] + r * (dg - xr * jnp.mean(dg * xr, axis=-1, keepdims=True))
            acc[...] += jnp.sum(d * xr, axis=0, keepdims=True)
            pump()

        row = pl.BlockSpec((tile, model), lambda i: (i, 0))
        pair = pl.BlockSpec((2, tile, width), lambda i: (0, i, 0))
        side = lambda c: pl.BlockSpec((model, width), lambda i: (0, c), pipeline_mode=pl.Buffered(1))
        pltpu.emit_pipeline(
            input_grad, grid=(rows // tile,), in_specs=[pair, pair, side(1 - core), side(core), side(1 - core), side(core), row, row], out_specs=[row]
        )(ggate, gb, gw, gw, bw, bw, tok, gres, tokens_grad)

        small[0, 8:9, 0:model] = acc[...]
        small[0, 9:10, 0:model] = gain_sum[...]

        def small_step(k):
            return pltpu.make_async_remote_copy(
                src_ref=small.at[0], dst_ref=small.at[k + 1], send_sem=s_send.at[k], recv_sem=s_recv.at[k],
                device_id=peers[k], device_id_type=MESH,
            )

        def small_event(k):
            small_step(k).wait()
            small[0] = small[0] + small[k + 1]
            if k + 1 < n_steps:
                small_step(k + 1).start()

        small_events = [functools.partial(small_event, k) for k in range(n_steps)]
        small_step(0).start()
        if own:
            exchange.further[7] = small_events
        begin_out = plan("o", 4)
        tile_out = 256

        def last(r, *rest):
            pump = begin_out()
            hid_refs, down_refs, out = rest[: 2 * parts], rest[2 * parts : 4 * parts], rest[-1]
            total = r[...]
            for l, w in zip(hid_refs, down_refs):
                total = total + nn(l[0, 0], w[...])
            out[...] = total.astype(BF16)
            pump()

        col = pl.BlockSpec((rows, tile_out), lambda i: (0, i))
        order = [(side, p) for side in range(2) for p in range(parts)]
        hid_spec = lambda side, p: pl.BlockSpec((1, 1, rows, unit), lambda i: (side, p, 0, 0), pipeline_mode=pl.Buffered(1))
        down_spec = lambda half, p: pl.BlockSpec((unit, tile_out), lambda i: (half * parts + p, i))
        pltpu.emit_pipeline(
            last, grid=(model // tile_out,),
            in_specs=[col] + [hid_spec(*o) for o in order] + [down_spec(core if side else 1 - core, p) for side, p in order], out_specs=[col],
        )(resid, *([hid] * 2 * parts), *([fd] * 2 * parts), block_out)
        if own:
            exchange.drain()
        else:
            for event in small_events:
                event()
        totals[...] = small[0]

    f = lambda *shape: jax.ShapeDtypeStruct(shape, F32)
    b = lambda *shape: jax.ShapeDtypeStruct(shape, BF16)
    vm, dma = pltpu.VMEM, lambda *shape: pltpu.SemaphoreType.DMA(shape)
    out_shape = [
        f(rows, model), b(rows, model), f(16, lru),
        f(rows, model), b(rows, model), b(rows, model), b(2, rows, width), b(rows, width), f(rows, lru), f(rows, lru), b(2, rows, width), b(rows, width),
        b(2, parts, rows, unit), b(2, parts, rows, unit), b(2, 2, parts, rows, unit), b(2, parts, rows, unit), b(rows, model), b(rows, lru),
    ]
    out_specs = [ANY, ANY, INSIDE] + [ANY] * 15
    scratch = [
        vm((rows, model), BF16), vm((2, 2, seqs, width), F32), vm((seq_n, 2, 2, seqs, width), F32), vm((2, seqs, width), F32),
        vm((sub, sub), BF16), vm((sub, sub), BF16), vm((rows, width), BF16), vm((rows, width), BF16),
        vm((seqs, length + 8, width), F32), vm((seqs, length + 8, width), F32), vm((2, 8 * seqs, width), F32), vm((2, 16 * seqs, width), F32),
        vm((2, 8 * seqs, width), F32), vm((2, 16 * seqs, width), BF16), vm((1, model), F32), vm((1, model), F32), vm((n_steps + 1, 16, lru), F32), vm((rows, model), F32),
        dma(seq_n), dma(seq_n), dma(SWAPS), dma(SWAPS), pltpu.SemaphoreType.DMA, dma(2, seqs), dma(n_steps), dma(n_steps),
    ]
    if own:
        out_shape += [b(2, 2, sum(PARTS), 128), b(4 * per, bw_, 128)]
        out_specs += [INSIDE, INSIDE]
        scratch += [vm((16, 768, 128), BF16)] * 3 + Exchange.scratch(len(PARTS), sum(PARTS))
        scratch += [vm((4 * per, bw_, 128), BF16)] + BlockSums.scratch(bw_)
    else:
        out_shape += [f(*wr.shape), f(*wi.shape)]
        out_specs += [INSIDE, INSIDE]
    ins = [ANY] * (len(grads_in) + len(values))
    for j in (3, 16, 20):
        ins[len(grads_in) + j] = INSIDE
    return pl.pallas_call(
        kernel,
        in_specs=ins,
        out_specs=out_specs,
        out_shape=out_shape,
        scratch_shapes=scratch,
        compiler_params=pltpu.CompilerParams(collective_id=collective_id, has_side_effects=True, vmem_limit_bytes=60 * 2**20),
        name="backward",
    )(*grads_in, *values)


def lay(sums, totals, blocks, model, lru, units, n):
    shapes = [(model // n, units), (model // n, units), (units // n, model), (lru // n, model), (model // n, lru), (model // n, lru)]
    rows = sums.shape[2]
    count, wide_b = blocks.shape[0] // 2, blocks.shape[1]

    def kernel(v, b, rate, inlet, *outs):
        for y in range(2):
            for m, out in enumerate(outs):
                part, wide = out.shape
                for t in range(wide // 256):
                    if m < 2:
                        at, col = t // 2 * 512 + m * 256 + t % 2 * 128, t // 2 * 512 + y * 256 + t % 2 * 128
                    else:
                        at, col = 1536 + [0, 768, 1152, 1536][m - 2] + t * part, y * wide // 2 + t * 128
                    out[:, col : col + 128] = v[0, y, at : at + part, :].astype(F32)
        for j in range(count // 2):
            rate[j] = b[0, j, :, 0:wide_b].astype(F32)
            inlet[j] = b[1, j, :, 0:wide_b].astype(F32)

    block = pl.BlockSpec((count // 2, wide_b, wide_b), lambda i: (i, 0, 0))
    rate, inlet, *grads = pl.pallas_call(
        kernel,
        grid=(2,),
        in_specs=[pl.BlockSpec((1, 2, rows, 128), lambda i: (i, 0, 0, 0)), pl.BlockSpec((2, count // 2, wide_b, 128), lambda i: (0, i, 0, 0))],
        out_specs=[block, block] + [pl.BlockSpec((part, wide // 2), lambda i: (0, i)) for part, wide in shapes],
        out_shape=[jax.ShapeDtypeStruct((count, wide_b, wide_b), F32)] * 2 + [jax.ShapeDtypeStruct(shape, F32) for shape in shapes],
        compiler_params=params(),
        name="lay",
    )(sums, blocks.reshape(2, count, wide_b, 128))
    return rate, inlet, grads


def swap(value):
    count = lax.axis_size("batch")
    return lax.ppermute(value, "batch", [(i, i ^ 1) for i in range(count)])


def local(
    tokens, cotangent, gate_weight, branch_weight, out_weight, conv_taps, conv_offset, rate_weight, inlet_weight,
    rate_offset, inlet_offset, decay_param, mixer_gain, feed_gain, feed_gate, feed_up, feed_down,
):
    seqs, length, model = tokens.shape
    lru, units = gate_weight.shape[1], feed_gate.shape[1]
    rows = seqs * length
    seq_n, batch_n = lax.axis_size("seq"), lax.axis_size("batch")
    core = lax.rem(lax.axis_index("batch"), 2)

    tok, cot = tokens.reshape(rows, model), cotangent.reshape(rows, model)
    cot_far = swap(cot)
    none = jnp.zeros_like(conv_offset)
    vec = jnp.stack(
        [conv_offset, rate_offset, inlet_offset, jax.nn.softplus(decay_param), jax.nn.sigmoid(decay_param), none, none, none]
    )
    gain1, gain2 = mixer_gain[None], feed_gain[None]

    normed, gate, branch, edge, mixed, rate, inlet, h, p, entry = front(
        tok, gain1, gate_weight, branch_weight, conv_taps, vec, rate_weight, inlet_weight, seqs, length, seq_n, 0
    )
    normed_far = swap(normed)
    joined, resid, normed_two, state = join(tok, gate, h, p, entry, out_weight, gain2, seqs, length)

    own = (seq_n, batch_n) == (8, 4)
    tokens_grad, out, totals, _, grad_low, _, ggate, _, _, _, gb, _, hid, _, ups, _, _, _, *sums = backward(
        own, seqs, length, seq_n, batch_n, [cot_far, normed_far],
        [
            normed_two, resid, cot, gain2, out_weight, gate, state, entry, rate, vec, inlet, mixed, branch, edge,
            rate_weight, inlet_weight, conv_taps, gate_weight, branch_weight, tok, gain1, feed_gate, feed_up, feed_down, joined, normed,
        ],
        1,
    )
    if own:
        rate_all, inlet_all, grads = lay(sums[0], totals, sums[1], model, lru, units, seq_n)
        gate_feed_all, up_feed_all, down_all, out_all, gate_all, branch_all = grads
    else:
        rate_all, inlet_all = lax.psum((sums[0], sums[1]), ("seq", "batch"))

        def full(pair):
            pair = pair if pair.ndim == 4 else pair[:, None]
            pair = jnp.where(core == 0, pair[::-1], pair)
            return pair.transpose(2, 0, 1, 3).reshape(rows, -1)

        def total(left, right):
            return lax.psum(lax.psum_scatter(tn(left, right), "seq", scatter_dimension=0, tiled=True), "batch")

        down_all = total(full(hid), cot)
        gate_feed_all, up_feed_all = total(normed_two, full(ups[0])), total(normed_two, full(ups[1]))
        out_all = total(joined, grad_low)
        gate_all, branch_all = total(normed, full(ggate)), total(normed, full(gb))

    return (
        out.reshape(seqs, length, model), tokens_grad.reshape(seqs, length, model), gate_all, branch_all, out_all,
        totals[0:4], totals[7], rate_all, inlet_all, totals[5], totals[6], totals[4], totals[8, :model], totals[9, :model],
        gate_feed_all, up_feed_all, down_all,
    )


def solution(mesh):
    big = P("batch", "seq", None)
    in_specs = (big, big) + (P(),) * 15
    out_specs = (big, big) + (P("seq", None),) * 3 + (P(),) * 9 + (P("seq", None),) * 3
    return jax.shard_map(local, mesh=mesh, in_specs=in_specs, out_specs=out_specs, check_vma=False)
```

```python
import functools
import jax
import jax.numpy as jnp
from jax import lax
from jax.experimental import pallas as pl
from jax.experimental.pallas import tpu as pltpu
from jax.sharding import PartitionSpec as P

F32, BF16 = jnp.float32, jnp.bfloat16
VLIM = 56 * 2**20
GELU_A, GELU_B = 0.7978845608028654, 0.044715


def nn(a, b):
    return lax.dot_general(a, b, (((1,), (0,)), ((), ())), preferred_element_type=F32)


def nt(a, b):
    return lax.dot_general(a, b, (((1,), (1,)), ((), ())), preferred_element_type=F32)


def tn(a, b):
    return lax.dot_general(a, b, (((0,), (0,)), ((), ())), preferred_element_type=F32)


def sigmoid(v):
    return 1.0 / (1.0 + jnp.exp(-v))


def drop(u, decay):
    v = 2.0 * u
    series = 1.0 + v * (1.0 / 7.0)
    for k in (6.0, 5.0, 4.0, 3.0, 2.0):
        series = 1.0 + (v * (1.0 / k)) * series
    return jnp.where(v > -0.35, -v * series, 1.0 - decay * decay)


def gelu_parts(v):
    square = v * v
    inner = jnp.tanh(GELU_A * v * (1.0 + GELU_B * square))
    half = 0.5 + 0.5 * inner
    act = v * half
    slope = half + 0.5 * v * (1.0 - inner * inner) * (GELU_A + 3.0 * GELU_A * GELU_B * square)
    return act, slope


def gelu(v):
    inner = jnp.tanh(GELU_A * v * (1.0 + GELU_B * (v * v)))
    return v * (0.5 + 0.5 * inner)


def spread(dense, blocks, count, width):
    for a in range(count):
        parts = []
        if a > 0:
            parts.append(jnp.zeros((width, a * width), dense.dtype))
        parts.append(blocks[a])
        if a < count - 1:
            parts.append(jnp.zeros((width, (count - 1 - a) * width), dense.dtype))
        dense[a * width : (a + 1) * width, :] = jnp.concatenate(parts, axis=1)


def params(sem=("arbitrary",), **kw):
    return pltpu.CompilerParams(dimension_semantics=sem, vmem_limit_bytes=VLIM, **kw)


def whole(shape):
    return pl.BlockSpec(shape, lambda *_: (0,) * len(shape))


MESH = pl.DeviceIdType.MESH


def meet(peers):
    barrier = pltpu.get_barrier_semaphore()
    for peer in peers:
        pl.semaphore_signal(barrier, inc=1, device_id=peer, device_id_type=MESH)
    pl.semaphore_wait(barrier, len(peers))


def flip(index, bit):
    return index + bit - 2 * bit * (lax.rem(index // bit, 2))


class Entry:
    def __init__(self, part, got, n, send, recv):
        self.part, self.got, self.n = part, got, n
        self.me = lax.axis_index("seq")
        self.copies = [
            pltpu.make_async_remote_copy(
                src_ref=part, dst_ref=got.at[self.me], send_sem=send.at[k], recv_sem=recv.at[k],
                device_id=(lax.rem(self.me + k, n), lax.axis_index("batch")), device_id_type=MESH,
            )
            for k in range(1, n)
        ]

    def start(self):
        for copy in self.copies:
            copy.start()
        self.got[self.me] = self.part[...]

    def finish(self, out, reverse):
        for copy in self.copies:
            copy.wait()

        def one(k, state):
            j = self.n - 1 - k if reverse else k
            before = (j > self.me) if reverse else (j < self.me)
            return jnp.where(before, self.got[j, :, 0] * state + self.got[j, :, 1], state)

        out[...] = lax.fori_loop(0, self.n, one, jnp.zeros(out.shape, F32))


def front_kernel(
    seqs, length, seq_n, tok, gain, gw, bw, taps, vec, wr, wi,
    normed, gate, branch, edge, mixed, rate, inlet, h, p, entry,
    halo, hn, ext, dr, di, rp, ip, carry, got, state, h_send, h_recv, send, recv,
):
    rows, width = seqs * length, gw.shape[1]
    sub = dr.shape[-1]

    seq, bat = lax.axis_index("seq"), lax.axis_index("batch")

    @pl.when(pl.program_id(0) == 0)
    def _():
        meet([(lax.rem(seq + k, seq_n), bat) for k in range(1, seq_n)])
        copies = [
            pltpu.make_async_remote_copy(
                src_ref=tok.at[(s + 1) * length - 16 : (s + 1) * length], dst_ref=halo.at[s], send_sem=h_send.at[s], recv_sem=h_recv.at[s],
                device_id=(lax.rem(seq + 1, seq_n), bat), device_id_type=MESH,
            )
            for s in range(seqs)
        ]
        for copy in copies:
            copy.start()

        def norm(i, _):
            x = tok[pl.ds(i * 32, 32), :].astype(F32)
            r = lax.rsqrt(jnp.mean(x * x, axis=-1, keepdims=True) + 1e-06)
            normed[pl.ds(i * 32, 32), :] = (x * r * gain[...]).astype(BF16)
            return 0

        lax.fori_loop(0, rows // 32, norm, 0)
        for s in range(seqs):
            copies[s].wait()
            x = halo[s].astype(F32)
            r = lax.rsqrt(jnp.mean(x * x, axis=-1, keepdims=True) + 1e-06)
            hn[16 * s : 16 * s + 16, :] = (x * r * gain[...]).astype(BF16)

    gate[...] = nn(normed[...], gw[...])
    b16 = nn(normed[...], bw[...]).astype(BF16)
    e16 = (nn(hn[...], bw[...]) * (seq > 0).astype(F32)).astype(BF16)
    branch[...] = b16
    edge[...] = e16
    e32 = e16.astype(F32)
    for s in range(seqs):
        ext[s, 0:8, :] = e32[16 * s + 8 : 16 * s + 16]
        ext[s, 8 : 8 + length, :] = b16[length * s : length * (s + 1)].astype(F32)

    tap = [taps[k : k + 1, :] for k in range(4)]
    off = vec[0:1, :]
    for s in range(seqs):

        def conv(i, _):
            x = ext[s, pl.ds(pl.multiple_of(i * 16, 16), 24), :]
            total = off + tap[0] * x[8:24]
            for k in range(1, 4):
                total = total + tap[k] * x[8 - k : 24 - k]
            mixed[pl.ds(pl.multiple_of(s * length + i * 16, 16), 16), :] = total.astype(BF16)
            return 0

        lax.fori_loop(0, length // 16, conv, 0)

    for g in range(width // sub):
        cols = slice(g * sub, (g + 1) * sub)
        spread(dr.at[g], [wr[g * 4 + a] for a in range(4)], 4, wr.shape[-1])
        spread(di.at[g], [wi[g * 4 + a] for a in range(4)], 4, wi.shape[-1])
        rp[:, cols] = nn(mixed[:, cols], dr[g])
        ip[:, cols] = nn(mixed[:, cols], di[g])

    ro, io, slope = vec[1:2, :], vec[2:3, :], -8.0 * vec[3:4, :]

    def gates(i, _):
        at = pl.ds(pl.multiple_of(i * 16, 16), 16)
        rt = sigmoid(rp[at, :] + ro)
        it = sigmoid(ip[at, :] + io)
        log_decay = rt * slope
        decay = jnp.exp(log_decay)
        rate[at, :] = rt
        inlet[at, :] = it
        p[at, :] = decay
        h[at, :] = jnp.sqrt(drop(log_decay, decay)) * it * mixed[at, :].astype(F32)
        return 0

    lax.fori_loop(0, rows // 16, gates, 0)

    row = lax.broadcasted_iota(jnp.int32, (8, width), 0)

    def scan(i, last):
        out = []
        for s in range(seqs):
            at = pl.ds(pl.multiple_of(s * length + i * 8, 8), 8)
            a, b = p[at, :], h[at, :]
            for d in (1, 2, 4):
                keep = row >= d
                b = b + a * jnp.where(keep, pltpu.roll(b, d, 0), 0.0)
                a = a * jnp.where(keep, pltpu.roll(a, d, 0), 1.0)
            ap, bp = last[s]
            b = b + a * bp
            a = a * ap
            p[at, :] = a
            h[at, :] = b
            out.append((a[7:8], b[7:8]))
        return tuple(out)

    init = tuple((jnp.ones((1, width), F32), jnp.zeros((1, width), F32)) for _ in range(seqs))
    last = lax.fori_loop(0, length // 8, scan, init)
    for s in range(seqs):
        carry[pl.program_id(0), 0, s : s + 1, :] = last[s][0]
        carry[pl.program_id(0), 1, s : s + 1, :] = last[s][1]

    @pl.when(pl.program_id(0) == 1)
    def _():
        arriving = Entry(carry, got, seq_n, send, recv)
        arriving.start()
        arriving.finish(state, False)
        for g in range(2):
            for s in range(seqs):
                entry[s, :, g * width : (g + 1) * width] = state[g, s : s + 1, :]


def front(tok, gain, gw, bw, taps, vec, wr, wi, seqs, length, seq_n, collective_id):
    rows, model = tok.shape
    lru, bw_ = gw.shape[1], wr.shape[-1]
    width, sub, per = lru // 2, 4 * bw_, lru // 2 // bw_
    col = lambda r: pl.BlockSpec((r, width), lambda j: (0, j))
    blk = pl.BlockSpec((per, bw_, bw_), lambda j: (j, 0, 0))
    f = lambda dt: jax.ShapeDtypeStruct((rows, lru), dt)
    vm, dma = pltpu.VMEM, lambda n: pltpu.SemaphoreType.DMA((n,))
    return pl.pallas_call(
        functools.partial(front_kernel, seqs, length, seq_n),
        grid=(2,),
        in_specs=[
            whole((rows, model)), whole((1, model)),
            pl.BlockSpec((model, width), lambda j: (0, j)), pl.BlockSpec((model, width), lambda j: (0, j)), col(4), col(8), blk, blk,
        ],
        out_specs=[
            whole((rows, model)), col(rows), col(rows), col(16 * seqs), col(rows), col(rows), col(rows), col(rows), col(rows),
            whole((seqs, 1, lru)),
        ],
        out_shape=[
            jax.ShapeDtypeStruct((rows, model), BF16), f(F32), f(BF16),
            jax.ShapeDtypeStruct((16 * seqs, lru), BF16), f(BF16), f(F32), f(F32), f(F32), f(F32),
            jax.ShapeDtypeStruct((seqs, 1, lru), F32),
        ],
        scratch_shapes=[
            vm((seqs, 16, model), BF16), vm((16 * seqs, model), BF16), vm((seqs, 8 + length, width), F32),
            vm((2, sub, sub), BF16), vm((2, sub, sub), BF16), vm((rows, width), F32), vm((rows, width), F32),
            vm((2, 2, seqs, width), F32), vm((seq_n, 2, 2, seqs, width), F32), vm((2, seqs, width), F32),
            dma(seqs), dma(seqs), dma(seq_n), dma(seq_n),
        ],
        compiler_params=params(collective_id=collective_id, has_side_effects=True),
        name="front",
    )(tok, gain, gw, bw, taps, vec, wr, wi)


def join_kernel(tok, gate, h, p, entry, ow, gain, joined, resid, normed, state_ref):
    rows = tok.shape[0]
    ent = entry[0]

    def join(i, _):
        at = pl.ds(pl.multiple_of(i * 16, 16), 16)
        state = h[at, :] + p[at, :] * ent
        state_ref[at, :] = state
        joined[at, :] = (gelu(gate[at, :]) * state).astype(BF16)
        return 0

    lax.fori_loop(0, rows // 16, join, 0)
    resid[...] = nn(joined[...], ow[...])

    def norm(i, _):
        at = pl.ds(pl.multiple_of(i * 32, 32), 32)
        y = tok[at, :].astype(F32) + resid[at, :]
        resid[at, :] = y
        r = lax.rsqrt(jnp.mean(y * y, axis=-1, keepdims=True) + 1e-06)
        normed[at, :] = (y * r * gain[...]).astype(BF16)
        return 0

    lax.fori_loop(0, rows // 32, norm, 0)


def join(tok, gate, h, p, entry, ow, gain, seqs, length):
    rows, model = tok.shape
    lru = gate.shape[1]
    tile = 128
    per = length // tile
    row = lambda w: pl.BlockSpec((tile, w), lambda i: (i, 0))
    return pl.pallas_call(
        join_kernel,
        grid=(rows // tile,),
        in_specs=[row(model), row(lru), row(lru), row(lru), pl.BlockSpec((1, 1, lru), lambda i: (i // per, 0, 0)), whole((lru, model)), whole((1, model))],
        out_specs=[row(lru), row(model), row(model), row(lru)],
        out_shape=[jax.ShapeDtypeStruct((rows, lru), BF16), jax.ShapeDtypeStruct((rows, model), F32), jax.ShapeDtypeStruct((rows, model), BF16), jax.ShapeDtypeStruct((rows, lru), F32)],
        compiler_params=params(),
        name="join",
    )(tok, gate, h, p, entry, ow, gain)


ORDERS = {"A": ("xhyl", "yxhl"), "E": ("xlhy", "yxlh"), "F": ("xylh", "yxlh")}


class Exchange:
    def __init__(self, chunks, bufs, fin, send, recv):
        self.chunks, self.bufs, self.fin, self.sems = chunks, bufs, fin, (send, recv)
        self.first = [sum(c[2] for c in chunks[:q]) for q in range(len(chunks))]
        seq, bat = lax.axis_index("seq"), lax.axis_index("batch")
        core, y = lax.rem(bat, 2), bat // 2
        x, low, high = lax.rem(seq, 2), lax.rem(seq // 2, 2), seq // 4
        bit = {"x": x, "y": y, "l": low, "h": high}
        move = {"x": (1 - 2 * x, 0), "y": (0, 2 - 4 * y), "l": (2 - 4 * low, 0), "h": (4 - 8 * high, 0)}
        pick = lambda a, b: a if a is b else (1 - core) * a + core * b
        self.core, self.y = core, y
        self.other, self.across = (seq, bat + 1 - 2 * core), (seq, bat + 2 - 4 * y)
        self.bits, self.peers = {}, {}
        for kind, (first, second) in ORDERS.items():
            self.bits[kind] = [pick(bit[a], bit[b]) for a, b in zip(first, second)]
            self.peers[kind] = [
                (seq + pick(move[a][0], move[b][0]), bat + pick(move[a][1], move[b][1])) for a, b in zip(first, second)
            ] + [self.across, self.other]
        self.greet = [(seq + move[a][0], bat) for a in "xlh"] + [self.across, self.other]
        self.freed, self.further = set(), {}

    def at(self, place):
        for k, q in PLAN.get(place, ()):
            self.step(k, q)

    def free(self, q):
        self.copy(0, q).wait_send()
        self.freed.add(q)

    def drain(self):
        self.at("drain")
        for q in range(len(self.chunks)):
            for k in range(4):
                if k > 0 or q not in self.freed:
                    self.copy(k, q).wait_send()

    def copy(self, k, q):
        grad, row, part, kind = self.chunks[q]
        size, bits = 8 >> k, self.bits[kind]
        at = slice(self.first[q], self.first[q] + part)
        if k == 0:
            src, dst = grad.at[pl.ds((1 - bits[0]) * 8, 8), row : row + part], self.bufs[0].at[:, at]
        elif k < 4:
            src, dst = self.bufs[k - 1].at[pl.ds((1 - bits[k]) * size, size), at], self.bufs[k].at[:, at]
        elif k == 4:
            src = dst = self.fin.at[self.core, self.y, at]
        else:
            src = dst = self.fin.at[self.core, :, at]
        return pltpu.make_async_remote_copy(
            src_ref=src, dst_ref=dst, send_sem=self.sems[0].at[k, q], recv_sem=self.sems[1].at[k, q],
            device_id=self.peers[kind][k], device_id_type=MESH,
        )

    def add(self, k, q, base, size):
        grad, row, part, kind = self.chunks[q]
        dst, bits = self.bufs[k], self.bits[kind]
        for j in range(size):

            def body(i, _):
                a = pl.ds(pl.multiple_of(self.first[q] + i * 128, 128), 128)
                if k == 0:
                    own = grad[bits[0] * 8 + base + j, pl.ds(pl.multiple_of(row + i * 128, 128), 128), :]
                else:
                    own = self.bufs[k - 1][bits[k] * (8 >> k) + base + j, a, :]
                dst[base + j, a, :] = dst[base + j, a, :] + own
                return 0

            lax.fori_loop(0, part // 128, body, 0)

    def step(self, k, q):
        if k > 5:
            self.further[k][q]()
        elif k < 0:
            self.copy(0, q).start()
        elif k < 3:
            half, bits = 4 >> k, self.bits[self.chunks[q][3]]
            self.copy(k, q).wait_recv()
            self.add(k, q, (1 - bits[k + 1]) * half, half)
            self.copy(k + 1, q).start()
            self.add(k, q, bits[k + 1] * half, half)
        elif k == 3:
            bits = self.bits[self.chunks[q][3]]
            self.copy(3, q).wait_recv()

            def body(i, _):
                a = pl.ds(pl.multiple_of(self.first[q] + i * 128, 128), 128)
                self.fin[self.core, self.y, a, :] = self.bufs[3][0, a, :] + self.bufs[2][bits[3], a, :]
                return 0

            lax.fori_loop(0, self.chunks[q][2] // 128, body, 0)
            self.copy(4, q).start()
        elif k == 4:
            self.copy(4, q).wait()
            self.copy(5, q).start()
        else:
            self.copy(5, q).wait()

    @staticmethod
    def scratch(chunks, rows):
        return [pltpu.VMEM((8 >> k, rows, 128), BF16) for k in range(4)] + [pltpu.SemaphoreType.DMA((6, chunks))] * 2


class BlockSums:
    def __init__(self, value, bufs, out, send, recv):
        self.value, self.bufs, self.out, self.sems = value, bufs, out, (send, recv)
        seq, bat = lax.axis_index("seq"), lax.axis_index("batch")
        core, y = lax.rem(bat, 2), bat // 2
        x, low, high = lax.rem(seq, 2), lax.rem(seq // 2, 2), seq // 4
        self.bits = [core, low, high, x, y]
        self.peers = [(seq, bat + 1 - 2 * core), (seq + 2 - 4 * low, bat), (seq + 4 - 8 * high, bat), (seq + 1 - 2 * x, bat), (seq, bat + 2 - 4 * y)]
        self.base = [0]
        for k in range(5):
            self.base.append(self.base[-1] + self.bits[k] * (16 >> k))

    def halve(self, k):
        size = 16 >> k
        return pltpu.make_async_remote_copy(
            src_ref=self.value.at[pl.ds(self.base[k] + (1 - self.bits[k]) * size, size)], dst_ref=self.bufs[k],
            send_sem=self.sems[0].at[k], recv_sem=self.sems[1].at[k], device_id=self.peers[k], device_id_type=MESH,
        )

    def hand(self, k):
        at = pl.ds(self.base[k + 1], 16 >> k)
        return pltpu.make_async_remote_copy(
            src_ref=self.out.at[at], dst_ref=self.out.at[at],
            send_sem=self.sems[0].at[5 + k], recv_sem=self.sems[1].at[5 + k], device_id=self.peers[k], device_id_type=MESH,
        )

    def events(self):
        def took(k):
            size = 16 >> k
            self.halve(k).wait()

            def body(j, _):
                at = self.base[k + 1] + j
                total = (self.value[at].astype(F32) + self.bufs[k][j].astype(F32)).astype(BF16)
                if k < 4:
                    self.value[at] = total
                else:
                    self.out[at] = total
                return 0

            lax.fori_loop(0, size, body, 0)
            if k < 4:
                self.halve(k + 1).start()
            else:
                self.hand(4).start()

        def got(k):
            self.hand(k).wait()
            if k > 0:
                self.hand(k - 1).start()

        first = [lambda: self.halve(0).start()]
        return first + [functools.partial(took, k) for k in range(5)] + [functools.partial(got, k) for k in range(4, -1, -1)]

    @staticmethod
    def scratch(width):
        return [pltpu.VMEM((16 >> k, width, 128), BF16) for k in range(5)] + [pltpu.SemaphoreType.DMA((10,))] * 2


def core_of():
    return lax.rem(lax.axis_index("batch"), 2)


def group(core):
    i = pl.program_id(0)
    return (1 - i) * (1 - core) + i * core


def put_pieces(chunks, row, acc, core, y, s):
    part, cols = acc.shape
    for t in range(cols // 128):
        at = row[t] if isinstance(row, (list, tuple)) else row + t * part
        base = 0
        for ref, first, rows, kind in chunks:
            low, high = max(at, base), min(at + part, base + rows)
            if low < high:
                ref[place_of(core, s, y, kind), first + low - base : first + high - base, :] = acc[
                    low - at : high - at, t * 128 : (t + 1) * 128
                ].astype(BF16)
            base += rows


def place_of(core, s, y, kind):
    bit = {"x": s % 2, "l": (s // 2) % 2, "h": s // 4, "y": y}
    place = lambda order: sum(bit[a] * (8 >> k) for k, a in enumerate(order))
    first, second = ORDERS[kind]
    return place(first) if first == second else (1 - core) * place(first) + core * place(second)


def wgrad(core, chunks, lhs, lhs_far, rhs, rhs_far, own_columns):
    rows, deep = lhs.shape
    tile = rhs.shape[1] // (2 if own_columns else 4)
    base, part = 0 if own_columns else 2 * core, deep // 8

    def body(a, b, c, d):
        acc = tn(a[...], c[...]) + tn(b[...], d[...])
        for s in range(8):
            put_pieces(chunks, 0, acc[s * part : (s + 1) * part], core, pl.program_id(0), s)

    left = pl.BlockSpec(lhs.shape, lambda y: (0, 0), pipeline_mode=pl.Buffered(1))
    right = pl.BlockSpec((rows, tile), lambda y: (0, base + y))
    pltpu.emit_pipeline(body, grid=(2,), in_specs=[left, left, right, right])(lhs, lhs_far, rhs, rhs_far)


def wgrad_up(core, gate_chunk, up_chunk, lhs, lhs_far, rhs, rhs_far, begin):
    rows, deep = lhs.shape
    tile, part = rhs.shape[2], deep // 8

    def body(a, b, c, d):
        pump = begin()
        acc = tn(a[...], c[0]) + tn(b[...], d[0])
        for j, chunk in enumerate((gate_chunk, up_chunk)):

            @pl.when(pl.program_id(0) == j)
            def _():
                for s in range(8):
                    for y in range(2):
                        put_pieces([chunk], 0, acc[s * part : (s + 1) * part, y * tile // 2 : (y + 1) * tile // 2], core, y, s)

        pump()

    left = pl.BlockSpec(lhs.shape, lambda i: (0, 0), pipeline_mode=pl.Buffered(1))
    right = pl.BlockSpec((1, rows, tile), lambda i: (i, 0, 0))
    pltpu.emit_pipeline(body, grid=(2,), in_specs=[left, left, right, right])(lhs, lhs_far, rhs, rhs_far)


def wgrad_down(core, chunks, hid, hid_far, cot, cot_far, begin):
    _, parts, rows, units = hid.shape
    half_cols = cot.shape[1] // 2
    block = 2 * parts * units // 8

    def body(l, m, c, d):
        pump = begin()
        i = pl.program_id(0)
        acc = tn(l[0, 0], c[...]) + tn(m[0, 0], d[...])
        for side in range(2):
            for p in range(parts):

                @pl.when(i == side * parts + p)
                def _():
                    half = core if side else 1 - core
                    for j in range(units // 128):
                        unit = p * units + j * 128
                        s = 4 * half + unit // block
                        row = unit % block
                        for y in range(2):
                            cut = acc[j * 128 : (j + 1) * 128, y * half_cols // 2 : (y + 1) * half_cols // 2]
                            put_pieces(chunks, [row, block + row], cut, core, y, s)

        pump()

    mine = pl.BlockSpec((1, 1, rows, units), lambda i: (i // parts, i % parts, 0, 0))
    theirs = pl.BlockSpec((1, 1, rows, units), lambda i: (1 - i // parts, i % parts, 0, 0))
    right = pl.BlockSpec((rows, half_cols), lambda i: (0, core), pipeline_mode=pl.Buffered(1))
    pltpu.emit_pipeline(body, grid=(2 * parts,), in_specs=[mine, theirs, right, right])(hid, hid_far, cot, cot_far)


def feed(core, part, n2, cot, fg, fu, fd, hid, ups, acc, begin):
    rows, model = n2.shape
    parts, tile = hid.shape[1], hid.shape[3]
    block = rows // 2

    def body(n2_ref, cot_ref, fg_ref, fu_ref, fd_ref, hid_ref, gg_ref, gu_ref):
        pump = begin()
        for r in range(2):
            at = slice(r * block, (r + 1) * block)
            gate, up = nn(n2_ref[at, :], fg_ref[...]), nn(n2_ref[at, :], fu_ref[...])
            g = nt(cot_ref[at, :], fd_ref[...])
            act, slope = gelu_parts(gate)
            hid_ref[0, 0, at, :] = (act * up).astype(BF16)
            gg_ref[0, 0, at, :] = (g * up * slope).astype(BF16)
            gu_ref[0, 0, at, :] = (g * act).astype(BF16)
        total = nt(gg_ref[0, 0], fg_ref[...]) + nt(gu_ref[0, 0], fu_ref[...])
        if part == 0:

            @pl.when(pl.program_id(0) == 0)
            def _():
                acc[...] = total

            @pl.when(pl.program_id(0) > 0)
            def _():
                acc[...] += total

        else:
            acc[...] += total
        pump()

    unit = lambda i: ((1 - i) * (1 - core) + i * core) * parts + part
    flat = pl.BlockSpec((rows, model), lambda i: (0, 0), pipeline_mode=pl.Buffered(1))
    col = pl.BlockSpec((model, tile), lambda i: (0, unit(i)))
    out = pl.BlockSpec((1, 1, rows, tile), lambda i: (i, part, 0, 0))
    pltpu.emit_pipeline(
        body, grid=(2,), in_specs=[flat, flat, col, col, pl.BlockSpec((tile, model), lambda i: (unit(i), 0))], out_specs=[out, out, out]
    )(n2, cot, fg, fu, fd, hid, ups.at[0], ups.at[1])


def norm_back(core, gn, resid, cot, fgain, gres, low, gain_sum):
    rows, model = gn.shape
    tile = 128
    gain_sum[...] = jnp.zeros_like(gain_sum)

    def body(y_ref, c_ref, out_ref):
        g = fgain[...]

        def norm(i, total):
            at = pl.ds(pl.multiple_of(i * 16, 16), 16)
            place = pl.ds(pl.multiple_of(pl.program_id(0) * tile + i * 16, 16), 16)
            y, d = y_ref[at, :], gn[place, :]
            r = lax.rsqrt(jnp.mean(y * y, axis=-1, keepdims=True) + 1e-06)
            dg, yr = d * g, y * r
            dot = jnp.mean(dg * yr, axis=-1, keepdims=True)
            out = c_ref[at, :].astype(F32) + r * (dg - yr * dot)
            out_ref[at, :] = out
            low[place, :] = out.astype(BF16)
            add = d * yr
            return total + add[0:8] + add[8:16]

        total = lax.fori_loop(0, tile // 16, norm, jnp.zeros((8, model), F32))
        gain_sum[...] += jnp.sum(total, axis=0, keepdims=True)

    row = pl.BlockSpec((tile, model), lambda i: (i, 0))
    pltpu.emit_pipeline(body, grid=(rows // tile,), in_specs=[row, row], out_specs=[row])(resid, cot, gres)


def turn(core, seqs, length, low, ow, gate, state, rate, vec, ggate, lc, q, carry, gj, begin):
    rows, lru = gate.shape
    width = lru // 2

    def body(ow_ref, gate_ref, state_ref, rate_ref, vec_ref, gg_ref, lc_ref, q_ref):
        pump = begin()
        for s in range(seqs):
            gj[s, 0:length, :] = nt(low[s * length : (s + 1) * length, :], ow_ref[...])
        pump()
        slope = -8.0 * vec_ref[3:4, :]
        for s in range(seqs):

            def act(i, _):
                at = pl.ds(pl.multiple_of(s * length + i * 16, 16), 16)
                here = pl.ds(pl.multiple_of(i * 16, 16), 16)
                value, der = gelu_parts(gate_ref[at, :])
                d = gj[s, here, :]
                gg_ref[0, at, :] = (d * state_ref[at, :] * der).astype(BF16)
                gj[s, here, :] = d * value
                return 0

            lax.fori_loop(0, length // 16, act, 0)
            pump()

        row = lax.broadcasted_iota(jnp.int32, (8, width), 0)
        tiles = length // 8

        def scan(k, last):
            i = tiles - 1 - k
            out = []
            for s in range(seqs):
                at = pl.ds(pl.multiple_of(s * length + i * 8, 8), 8)
                g = gj[s, pl.ds(pl.multiple_of(i * 8, 8), 8), :]
                a = jnp.exp(rate_ref[at, :] * slope)
                b = a * g
                for d in (1, 2, 4):
                    keep = row < 8 - d
                    b = b + a * jnp.where(keep, pltpu.roll(b, 8 - d, 0), 0.0)
                    a = a * jnp.where(keep, pltpu.roll(a, 8 - d, 0), 1.0)
                ap, bp = last[s]
                b = b + a * bp
                a = a * ap
                lc_ref[at, :] = g + jnp.where(row < 7, pltpu.roll(b, 7, 0), bp)
                q_ref[at, :] = jnp.where(row < 7, pltpu.roll(a, 7, 0), ap)
                out.append((a[0:1], b[0:1]))
            return tuple(out)

        init = tuple((jnp.ones((1, width), F32), jnp.zeros((1, width), F32)) for _ in range(seqs))
        last = lax.fori_loop(0, tiles, scan, init)
        for s in range(seqs):
            carry[group(core), 0, s : s + 1, :] = last[s][0]
            carry[group(core), 1, s : s + 1, :] = last[s][1]
        pump()

    grp = lambda i: (1 - i) * (1 - core) + i * core
    col = lambda r: pl.BlockSpec((r, width), lambda i: (0, grp(i)))
    pltpu.emit_pipeline(
        body, grid=(2,),
        in_specs=[
            pl.BlockSpec((width, ow.shape[1]), lambda i: (grp(i), 0)), col(rows), col(rows), col(rows), col(8),
        ],
        out_specs=[pl.BlockSpec((1, rows, width), lambda i: (i, 0, 0)), col(rows), col(rows)],
    )(ow, gate, state, rate, vec, ggate, lc, q)


def gates_back(
    own, core, seqs, length, lc, q, cin, states, entry, rate, inlet, mixed, branch, edge, wr, wi, taps, vec,
    gb, head, tail, blocks, rate_sum, inlet_sum, sums_out, dr, di, gr, gi, gm, ext, begin,
):
    rows, lru = lc.shape
    width, bw_ = lru // 2, wr.shape[-1]
    per, sub = width // bw_, dr.shape[-1]

    def body(
        lc_ref, q_ref, state_ref, e_ref, rate_ref, inlet_ref, mixed_ref, branch_ref, edge_ref, wr_ref, wi_ref, taps_ref, vec_ref,
        gb_ref,
    ):
        pump = begin()
        mine = group(core)
        slope = -8.0 * vec_ref[3:4, :]
        zero = jnp.zeros((8, width), F32)
        row = lax.broadcasted_iota(jnp.int32, (16, width), 0)

        sums = (zero, zero, zero)
        for s in range(seqs):
            c_in, ent = cin[mine, s : s + 1, :], e_ref[s]

            def gates(i, carry):
                (before, t0, t1, t2) = carry
                at = pl.ds(pl.multiple_of(s * length + i * 16, 16), 16)
                state = state_ref[at, :]
                prev = jnp.where(row > 0, pltpu.roll(state, 1, 0), before)
                carried = lc_ref[at, :] + q_ref[at, :] * c_in
                rt, it, mx = rate_ref[at, :], inlet_ref[at, :], mixed_ref[at, :].astype(F32)
                log_decay = rt * slope
                decay = jnp.exp(log_decay)
                gap = drop(log_decay, decay)
                inv = lax.rsqrt(gap)
                nf = gap * inv
                im = it * mx
                g_log = carried * decay * (prev - im * decay * inv)
                cn = carried * nf
                g_rt = g_log * slope * (rt * (1.0 - rt))
                g_it = cn * im * (1.0 - it)
                gr[at, :] = g_rt.astype(BF16)
                gi[at, :] = g_it.astype(BF16)
                gm[s, pl.ds(pl.multiple_of(i * 16, 16), 16), :] = cn * it
                lr = g_log * rt
                return (state[15:16], t0 + lr[0:8] + lr[8:16], t1 + g_rt[0:8] + g_rt[8:16], t2 + g_it[0:8] + g_it[8:16])

            _, *sums = lax.fori_loop(0, length // 16, gates, (ent, *sums))
            pump()
        down = lambda v: jnp.sum(v, axis=0, keepdims=True)
        lanes = pl.ds(pl.multiple_of(mine * width, 128), width)
        sums_out[4:5, lanes] = down(sums[0]) * (-8.0 * vec_ref[4:5, :])
        sums_out[5:6, lanes] = down(sums[1])
        sums_out[6:7, lanes] = down(sums[2])

        for g in range(width // sub):
            cols = slice(g * sub, (g + 1) * sub)
            spread(dr, [wr_ref[g * 4 + a] for a in range(4)], 4, bw_)
            spread(di, [wi_ref[g * 4 + a] for a in range(4)], 4, bw_)
            back = nt(gr[:, cols], dr[...]) + nt(gi[:, cols], di[...])
            rs = tn(mixed_ref[:, cols], gr[:, cols])
            is_ = tn(mixed_ref[:, cols], gi[:, cols])
            for a in range(4):
                block = slice(a * bw_, (a + 1) * bw_)
                if own:
                    blocks[mine * per + g * 4 + a, :, 0:bw_] = rs[block, block].astype(BF16)
                    blocks[2 * per + mine * per + g * 4 + a, :, 0:bw_] = is_[block, block].astype(BF16)
                else:
                    rate_sum[mine * per + g * 4 + a] = rs[block, block]
                    inlet_sum[mine * per + g * 4 + a] = is_[block, block]
            for s in range(seqs):
                gm[s, 0:length, cols] += back[s * length : (s + 1) * length]
        pump()

        for s in range(seqs):
            gm[s, length : length + 8, :] = zero
            ext[s, 0:8, :] = edge_ref[16 * s : 16 * s + 16].astype(F32)[8:16]
            ext[s, 8 : 8 + length, :] = branch_ref[s * length : (s + 1) * length].astype(F32)
            head[mine, 8 * s : 8 * s + 8, :] = gm[s, 0:8, :]

        tap = [taps_ref[k : k + 1, :] for k in range(4)]
        acc = (zero,) * 5
        for s in range(seqs):

            def conv(i, acc):
                lo = pl.multiple_of(i * 16, 16)
                y = gm[s, pl.ds(lo, 24), :]
                x = ext[s, pl.ds(lo, 24), :]
                total = tap[0] * y[0:16]
                for k in range(1, 4):
                    total = total + tap[k] * y[k : k + 16]
                gb_ref[0, pl.ds(pl.multiple_of(s * length + i * 16, 16), 16), :] = total.astype(BF16)
                now = y[0:16]
                new = []
                for k in range(4):
                    prod = now * x[8 - k : 24 - k]
                    new.append(acc[k] + prod[0:8] + prod[8:16])
                new.append(acc[4] + now[0:8] + now[8:16])
                return tuple(new)

            acc = lax.fori_loop(0, length // 16, conv, acc)
            y = gm[s, length - 16 : length + 8, :]
            total = tap[0] * y[0:16]
            for k in range(1, 4):
                total = total + tap[k] * y[k : k + 16]
            tail[mine, 16 * s : 16 * s + 16, :] = total
            pump()
        for k in range(4):
            sums_out[k : k + 1, lanes] = down(acc[k])
        sums_out[7:8, lanes] = down(acc[4])

    grp = lambda i: (1 - i) * (1 - core) + i * core
    col = lambda r: pl.BlockSpec((r, width), lambda i: (0, grp(i)))
    blk = pl.BlockSpec((per, bw_, bw_), lambda i: (grp(i), 0, 0))
    pltpu.emit_pipeline(
        body, grid=(2,),
        in_specs=[
            col(rows), col(rows), col(rows), pl.BlockSpec((seqs, 1, width), lambda i: (0, 0, grp(i))),
            col(rows), col(rows), col(rows), col(rows), col(edge.shape[0]), blk, blk, col(4), col(8),
        ],
        out_specs=[pl.BlockSpec((1, rows, width), lambda i: (i, 0, 0))],
    )(lc, q, states, entry, rate, inlet, mixed, branch, edge, wr, wi, taps, vec, gb)


def spaced(exchange, name, steps):
    def begin():
        place = iter(range(64))

        def pump():
            j = next(place)
            for i in range(steps):
                if PLAN.get(f"{name}{i}{j}"):

                    @pl.when(pl.program_id(0) == i)
                    def _():
                        exchange.at(f"{name}{i}{j}")

        return pump

    return begin


def no_pump():
    return lambda: None


ANY = pl.BlockSpec(memory_space=pl.ANY)
INSIDE = pl.BlockSpec(memory_space=pltpu.VMEM)


KINDS = "AFEAFEAFEAFE"
PLAN = {
    "u000": [(-1, 0)],
    "u010": [(-1, 1)],
    "f200": [(0, 0), (0, 1)],
    "u100": [(-1, 2)],
    "u110": [(1, 0), (-1, 3), (1, 1)],
    "u200": [(-1, 4)],
    "d00": [(2, 0), (2, 1)],
    "d40": [(3, 0), (3, 1), (0, 2), (-1, 5)],
    "t00": [(4, 0), (4, 1), (0, 3), (-1, 6)],
    "t01": [(1, 2)],
    "t02": [(5, 0), (5, 1), (0, 4), (-1, 7)],
    "t12": [(2, 2)],
    "b1": [(3, 2), (1, 3), (0, 5), (-1, 8)],
    "b2": [(1, 4)],
    "g01": [(4, 2), (0, 6), (-1, 9)],
    "g02": [(2, 3), (2, 4)],
    "g03": [(5, 2), (0, 7)],
    "g10": [(1, 5)],
    "g11": [(3, 3), (3, 4)],
    "c1": [(-1, 10), (4, 3), (4, 4), (2, 5), (1, 6), (1, 7), (0, 8), (6, 0)],
    "c3": [(5, 3), (5, 4), (6, 1)],
    "c4": [(-1, 11), (3, 5)],
    "i00": [(2, 6), (2, 7), (0, 9)],
    "i10": [(4, 5)],
    "i30": [(5, 5)],
    "o00": [(3, 6), (3, 7), (1, 8), (6, 2)],
    "o10": [(7, 0)],
    "drain": [(4, 6), (4, 7), (0, 10), (7, 1), (5, 6), (5, 7), (6, 3), (2, 8), (0, 11), (1, 9), (7, 2), (3, 8), (6, 4), (6, 5), (4, 8), (1, 10), (7, 3), (6, 6), (2, 9), (5, 8), (6, 7), (1, 11), (7, 4), (3, 9), (6, 8), (2, 10), (4, 9), (5, 9), (2, 11), (3, 10), (6, 9), (3, 11), (4, 10), (6, 10), (5, 10), (4, 11), (5, 11)],
}

PARTS = [256] * 9 + [384] * 3
SWAPS = 10


def backward(own, seqs, length, seq_n, batch_n, grads_in, values, collective_id):
    (
        n2, resid, cot, fgain, ow, gate, state, entry, rate, vec, inlet, mixed, branch, edge, wr, wi, taps, gw, bw, tok, mgain,
        fg, fu, fd, joined, normed,
    ) = values
    rows, model = n2.shape
    lru, units = gate.shape[1], fd.shape[0]
    width, bw_ = lru // 2, wr.shape[-1]
    per, sub = width // bw_, 4 * bw_
    steps = [("batch", 1 << k) for k in range(batch_n.bit_length() - 1)] + [("seq", 1 << k) for k in range(seq_n.bit_length() - 1)]
    n_steps = len(steps)
    parts, unit = 3, units // 6
    if not own:
        grads_in = []

    def kernel(*refs):
        refs = list(refs)
        cut = lambda n: [refs.pop(0) for _ in range(n)]
        far_in = cut(len(grads_in))
        (
            n2, resid, cot, fgain, ow, gate, state, entry, rate, vec, inlet, mixed, branch, edge, wr, wi, taps, gw, bw, tok, mgain,
            fg, fu, fd, joined, normed,
        ) = cut(26)
        tokens_grad, block_out, totals, gres, low_out, low_far, ggate, ggate_far, lc, q, gb, gb_far, hid, hid_far, ups, ups_far, n2_far, joined_far = cut(18)
        fin, block_total = cut(2) if own else (None, None)
        rate_sum, inlet_sum = (None, None) if own else cut(2)
        low, carry, got, cin, dr, di, gr, gi, gm, ext, head, tail, ahead, fixed, gain_sum, acc, small, gn = cut(18)
        send, recv, swap_send, swap_recv, one, local, s_send, s_recv = cut(8)

        core = core_of()
        seq, bat = lax.axis_index("seq"), lax.axis_index("batch")
        other = (seq, bat + 1 - 2 * core)
        peers = [(flip(seq, bit), bat) if axis == "seq" else (seq, flip(bat, bit)) for axis, bit in steps]
        exchange, blocks = None, None
        if own:
            g0, g1, g2, *bufs, x_send, x_recv = cut(9)
            blocks, *block_bufs, b_send, b_recv = cut(8)
            places = [(ref, row) for row in (0, 256, 512) for ref in (g0, g1)] + [(g2, 0), (g2, 256), (g2, 512), (g0, 0), (g0, 384), (g1, 0)]
            chunks = [(ref, row, part, kind) for (ref, row), part, kind in zip(places, PARTS, KINDS)]
            exchange = Exchange(chunks, bufs, fin, x_send, x_recv)
            exchange.further[6] = BlockSums(blocks, block_bufs, block_total, b_send, b_recv).events()
            blocks[...] = jnp.zeros_like(blocks)
        small[0] = jnp.zeros((16, lru), F32)
        greet = [(lax.rem(seq + k, seq_n), bat) for k in range(1, seq_n)] + [peer for peer, step in zip(peers, steps) if step[0] == "batch"]
        meet(greet)

        def swap(j, src, dst):
            return pltpu.make_async_remote_copy(
                src_ref=src, dst_ref=dst, send_sem=swap_send.at[j], recv_sem=swap_recv.at[j], device_id=other, device_id_type=MESH
            )

        at = exchange.at if own else (lambda place: None)
        plan = lambda name, steps: spaced(exchange, name, steps) if own else no_pump
        run_feed = lambda p: feed(core, p, n2, cot, fg, fu, fd, hid, ups, gn, plan(f"f{p}", 2))
        if own:
            cot_far, normed_far = far_in
            n2_swap, joined_swap = swap(4, n2, n2_far), swap(5, joined, joined_far)
            ups_swaps = [swap(6 + p, ups.at[:, 0, p], ups_far.at[:, p]) for p in range(parts)]
            hid_swap = swap(9, hid, hid_far)
            run_up = lambda p: wgrad_up(core, chunks[2 * p], chunks[2 * p + 1], n2, n2_far, ups.at[:, 1, p], ups_far.at[:, p], plan(f"u{p}", 2))
            n2_swap.start()
            run_feed(0)
            ups_swaps[0].start()
            joined_swap.start()
            n2_swap.wait()
            ups_swaps[0].wait()
            run_up(0)
            run_feed(1)
            ups_swaps[1].start()
            run_feed(2)
            ups_swaps[2].start()
            hid_swap.start()
            ups_swaps[1].wait()
            run_up(1)
            ups_swaps[2].wait()
            run_up(2)
            joined_swap.wait()
            hid_swap.wait()
            wgrad_down(core, chunks[6:9], hid, hid_far, cot, cot_far, plan("d", 2 * parts))
        else:
            for p in range(parts):
                run_feed(p)
        norm_back(core, gn, resid, cot, fgain, gres, low, gain_sum)
        at("a4")
        keep = pltpu.make_async_copy(low, low_out, one)
        keep.start()
        low_swap = swap(0, low, low_far)
        low_swap.start()
        turn(
            core, seqs, length, low, ow, gate, state, rate, vec, ggate, lc, q, carry, gm,
            plan("t", 2),
        )
        gate_swap = swap(1, ggate.at[0], ggate_far)
        gate_swap.start()
        arriving = Entry(carry, got, seq_n, send, recv)
        arriving.start()
        keep.wait()
        low_swap.wait()
        if own:
            at("b0")
            exchange.free(0)
            exchange.free(2)
            wgrad(core, chunks[9:10], joined, joined_far, low_out, low_far, False)
            at("b1")
        arriving.finish(cin, True)
        gate_swap.wait()
        at("b2")
        gates_back(
            own, core, seqs, length, lc, q, cin, state, entry, rate, inlet, mixed, branch, edge, wr, wi, taps, vec,
            gb, head, tail, blocks, rate_sum, inlet_sum, small.at[0], dr, di, gr, gi, gm, ext,
            plan("g", 2),
        )

        to_left = pltpu.make_async_remote_copy(
            src_ref=head, dst_ref=ahead, send_sem=swap_send.at[2], recv_sem=swap_recv.at[2],
            device_id=(lax.rem(seq + seq_n - 1, seq_n), bat), device_id_type=MESH,
        )
        to_left.start()
        if own:
            at("c0")
            exchange.free(4)
            wgrad(core, chunks[10:11], normed, normed_far, ggate.at[1], ggate_far, True)
            at("c1")
        to_left.wait()
        weight = (seq < seq_n - 1).astype(F32)
        copies = []
        for i in range(2):
            mine = (1 - i) * (1 - core) + i * core
            for s in range(seqs):
                y = ahead[mine, 8 * s : 8 * s + 8, :] * weight
                t = tail[mine, 16 * s : 16 * s + 16, :]
                grown = jnp.concatenate([jnp.zeros((16, width), F32), y], axis=0)
                for k in range(1, 4):
                    t = t + taps[k : k + 1, pl.ds(pl.multiple_of(mine * width, 128), width)] * grown[k : k + 16]
                fixed[i, 16 * s : 16 * s + 16, :] = t.astype(BF16)
                copy = pltpu.make_async_copy(
                    fixed.at[i, 16 * s : 16 * s + 16], gb.at[i, (s + 1) * length - 16 : (s + 1) * length], local.at[i, s]
                )
                copy.start()
                copies.append(copy)
        for copy in copies:
            copy.wait()
        branch_swap = swap(3, gb.at[0], gb_far)
        branch_swap.start()
        at("c2")
        branch_swap.wait()
        at("c3")
        if own:
            exchange.free(1)
            exchange.free(3)
            wgrad(core, chunks[11:12], normed, normed_far, gb.at[1], gb_far, True)
            at("c4")

        begin = plan("i", 4)
        tile = 128
        acc[...] = jnp.zeros_like(acc)

        def input_grad(gg_ref, gb_ref, gwt, gwm, bwt, bwm, x_ref, gr_ref, out):
            pump = begin()
            d = nt(gg_ref[0], gwt[...]) + nt(gg_ref[1], gwm[...]) + nt(gb_ref[0], bwt[...]) + nt(gb_ref[1], bwm[...])
            x = x_ref[...].astype(F32)
            r = lax.rsqrt(jnp.mean(x * x, axis=-1, keepdims=True) + 1e-06)
            xr, dg = x * r, d * mgain[...]
            out[...] = gr_ref[...] + r * (dg - xr * jnp.mean(dg * xr, axis=-1, keepdims=True))
            acc[...] += jnp.sum(d * xr, axis=0, keepdims=True)
            pump()

        row = pl.BlockSpec((tile, model), lambda i: (i, 0))
        pair = pl.BlockSpec((2, tile, width), lambda i: (0, i, 0))
        side = lambda c: pl.BlockSpec((model, width), lambda i: (0, c), pipeline_mode=pl.Buffered(1))
        pltpu.emit_pipeline(
            input_grad, grid=(rows // tile,), in_specs=[pair, pair, side(1 - core), side(core), side(1 - core), side(core), row, row], out_specs=[row]
        )(ggate, gb, gw, gw, bw, bw, tok, gres, tokens_grad)

        small[0, 8:9, 0:model] = acc[...]
        small[0, 9:10, 0:model] = gain_sum[...]

        def small_step(k):
            return pltpu.make_async_remote_copy(
                src_ref=small.at[0], dst_ref=small.at[k + 1], send_sem=s_send.at[k], recv_sem=s_recv.at[k],
                device_id=peers[k], device_id_type=MESH,
            )

        def small_event(k):
            small_step(k).wait()
            small[0] = small[0] + small[k + 1]
            if k + 1 < n_steps:
                small_step(k + 1).start()

        small_events = [functools.partial(small_event, k) for k in range(n_steps)]
        small_step(0).start()
        if own:
            exchange.further[7] = small_events
        begin_out = plan("o", 4)
        tile_out = 256

        def last(r, *rest):
            pump = begin_out()
            hid_refs, down_refs, out = rest[: 2 * parts], rest[2 * parts : 4 * parts], rest[-1]
            total = r[...]
            for l, w in zip(hid_refs, down_refs):
                total = total + nn(l[0, 0], w[...])
            out[...] = total.astype(BF16)
            pump()

        col = pl.BlockSpec((rows, tile_out), lambda i: (0, i))
        order = [(side, p) for side in range(2) for p in range(parts)]
        hid_spec = lambda side, p: pl.BlockSpec((1, 1, rows, unit), lambda i: (side, p, 0, 0), pipeline_mode=pl.Buffered(1))
        down_spec = lambda half, p: pl.BlockSpec((unit, tile_out), lambda i: (half * parts + p, i))
        pltpu.emit_pipeline(
            last, grid=(model // tile_out,),
            in_specs=[col] + [hid_spec(*o) for o in order] + [down_spec(core if side else 1 - core, p) for side, p in order], out_specs=[col],
        )(resid, *([hid] * 2 * parts), *([fd] * 2 * parts), block_out)
        if own:
            exchange.drain()
        else:
            for event in small_events:
                event()
        totals[...] = small[0]

    f = lambda *shape: jax.ShapeDtypeStruct(shape, F32)
    b = lambda *shape: jax.ShapeDtypeStruct(shape, BF16)
    vm, dma = pltpu.VMEM, lambda *shape: pltpu.SemaphoreType.DMA(shape)
    out_shape = [
        f(rows, model), b(rows, model), f(16, lru),
        f(rows, model), b(rows, model), b(rows, model), b(2, rows, width), b(rows, width), f(rows, lru), f(rows, lru), b(2, rows, width), b(rows, width),
        b(2, parts, rows, unit), b(2, parts, rows, unit), b(2, 2, parts, rows, unit), b(2, parts, rows, unit), b(rows, model), b(rows, lru),
    ]
    out_specs = [ANY, ANY, INSIDE] + [ANY] * 15
    scratch = [
        vm((rows, model), BF16), vm((2, 2, seqs, width), F32), vm((seq_n, 2, 2, seqs, width), F32), vm((2, seqs, width), F32),
        vm((sub, sub), BF16), vm((sub, sub), BF16), vm((rows, width), BF16), vm((rows, width), BF16),
        vm((seqs, length + 8, width), F32), vm((seqs, length + 8, width), F32), vm((2, 8 * seqs, width), F32), vm((2, 16 * seqs, width), F32),
        vm((2, 8 * seqs, width), F32), vm((2, 16 * seqs, width), BF16), vm((1, model), F32), vm((1, model), F32), vm((n_steps + 1, 16, lru), F32), vm((rows, model), F32),
        dma(seq_n), dma(seq_n), dma(SWAPS), dma(SWAPS), pltpu.SemaphoreType.DMA, dma(2, seqs), dma(n_steps), dma(n_steps),
    ]
    if own:
        out_shape += [b(2, 2, sum(PARTS), 128), b(4 * per, bw_, 128)]
        out_specs += [INSIDE, INSIDE]
        scratch += [vm((16, 768, 128), BF16)] * 3 + Exchange.scratch(len(PARTS), sum(PARTS))
        scratch += [vm((4 * per, bw_, 128), BF16)] + BlockSums.scratch(bw_)
    else:
        out_shape += [f(*wr.shape), f(*wi.shape)]
        out_specs += [INSIDE, INSIDE]
    ins = [ANY] * (len(grads_in) + len(values))
    for j in (3, 16, 20):
        ins[len(grads_in) + j] = INSIDE
    return pl.pallas_call(
        kernel,
        in_specs=ins,
        out_specs=out_specs,
        out_shape=out_shape,
        scratch_shapes=scratch,
        compiler_params=pltpu.CompilerParams(collective_id=collective_id, has_side_effects=True, vmem_limit_bytes=60 * 2**20),
        name="backward",
    )(*grads_in, *values)


def lay(sums, totals, blocks, model, lru, units, n):
    shapes = [(model // n, units), (model // n, units), (units // n, model), (lru // n, model), (model // n, lru), (model // n, lru)]
    rows = sums.shape[2]
    count, wide_b = blocks.shape[0] // 2, blocks.shape[1]

    def kernel(v, b, s, rate, inlet, taps, decay, rate_off, inlet_off, conv_off, gain1, gain2, *outs):
        taps[...] = s[0:4, :]
        for j, vector in enumerate((decay, rate_off, inlet_off, conv_off)):
            vector[...] = s[4 + j, :]
        gain1[...] = s[8, 0:model]
        gain2[...] = s[9, 0:model]
        for y in range(2):
            for m, out in enumerate(outs):
                part, wide = out.shape
                for t in range(wide // 256):
                    if m < 2:
                        at, col = t // 2 * 512 + m * 256 + t % 2 * 128, t // 2 * 512 + y * 256 + t % 2 * 128
                    else:
                        at, col = 1536 + [0, 768, 1152, 1536][m - 2] + t * part, y * wide // 2 + t * 128
                    out[:, col : col + 128] = v[0, y, at : at + part, :].astype(F32)
        for j in range(count // 2):
            rate[j] = b[0, j, :, 0:wide_b].astype(F32)
            inlet[j] = b[1, j, :, 0:wide_b].astype(F32)

    block = pl.BlockSpec((count // 2, wide_b, wide_b), lambda i: (i, 0, 0))
    flat = lambda size: (pl.BlockSpec((size,), lambda i: (0,)), jax.ShapeDtypeStruct((size,), F32))
    vectors = [(whole((4, lru)), jax.ShapeDtypeStruct((4, lru), F32))] + [flat(lru)] * 4 + [flat(model)] * 2
    return pl.pallas_call(
        kernel,
        grid=(2,),
        in_specs=[pl.BlockSpec((1, 2, rows, 128), lambda i: (i, 0, 0, 0)), pl.BlockSpec((2, count // 2, wide_b, 128), lambda i: (0, i, 0, 0)), whole(totals.shape)],
        out_specs=[block, block] + [v[0] for v in vectors] + [pl.BlockSpec((part, wide // 2), lambda i: (0, i)) for part, wide in shapes],
        out_shape=[jax.ShapeDtypeStruct((count, wide_b, wide_b), F32)] * 2 + [v[1] for v in vectors] + [jax.ShapeDtypeStruct(shape, F32) for shape in shapes],
        compiler_params=params(),
        name="lay",
    )(sums, blocks.reshape(2, count, wide_b, 128), totals)


def swap(value):
    count = lax.axis_size("batch")
    return lax.ppermute(value, "batch", [(i, i ^ 1) for i in range(count)])


def local(
    tokens, cotangent, gate_weight, branch_weight, out_weight, conv_taps, conv_offset, rate_weight, inlet_weight,
    rate_offset, inlet_offset, decay_param, mixer_gain, feed_gain, feed_gate, feed_up, feed_down,
):
    seqs, length, model = tokens.shape
    lru, units = gate_weight.shape[1], feed_gate.shape[1]
    rows = seqs * length
    seq_n, batch_n = lax.axis_size("seq"), lax.axis_size("batch")
    core = lax.rem(lax.axis_index("batch"), 2)

    tok, cot = tokens.reshape(rows, model), cotangent.reshape(rows, model)
    cot_far = swap(cot)
    none = jnp.zeros_like(conv_offset)
    vec = jnp.stack(
        [conv_offset, rate_offset, inlet_offset, jax.nn.softplus(decay_param), jax.nn.sigmoid(decay_param), none, none, none]
    )
    gain1, gain2 = mixer_gain[None], feed_gain[None]

    normed, gate, branch, edge, mixed, rate, inlet, h, p, entry = front(
        tok, gain1, gate_weight, branch_weight, conv_taps, vec, rate_weight, inlet_weight, seqs, length, seq_n, 0
    )
    normed_far = swap(normed)
    joined, resid, normed_two, state = join(tok, gate, h, p, entry, out_weight, gain2, seqs, length)

    own = (seq_n, batch_n) == (8, 4)
    tokens_grad, out, totals, _, grad_low, _, ggate, _, _, _, gb, _, hid, _, ups, _, _, _, *sums = backward(
        own, seqs, length, seq_n, batch_n, [cot_far, normed_far],
        [
            normed_two, resid, cot, gain2, out_weight, gate, state, entry, rate, vec, inlet, mixed, branch, edge,
            rate_weight, inlet_weight, conv_taps, gate_weight, branch_weight, tok, gain1, feed_gate, feed_up, feed_down, joined, normed,
        ],
        1,
    )
    if own:
        rate_all, inlet_all, *vectors = lay(sums[0], totals, sums[1], model, lru, units, seq_n)
        vectors, (gate_feed_all, up_feed_all, down_all, out_all, gate_all, branch_all) = vectors[:7], vectors[7:]
    else:
        vectors = [totals[0:4], *totals[4:8], totals[8, :model], totals[9, :model]]
        rate_all, inlet_all = lax.psum((sums[0], sums[1]), ("seq", "batch"))

        def full(pair):
            pair = pair if pair.ndim == 4 else pair[:, None]
            pair = jnp.where(core == 0, pair[::-1], pair)
            return pair.transpose(2, 0, 1, 3).reshape(rows, -1)

        def total(left, right):
            return lax.psum(lax.psum_scatter(tn(left, right), "seq", scatter_dimension=0, tiled=True), "batch")

        down_all = total(full(hid), cot)
        gate_feed_all, up_feed_all = total(normed_two, full(ups[0])), total(normed_two, full(ups[1]))
        out_all = total(joined, grad_low)
        gate_all, branch_all = total(normed, full(ggate)), total(normed, full(gb))

    return (
        out.reshape(seqs, length, model), tokens_grad.reshape(seqs, length, model), gate_all, branch_all, out_all,
        vectors[0], vectors[4], rate_all, inlet_all, vectors[2], vectors[3], vectors[1], vectors[5], vectors[6],
        gate_feed_all, up_feed_all, down_all,
    )


def solution(mesh):
    big = P("batch", "seq", None)
    in_specs = (big, big) + (P(),) * 15
    out_specs = (big, big) + (P("seq", None),) * 3 + (P(),) * 9 + (P("seq", None),) * 3
    return jax.shard_map(local, mesh=mesh, in_specs=in_specs, out_specs=out_specs, check_vma=False)
```

```python
import functools
import jax
import jax.numpy as jnp
from jax import lax
from jax.experimental import pallas as pl
from jax.experimental.pallas import tpu as pltpu
from jax.sharding import PartitionSpec as P

F32, BF16 = jnp.float32, jnp.bfloat16
VLIM = 56 * 2**20
GELU_A, GELU_B = 0.7978845608028654, 0.044715


def nn(a, b):
    return lax.dot_general(a, b, (((1,), (0,)), ((), ())), preferred_element_type=F32)


def nt(a, b):
    return lax.dot_general(a, b, (((1,), (1,)), ((), ())), preferred_element_type=F32)


def tn(a, b):
    return lax.dot_general(a, b, (((0,), (0,)), ((), ())), preferred_element_type=F32)


def sigmoid(v):
    return 1.0 / (1.0 + jnp.exp(-v))


def drop(u, decay):
    v = 2.0 * u
    series = 1.0 + v * (1.0 / 7.0)
    for k in (6.0, 5.0, 4.0, 3.0, 2.0):
        series = 1.0 + (v * (1.0 / k)) * series
    return jnp.where(v > -0.35, -v * series, 1.0 - decay * decay)


def gelu_parts(v):
    square = v * v
    inner = jnp.tanh(GELU_A * v * (1.0 + GELU_B * square))
    half = 0.5 + 0.5 * inner
    act = v * half
    slope = half + 0.5 * v * (1.0 - inner * inner) * (GELU_A + 3.0 * GELU_A * GELU_B * square)
    return act, slope


def gelu(v):
    inner = jnp.tanh(GELU_A * v * (1.0 + GELU_B * (v * v)))
    return v * (0.5 + 0.5 * inner)


def spread(dense, blocks, count, width):
    for a in range(count):
        parts = []
        if a > 0:
            parts.append(jnp.zeros((width, a * width), dense.dtype))
        parts.append(blocks[a])
        if a < count - 1:
            parts.append(jnp.zeros((width, (count - 1 - a) * width), dense.dtype))
        dense[a * width : (a + 1) * width, :] = jnp.concatenate(parts, axis=1)


def params(sem=("arbitrary",), **kw):
    return pltpu.CompilerParams(dimension_semantics=sem, vmem_limit_bytes=VLIM, **kw)


def whole(shape):
    return pl.BlockSpec(shape, lambda *_: (0,) * len(shape))


MESH = pl.DeviceIdType.MESH


def greet(peers):
    barrier = pltpu.get_barrier_semaphore()
    for peer in peers:
        pl.semaphore_signal(barrier, inc=1, device_id=peer, device_id_type=MESH)


def met(count):
    pl.semaphore_wait(pltpu.get_barrier_semaphore(), count)


def flip(index, bit):
    return index + bit - 2 * bit * (lax.rem(index // bit, 2))


class Entry:
    def __init__(self, part, got, n, send, recv):
        self.part, self.got, self.n = part, got, n
        self.me = lax.axis_index("seq")
        self.copies = [
            pltpu.make_async_remote_copy(
                src_ref=part, dst_ref=got.at[self.me], send_sem=send.at[k], recv_sem=recv.at[k],
                device_id=(lax.rem(self.me + k, n), lax.axis_index("batch")), device_id_type=MESH,
            )
            for k in range(1, n)
        ]

    def start(self):
        for copy in self.copies:
            copy.start()
        self.got[self.me] = self.part[...]

    def finish(self, out, reverse):
        for copy in self.copies:
            copy.wait()

        def one(k, state):
            j = self.n - 1 - k if reverse else k
            before = (j > self.me) if reverse else (j < self.me)
            return jnp.where(before, self.got[j, :, 0] * state + self.got[j, :, 1], state)

        out[...] = lax.fori_loop(0, self.n, one, jnp.zeros(out.shape, F32))


def front_kernel(
    seqs, length, seq_n, tok, gain, gw, bw, taps, vec, wr, wi,
    normed, gate, branch, edge, mixed, rate, inlet, h, p, entry,
    halo, hn, ext, dr, di, rp, ip, carry, got, state, h_send, h_recv, send, recv,
):
    rows, width = seqs * length, gw.shape[1]
    sub = dr.shape[-1]

    seq, bat = lax.axis_index("seq"), lax.axis_index("batch")

    copies = [
        pltpu.make_async_remote_copy(
            src_ref=tok.at[(s + 1) * length - 16 : (s + 1) * length], dst_ref=halo.at[s], send_sem=h_send.at[s], recv_sem=h_recv.at[s],
            device_id=(lax.rem(seq + 1, seq_n), bat), device_id_type=MESH,
        )
        for s in range(seqs)
    ]

    @pl.when(pl.program_id(0) == 0)
    def _():
        greet([(lax.rem(seq + k, seq_n), bat) for k in range(1, seq_n)])

        def norm(i, _):
            x = tok[pl.ds(i * 32, 32), :].astype(F32)
            r = lax.rsqrt(jnp.mean(x * x, axis=-1, keepdims=True) + 1e-06)
            normed[pl.ds(i * 32, 32), :] = (x * r * gain[...]).astype(BF16)
            return 0

        lax.fori_loop(0, rows // 32, norm, 0)
        met(seq_n - 1)
        for copy in copies:
            copy.start()

    gate[...] = nn(normed[...], gw[...])
    b16 = nn(normed[...], bw[...]).astype(BF16)

    @pl.when(pl.program_id(0) == 0)
    def _():
        for s in range(seqs):
            copies[s].wait()
            x = halo[s].astype(F32)
            r = lax.rsqrt(jnp.mean(x * x, axis=-1, keepdims=True) + 1e-06)
            hn[16 * s : 16 * s + 16, :] = (x * r * gain[...]).astype(BF16)

    e16 = (nn(hn[...], bw[...]) * (seq > 0).astype(F32)).astype(BF16)
    branch[...] = b16
    edge[...] = e16
    e32 = e16.astype(F32)
    for s in range(seqs):
        ext[s, 0:8, :] = e32[16 * s + 8 : 16 * s + 16]
        ext[s, 8 : 8 + length, :] = b16[length * s : length * (s + 1)].astype(F32)

    tap = [taps[k : k + 1, :] for k in range(4)]
    off = vec[0:1, :]
    for s in range(seqs):

        def conv(i, _):
            x = ext[s, pl.ds(pl.multiple_of(i * 16, 16), 24), :]
            total = off + tap[0] * x[8:24]
            for k in range(1, 4):
                total = total + tap[k] * x[8 - k : 24 - k]
            mixed[pl.ds(pl.multiple_of(s * length + i * 16, 16), 16), :] = total.astype(BF16)
            return 0

        lax.fori_loop(0, length // 16, conv, 0)

    for g in range(width // sub):
        cols = slice(g * sub, (g + 1) * sub)
        spread(dr.at[g], [wr[g * 4 + a] for a in range(4)], 4, wr.shape[-1])
        spread(di.at[g], [wi[g * 4 + a] for a in range(4)], 4, wi.shape[-1])
        rp[:, cols] = nn(mixed[:, cols], dr[g])
        ip[:, cols] = nn(mixed[:, cols], di[g])

    ro, io, slope = vec[1:2, :], vec[2:3, :], -8.0 * vec[3:4, :]

    def gates(i, _):
        at = pl.ds(pl.multiple_of(i * 16, 16), 16)
        rt = sigmoid(rp[at, :] + ro)
        it = sigmoid(ip[at, :] + io)
        log_decay = rt * slope
        decay = jnp.exp(log_decay)
        rate[at, :] = rt
        inlet[at, :] = it
        p[at, :] = decay
        h[at, :] = jnp.sqrt(drop(log_decay, decay)) * it * mixed[at, :].astype(F32)
        return 0

    lax.fori_loop(0, rows // 16, gates, 0)

    row = lax.broadcasted_iota(jnp.int32, (8, width), 0)

    def scan(i, last):
        out = []
        for s in range(seqs):
            at = pl.ds(pl.multiple_of(s * length + i * 8, 8), 8)
            a, b = p[at, :], h[at, :]
            for d in (1, 2, 4):
                keep = row >= d
                b = b + a * jnp.where(keep, pltpu.roll(b, d, 0), 0.0)
                a = a * jnp.where(keep, pltpu.roll(a, d, 0), 1.0)
            ap, bp = last[s]
            b = b + a * bp
            a = a * ap
            p[at, :] = a
            h[at, :] = b
            out.append((a[7:8], b[7:8]))
        return tuple(out)

    init = tuple((jnp.ones((1, width), F32), jnp.zeros((1, width), F32)) for _ in range(seqs))
    last = lax.fori_loop(0, length // 8, scan, init)
    for s in range(seqs):
        carry[pl.program_id(0), 0, s : s + 1, :] = last[s][0]
        carry[pl.program_id(0), 1, s : s + 1, :] = last[s][1]

    @pl.when(pl.program_id(0) == 1)
    def _():
        arriving = Entry(carry, got, seq_n, send, recv)
        arriving.start()
        arriving.finish(state, False)
        for g in range(2):
            for s in range(seqs):
                entry[s, :, g * width : (g + 1) * width] = state[g, s : s + 1, :]


def front(tok, gain, gw, bw, taps, vec, wr, wi, seqs, length, seq_n, collective_id):
    rows, model = tok.shape
    lru, bw_ = gw.shape[1], wr.shape[-1]
    width, sub, per = lru // 2, 4 * bw_, lru // 2 // bw_
    col = lambda r: pl.BlockSpec((r, width), lambda j: (0, j))
    blk = pl.BlockSpec((per, bw_, bw_), lambda j: (j, 0, 0))
    f = lambda dt: jax.ShapeDtypeStruct((rows, lru), dt)
    vm, dma = pltpu.VMEM, lambda n: pltpu.SemaphoreType.DMA((n,))
    return pl.pallas_call(
        functools.partial(front_kernel, seqs, length, seq_n),
        grid=(2,),
        in_specs=[
            whole((rows, model)), whole((1, model)),
            pl.BlockSpec((model, width), lambda j: (0, j)), pl.BlockSpec((model, width), lambda j: (0, j)), col(4), col(8), blk, blk,
        ],
        out_specs=[
            whole((rows, model)), col(rows), col(rows), col(16 * seqs), col(rows), col(rows), col(rows), col(rows), col(rows),
            whole((seqs, 1, lru)),
        ],
        out_shape=[
            jax.ShapeDtypeStruct((rows, model), BF16), f(F32), f(BF16),
            jax.ShapeDtypeStruct((16 * seqs, lru), BF16), f(BF16), f(F32), f(F32), f(F32), f(F32),
            jax.ShapeDtypeStruct((seqs, 1, lru), F32),
        ],
        scratch_shapes=[
            vm((seqs, 16, model), BF16), vm((16 * seqs, model), BF16), vm((seqs, 8 + length, width), F32),
            vm((2, sub, sub), BF16), vm((2, sub, sub), BF16), vm((rows, width), F32), vm((rows, width), F32),
            vm((2, 2, seqs, width), F32), vm((seq_n, 2, 2, seqs, width), F32), vm((2, seqs, width), F32),
            dma(seqs), dma(seqs), dma(seq_n), dma(seq_n),
        ],
        compiler_params=params(collective_id=collective_id, has_side_effects=True),
        name="front",
    )(tok, gain, gw, bw, taps, vec, wr, wi)


def join_kernel(tok, gate, h, p, entry, ow, gain, joined, resid, normed, state_ref):
    rows = tok.shape[0]
    ent = entry[0]

    def join(i, _):
        at = pl.ds(pl.multiple_of(i * 16, 16), 16)
        state = h[at, :] + p[at, :] * ent
        state_ref[at, :] = state
        joined[at, :] = (gelu(gate[at, :]) * state).astype(BF16)
        return 0

    lax.fori_loop(0, rows // 16, join, 0)
    resid[...] = nn(joined[...], ow[...])

    def norm(i, _):
        at = pl.ds(pl.multiple_of(i * 32, 32), 32)
        y = tok[at, :].astype(F32) + resid[at, :]
        resid[at, :] = y
        r = lax.rsqrt(jnp.mean(y * y, axis=-1, keepdims=True) + 1e-06)
        normed[at, :] = (y * r * gain[...]).astype(BF16)
        return 0

    lax.fori_loop(0, rows // 32, norm, 0)


def join(tok, gate, h, p, entry, ow, gain, seqs, length):
    rows, model = tok.shape
    lru = gate.shape[1]
    tile = 128
    per = length // tile
    row = lambda w: pl.BlockSpec((tile, w), lambda i: (i, 0))
    return pl.pallas_call(
        join_kernel,
        grid=(rows // tile,),
        in_specs=[row(model), row(lru), row(lru), row(lru), pl.BlockSpec((1, 1, lru), lambda i: (i // per, 0, 0)), whole((lru, model)), whole((1, model))],
        out_specs=[row(lru), row(model), row(model), row(lru)],
        out_shape=[jax.ShapeDtypeStruct((rows, lru), BF16), jax.ShapeDtypeStruct((rows, model), F32), jax.ShapeDtypeStruct((rows, model), BF16), jax.ShapeDtypeStruct((rows, lru), F32)],
        compiler_params=params(),
        name="join",
    )(tok, gate, h, p, entry, ow, gain)


ORDERS = {"A": ("xhyl", "yxhl"), "E": ("xlhy", "yxlh"), "F": ("xylh", "yxlh")}


class Exchange:
    def __init__(self, chunks, bufs, fin, send, recv):
        self.chunks, self.bufs, self.fin, self.sems = chunks, bufs, fin, (send, recv)
        self.first = [sum(c[2] for c in chunks[:q]) for q in range(len(chunks))]
        seq, bat = lax.axis_index("seq"), lax.axis_index("batch")
        core, y = lax.rem(bat, 2), bat // 2
        x, low, high = lax.rem(seq, 2), lax.rem(seq // 2, 2), seq // 4
        bit = {"x": x, "y": y, "l": low, "h": high}
        move = {"x": (1 - 2 * x, 0), "y": (0, 2 - 4 * y), "l": (2 - 4 * low, 0), "h": (4 - 8 * high, 0)}
        pick = lambda a, b: a if a is b else (1 - core) * a + core * b
        self.core, self.y = core, y
        self.other, self.across = (seq, bat + 1 - 2 * core), (seq, bat + 2 - 4 * y)
        self.bits, self.peers = {}, {}
        for kind, (first, second) in ORDERS.items():
            self.bits[kind] = [pick(bit[a], bit[b]) for a, b in zip(first, second)]
            self.peers[kind] = [
                (seq + pick(move[a][0], move[b][0]), bat + pick(move[a][1], move[b][1])) for a, b in zip(first, second)
            ] + [self.across, self.other]
        self.greet = [(seq + move[a][0], bat) for a in "xlh"] + [self.across, self.other]
        self.freed, self.further = set(), {}

    def at(self, place):
        for k, q in PLAN.get(place, ()):
            self.step(k, q)

    def free(self, q):
        self.copy(0, q).wait_send()
        self.freed.add(q)

    def drain(self):
        self.at("drain")
        for q in range(len(self.chunks)):
            for k in range(4):
                if k > 0 or q not in self.freed:
                    self.copy(k, q).wait_send()

    def copy(self, k, q):
        grad, row, part, kind = self.chunks[q]
        size, bits = 8 >> k, self.bits[kind]
        at = slice(self.first[q], self.first[q] + part)
        if k == 0:
            src, dst = grad.at[pl.ds((1 - bits[0]) * 8, 8), row : row + part], self.bufs[0].at[:, at]
        elif k < 4:
            src, dst = self.bufs[k - 1].at[pl.ds((1 - bits[k]) * size, size), at], self.bufs[k].at[:, at]
        elif k == 4:
            src = dst = self.fin.at[self.core, self.y, at]
        else:
            src = dst = self.fin.at[self.core, :, at]
        return pltpu.make_async_remote_copy(
            src_ref=src, dst_ref=dst, send_sem=self.sems[0].at[k, q], recv_sem=self.sems[1].at[k, q],
            device_id=self.peers[kind][k], device_id_type=MESH,
        )

    def add(self, k, q, base, size):
        grad, row, part, kind = self.chunks[q]
        dst, bits = self.bufs[k], self.bits[kind]
        for j in range(size):

            def body(i, _):
                a = pl.ds(pl.multiple_of(self.first[q] + i * 128, 128), 128)
                if k == 0:
                    own = grad[bits[0] * 8 + base + j, pl.ds(pl.multiple_of(row + i * 128, 128), 128), :]
                else:
                    own = self.bufs[k - 1][bits[k] * (8 >> k) + base + j, a, :]
                dst[base + j, a, :] = dst[base + j, a, :] + own
                return 0

            lax.fori_loop(0, part // 128, body, 0)

    def step(self, k, q):
        if k > 5:
            self.further[k][q]()
        elif k < 0:
            self.copy(0, q).start()
        elif k < 3:
            half, bits = 4 >> k, self.bits[self.chunks[q][3]]
            self.copy(k, q).wait_recv()
            self.add(k, q, (1 - bits[k + 1]) * half, half)
            self.copy(k + 1, q).start()
            self.add(k, q, bits[k + 1] * half, half)
        elif k == 3:
            bits = self.bits[self.chunks[q][3]]
            self.copy(3, q).wait_recv()

            def body(i, _):
                a = pl.ds(pl.multiple_of(self.first[q] + i * 128, 128), 128)
                self.fin[self.core, self.y, a, :] = self.bufs[3][0, a, :] + self.bufs[2][bits[3], a, :]
                return 0

            lax.fori_loop(0, self.chunks[q][2] // 128, body, 0)
            self.copy(4, q).start()
        elif k == 4:
            self.copy(4, q).wait()
            self.copy(5, q).start()
        else:
            self.copy(5, q).wait()

    @staticmethod
    def scratch(chunks, rows):
        return [pltpu.VMEM((8 >> k, rows, 128), BF16) for k in range(4)] + [pltpu.SemaphoreType.DMA((6, chunks))] * 2


class BlockSums:
    def __init__(self, value, bufs, out, send, recv):
        self.value, self.bufs, self.out, self.sems = value, bufs, out, (send, recv)
        seq, bat = lax.axis_index("seq"), lax.axis_index("batch")
        core, y = lax.rem(bat, 2), bat // 2
        x, low, high = lax.rem(seq, 2), lax.rem(seq // 2, 2), seq // 4
        self.bits = [core, low, high, x, y]
        self.peers = [(seq, bat + 1 - 2 * core), (seq + 2 - 4 * low, bat), (seq + 4 - 8 * high, bat), (seq + 1 - 2 * x, bat), (seq, bat + 2 - 4 * y)]
        self.base = [0]
        for k in range(5):
            self.base.append(self.base[-1] + self.bits[k] * (16 >> k))

    def halve(self, k):
        size = 16 >> k
        return pltpu.make_async_remote_copy(
            src_ref=self.value.at[pl.ds(self.base[k] + (1 - self.bits[k]) * size, size)], dst_ref=self.bufs[k],
            send_sem=self.sems[0].at[k], recv_sem=self.sems[1].at[k], device_id=self.peers[k], device_id_type=MESH,
        )

    def hand(self, k):
        at = pl.ds(self.base[k + 1], 16 >> k)
        return pltpu.make_async_remote_copy(
            src_ref=self.out.at[at], dst_ref=self.out.at[at],
            send_sem=self.sems[0].at[5 + k], recv_sem=self.sems[1].at[5 + k], device_id=self.peers[k], device_id_type=MESH,
        )

    def events(self):
        def took(k):
            size = 16 >> k
            self.halve(k).wait()

            def body(j, _):
                at = self.base[k + 1] + j
                total = (self.value[at].astype(F32) + self.bufs[k][j].astype(F32)).astype(BF16)
                if k < 4:
                    self.value[at] = total
                else:
                    self.out[at] = total
                return 0

            lax.fori_loop(0, size, body, 0)
            if k < 4:
                self.halve(k + 1).start()
            else:
                self.hand(4).start()

        def got(k):
            self.hand(k).wait()
            if k > 0:
                self.hand(k - 1).start()

        first = [lambda: self.halve(0).start()]
        return first + [functools.partial(took, k) for k in range(5)] + [functools.partial(got, k) for k in range(4, -1, -1)]

    @staticmethod
    def scratch(width):
        return [pltpu.VMEM((16 >> k, width, 128), BF16) for k in range(5)] + [pltpu.SemaphoreType.DMA((10,))] * 2


def core_of():
    return lax.rem(lax.axis_index("batch"), 2)


def group(core):
    i = pl.program_id(0)
    return (1 - i) * (1 - core) + i * core


def put_pieces(chunks, row, acc, core, y, s):
    part, cols = acc.shape
    for t in range(cols // 128):
        at = row[t] if isinstance(row, (list, tuple)) else row + t * part
        base = 0
        for ref, first, rows, kind in chunks:
            low, high = max(at, base), min(at + part, base + rows)
            if low < high:
                ref[place_of(core, s, y, kind), first + low - base : first + high - base, :] = acc[
                    low - at : high - at, t * 128 : (t + 1) * 128
                ].astype(BF16)
            base += rows


def place_of(core, s, y, kind):
    bit = {"x": s % 2, "l": (s // 2) % 2, "h": s // 4, "y": y}
    place = lambda order: sum(bit[a] * (8 >> k) for k, a in enumerate(order))
    first, second = ORDERS[kind]
    return place(first) if first == second else (1 - core) * place(first) + core * place(second)


def wgrad(core, chunks, lhs, lhs_far, rhs, rhs_far, own_columns):
    rows, deep = lhs.shape
    tile = rhs.shape[1] // (2 if own_columns else 4)
    base, part = 0 if own_columns else 2 * core, deep // 8

    def body(a, b, c, d):
        acc = tn(a[...], c[...]) + tn(b[...], d[...])
        for s in range(8):
            put_pieces(chunks, 0, acc[s * part : (s + 1) * part], core, pl.program_id(0), s)

    left = pl.BlockSpec(lhs.shape, lambda y: (0, 0), pipeline_mode=pl.Buffered(1))
    right = pl.BlockSpec((rows, tile), lambda y: (0, base + y))
    pltpu.emit_pipeline(body, grid=(2,), in_specs=[left, left, right, right])(lhs, lhs_far, rhs, rhs_far)


def wgrad_up(core, gate_chunk, up_chunk, lhs, lhs_far, rhs, rhs_far, begin):
    rows, deep = lhs.shape
    tile, part = rhs.shape[2], deep // 8

    def body(a, b, c, d):
        pump = begin()
        acc = tn(a[...], c[0]) + tn(b[...], d[0])
        for j, chunk in enumerate((gate_chunk, up_chunk)):

            @pl.when(pl.program_id(0) == j)
            def _():
                for s in range(8):
                    for y in range(2):
                        put_pieces([chunk], 0, acc[s * part : (s + 1) * part, y * tile // 2 : (y + 1) * tile // 2], core, y, s)

        pump()

    left = pl.BlockSpec(lhs.shape, lambda i: (0, 0), pipeline_mode=pl.Buffered(1))
    right = pl.BlockSpec((1, rows, tile), lambda i: (i, 0, 0))
    pltpu.emit_pipeline(body, grid=(2,), in_specs=[left, left, right, right])(lhs, lhs_far, rhs, rhs_far)


def wgrad_down(core, chunks, hid, hid_far, cot, cot_far, begin):
    _, parts, rows, units = hid.shape
    half_cols = cot.shape[1] // 2
    block = 2 * parts * units // 8

    def body(l, m, c, d):
        pump = begin()
        i = pl.program_id(0)
        acc = tn(l[0, 0], c[...]) + tn(m[0, 0], d[...])
        for side in range(2):
            for p in range(parts):

                @pl.when(i == side * parts + p)
                def _():
                    half = core if side else 1 - core
                    for j in range(units // 128):
                        unit = p * units + j * 128
                        s = 4 * half + unit // block
                        row = unit % block
                        for y in range(2):
                            cut = acc[j * 128 : (j + 1) * 128, y * half_cols // 2 : (y + 1) * half_cols // 2]
                            put_pieces(chunks, [row, block + row], cut, core, y, s)

        pump()

    mine = pl.BlockSpec((1, 1, rows, units), lambda i: (i // parts, i % parts, 0, 0))
    theirs = pl.BlockSpec((1, 1, rows, units), lambda i: (1 - i // parts, i % parts, 0, 0))
    right = pl.BlockSpec((rows, half_cols), lambda i: (0, core), pipeline_mode=pl.Buffered(1))
    pltpu.emit_pipeline(body, grid=(2 * parts,), in_specs=[mine, theirs, right, right])(hid, hid_far, cot, cot_far)


def feed(core, part, n2, cot, fg, fu, fd, hid, ups, acc, begin):
    rows, model = n2.shape
    parts, tile = hid.shape[1], hid.shape[3]
    block = rows // 2

    def body(n2_ref, cot_ref, fg_ref, fu_ref, fd_ref, hid_ref, gg_ref, gu_ref):
        pump = begin()
        for r in range(2):
            at = slice(r * block, (r + 1) * block)
            gate, up = nn(n2_ref[at, :], fg_ref[...]), nn(n2_ref[at, :], fu_ref[...])
            g = nt(cot_ref[at, :], fd_ref[...])
            act, slope = gelu_parts(gate)
            hid_ref[0, 0, at, :] = (act * up).astype(BF16)
            gg_ref[0, 0, at, :] = (g * up * slope).astype(BF16)
            gu_ref[0, 0, at, :] = (g * act).astype(BF16)
        total = nt(gg_ref[0, 0], fg_ref[...]) + nt(gu_ref[0, 0], fu_ref[...])
        if part == 0:

            @pl.when(pl.program_id(0) == 0)
            def _():
                acc[...] = total

            @pl.when(pl.program_id(0) > 0)
            def _():
                acc[...] += total

        else:
            acc[...] += total
        pump()

    unit = lambda i: ((1 - i) * (1 - core) + i * core) * parts + part
    flat = pl.BlockSpec((rows, model), lambda i: (0, 0), pipeline_mode=pl.Buffered(1))
    col = pl.BlockSpec((model, tile), lambda i: (0, unit(i)))
    out = pl.BlockSpec((1, 1, rows, tile), lambda i: (i, part, 0, 0))
    pltpu.emit_pipeline(
        body, grid=(2,), in_specs=[flat, flat, col, col, pl.BlockSpec((tile, model), lambda i: (unit(i), 0))], out_specs=[out, out, out]
    )(n2, cot, fg, fu, fd, hid, ups.at[0], ups.at[1])


def norm_back(core, gn, resid, cot, fgain, gres, low, gain_sum):
    rows, model = gn.shape
    tile = 128
    gain_sum[...] = jnp.zeros_like(gain_sum)

    def body(y_ref, c_ref, out_ref):
        g = fgain[...]

        def norm(i, total):
            at = pl.ds(pl.multiple_of(i * 16, 16), 16)
            place = pl.ds(pl.multiple_of(pl.program_id(0) * tile + i * 16, 16), 16)
            y, d = y_ref[at, :], gn[place, :]
            r = lax.rsqrt(jnp.mean(y * y, axis=-1, keepdims=True) + 1e-06)
            dg, yr = d * g, y * r
            dot = jnp.mean(dg * yr, axis=-1, keepdims=True)
            out = c_ref[at, :].astype(F32) + r * (dg - yr * dot)
            out_ref[at, :] = out
            low[place, :] = out.astype(BF16)
            add = d * yr
            return total + add[0:8] + add[8:16]

        total = lax.fori_loop(0, tile // 16, norm, jnp.zeros((8, model), F32))
        gain_sum[...] += jnp.sum(total, axis=0, keepdims=True)

    row = pl.BlockSpec((tile, model), lambda i: (i, 0))
    pltpu.emit_pipeline(body, grid=(rows // tile,), in_specs=[row, row], out_specs=[row])(resid, cot, gres)


def turn(core, seqs, length, low, ow, gate, state, rate, vec, ggate, lc, q, carry, gj, begin):
    rows, lru = gate.shape
    width = lru // 2

    def body(ow_ref, gate_ref, state_ref, rate_ref, vec_ref, gg_ref, lc_ref, q_ref):
        pump = begin()
        for s in range(seqs):
            gj[s, 0:length, :] = nt(low[s * length : (s + 1) * length, :], ow_ref[...])
        pump()
        slope = -8.0 * vec_ref[3:4, :]
        for s in range(seqs):

            def act(i, _):
                at = pl.ds(pl.multiple_of(s * length + i * 16, 16), 16)
                here = pl.ds(pl.multiple_of(i * 16, 16), 16)
                value, der = gelu_parts(gate_ref[at, :])
                d = gj[s, here, :]
                gg_ref[0, at, :] = (d * state_ref[at, :] * der).astype(BF16)
                gj[s, here, :] = d * value
                return 0

            lax.fori_loop(0, length // 16, act, 0)
            pump()

        row = lax.broadcasted_iota(jnp.int32, (8, width), 0)
        tiles = length // 8

        def scan(k, last):
            i = tiles - 1 - k
            out = []
            for s in range(seqs):
                at = pl.ds(pl.multiple_of(s * length + i * 8, 8), 8)
                g = gj[s, pl.ds(pl.multiple_of(i * 8, 8), 8), :]
                a = jnp.exp(rate_ref[at, :] * slope)
                b = a * g
                for d in (1, 2, 4):
                    keep = row < 8 - d
                    b = b + a * jnp.where(keep, pltpu.roll(b, 8 - d, 0), 0.0)
                    a = a * jnp.where(keep, pltpu.roll(a, 8 - d, 0), 1.0)
                ap, bp = last[s]
                b = b + a * bp
                a = a * ap
                lc_ref[at, :] = g + jnp.where(row < 7, pltpu.roll(b, 7, 0), bp)
                q_ref[at, :] = jnp.where(row < 7, pltpu.roll(a, 7, 0), ap)
                out.append((a[0:1], b[0:1]))
            return tuple(out)

        init = tuple((jnp.ones((1, width), F32), jnp.zeros((1, width), F32)) for _ in range(seqs))
        last = lax.fori_loop(0, tiles, scan, init)
        for s in range(seqs):
            carry[group(core), 0, s : s + 1, :] = last[s][0]
            carry[group(core), 1, s : s + 1, :] = last[s][1]
        pump()

    grp = lambda i: (1 - i) * (1 - core) + i * core
    col = lambda r: pl.BlockSpec((r, width), lambda i: (0, grp(i)))
    pltpu.emit_pipeline(
        body, grid=(2,),
        in_specs=[
            pl.BlockSpec((width, ow.shape[1]), lambda i: (grp(i), 0)), col(rows), col(rows), col(rows), col(8),
        ],
        out_specs=[pl.BlockSpec((1, rows, width), lambda i: (i, 0, 0)), col(rows), col(rows)],
    )(ow, gate, state, rate, vec, ggate, lc, q)


def gates_back(
    own, core, seqs, length, lc, q, cin, states, entry, rate, inlet, mixed, branch, edge, wr, wi, taps, vec,
    gb, head, tail, blocks, rate_sum, inlet_sum, sums_out, dr, di, gr, gi, gm, ext, begin,
):
    rows, lru = lc.shape
    width, bw_ = lru // 2, wr.shape[-1]
    per, sub = width // bw_, dr.shape[-1]

    def body(
        lc_ref, q_ref, state_ref, e_ref, rate_ref, inlet_ref, mixed_ref, branch_ref, edge_ref, wr_ref, wi_ref, taps_ref, vec_ref,
        gb_ref,
    ):
        pump = begin()
        mine = group(core)
        slope = -8.0 * vec_ref[3:4, :]
        zero = jnp.zeros((8, width), F32)
        row = lax.broadcasted_iota(jnp.int32, (16, width), 0)

        sums = (zero, zero, zero)
        for s in range(seqs):
            c_in, ent = cin[mine, s : s + 1, :], e_ref[s]

            def gates(i, carry):
                (before, t0, t1, t2) = carry
                at = pl.ds(pl.multiple_of(s * length + i * 16, 16), 16)
                state = state_ref[at, :]
                prev = jnp.where(row > 0, pltpu.roll(state, 1, 0), before)
                carried = lc_ref[at, :] + q_ref[at, :] * c_in
                rt, it, mx = rate_ref[at, :], inlet_ref[at, :], mixed_ref[at, :].astype(F32)
                log_decay = rt * slope
                decay = jnp.exp(log_decay)
                gap = drop(log_decay, decay)
                inv = lax.rsqrt(gap)
                nf = gap * inv
                im = it * mx
                g_log = carried * decay * (prev - im * decay * inv)
                cn = carried * nf
                g_rt = g_log * slope * (rt * (1.0 - rt))
                g_it = cn * im * (1.0 - it)
                gr[at, :] = g_rt.astype(BF16)
                gi[at, :] = g_it.astype(BF16)
                gm[s, pl.ds(pl.multiple_of(i * 16, 16), 16), :] = cn * it
                lr = g_log * rt
                return (state[15:16], t0 + lr[0:8] + lr[8:16], t1 + g_rt[0:8] + g_rt[8:16], t2 + g_it[0:8] + g_it[8:16])

            _, *sums = lax.fori_loop(0, length // 16, gates, (ent, *sums))
            pump()
        down = lambda v: jnp.sum(v, axis=0, keepdims=True)
        lanes = pl.ds(pl.multiple_of(mine * width, 128), width)
        sums_out[4:5, lanes] = down(sums[0]) * (-8.0 * vec_ref[4:5, :])
        sums_out[5:6, lanes] = down(sums[1])
        sums_out[6:7, lanes] = down(sums[2])

        for g in range(width // sub):
            cols = slice(g * sub, (g + 1) * sub)
            spread(dr, [wr_ref[g * 4 + a] for a in range(4)], 4, bw_)
            spread(di, [wi_ref[g * 4 + a] for a in range(4)], 4, bw_)
            back = nt(gr[:, cols], dr[...]) + nt(gi[:, cols], di[...])
            rs = tn(mixed_ref[:, cols], gr[:, cols])
            is_ = tn(mixed_ref[:, cols], gi[:, cols])
            for a in range(4):
                block = slice(a * bw_, (a + 1) * bw_)
                if own:
                    blocks[mine * per + g * 4 + a, :, 0:bw_] = rs[block, block].astype(BF16)
                    blocks[2 * per + mine * per + g * 4 + a, :, 0:bw_] = is_[block, block].astype(BF16)
                else:
                    rate_sum[mine * per + g * 4 + a] = rs[block, block]
                    inlet_sum[mine * per + g * 4 + a] = is_[block, block]
            for s in range(seqs):
                gm[s, 0:length, cols] += back[s * length : (s + 1) * length]
        pump()

        for s in range(seqs):
            gm[s, length : length + 8, :] = zero
            ext[s, 0:8, :] = edge_ref[16 * s : 16 * s + 16].astype(F32)[8:16]
            ext[s, 8 : 8 + length, :] = branch_ref[s * length : (s + 1) * length].astype(F32)
            head[mine, 8 * s : 8 * s + 8, :] = gm[s, 0:8, :]

        tap = [taps_ref[k : k + 1, :] for k in range(4)]
        acc = (zero,) * 5
        for s in range(seqs):

            def conv(i, acc):
                lo = pl.multiple_of(i * 16, 16)
                y = gm[s, pl.ds(lo, 24), :]
                x = ext[s, pl.ds(lo, 24), :]
                total = tap[0] * y[0:16]
                for k in range(1, 4):
                    total = total + tap[k] * y[k : k + 16]
                gb_ref[0, pl.ds(pl.multiple_of(s * length + i * 16, 16), 16), :] = total.astype(BF16)
                now = y[0:16]
                new = []
                for k in range(4):
                    prod = now * x[8 - k : 24 - k]
                    new.append(acc[k] + prod[0:8] + prod[8:16])
                new.append(acc[4] + now[0:8] + now[8:16])
                return tuple(new)

            acc = lax.fori_loop(0, length // 16, conv, acc)
            y = gm[s, length - 16 : length + 8, :]
            total = tap[0] * y[0:16]
            for k in range(1, 4):
                total = total + tap[k] * y[k : k + 16]
            tail[mine, 16 * s : 16 * s + 16, :] = total
            pump()
        for k in range(4):
            sums_out[k : k + 1, lanes] = down(acc[k])
        sums_out[7:8, lanes] = down(acc[4])

    grp = lambda i: (1 - i) * (1 - core) + i * core
    col = lambda r: pl.BlockSpec((r, width), lambda i: (0, grp(i)))
    blk = pl.BlockSpec((per, bw_, bw_), lambda i: (grp(i), 0, 0))
    pltpu.emit_pipeline(
        body, grid=(2,),
        in_specs=[
            col(rows), col(rows), col(rows), pl.BlockSpec((seqs, 1, width), lambda i: (0, 0, grp(i))),
            col(rows), col(rows), col(rows), col(rows), col(edge.shape[0]), blk, blk, col(4), col(8),
        ],
        out_specs=[pl.BlockSpec((1, rows, width), lambda i: (i, 0, 0))],
    )(lc, q, states, entry, rate, inlet, mixed, branch, edge, wr, wi, taps, vec, gb)


def spaced(exchange, name, steps):
    def begin():
        place = iter(range(64))

        def pump():
            j = next(place)
            for i in range(steps):
                if PLAN.get(f"{name}{i}{j}"):

                    @pl.when(pl.program_id(0) == i)
                    def _():
                        exchange.at(f"{name}{i}{j}")

        return pump

    return begin


def no_pump():
    return lambda: None


ANY = pl.BlockSpec(memory_space=pl.ANY)
INSIDE = pl.BlockSpec(memory_space=pltpu.VMEM)


KINDS = "AFEAFEAFEAFE"
PLAN = {
    "u000": [(-1, 0)],
    "u010": [(-1, 1)],
    "f200": [(0, 0), (0, 1)],
    "u100": [(-1, 2)],
    "u110": [(1, 0), (-1, 3), (1, 1)],
    "u200": [(-1, 4)],
    "d00": [(2, 0), (2, 1)],
    "d40": [(3, 0), (3, 1), (0, 2), (-1, 5)],
    "t00": [(4, 0), (4, 1), (0, 3), (-1, 6)],
    "t01": [(1, 2)],
    "t02": [(5, 0), (5, 1), (0, 4), (-1, 7)],
    "t12": [(2, 2)],
    "b1": [(3, 2), (1, 3), (0, 5), (-1, 8)],
    "b2": [(1, 4)],
    "g01": [(4, 2), (0, 6), (-1, 9)],
    "g02": [(2, 3), (2, 4)],
    "g03": [(5, 2), (0, 7)],
    "g10": [(1, 5)],
    "g11": [(3, 3), (3, 4)],
    "c1": [(-1, 10), (4, 3), (4, 4), (2, 5), (1, 6), (1, 7), (0, 8), (6, 0)],
    "c3": [(5, 3), (5, 4), (6, 1)],
    "c4": [(-1, 11), (3, 5)],
    "i00": [(2, 6), (2, 7), (0, 9)],
    "i10": [(4, 5)],
    "i30": [(5, 5)],
    "o00": [(3, 6), (3, 7), (1, 8), (6, 2)],
    "o10": [(7, 0)],
    "drain": [(4, 6), (4, 7), (0, 10), (7, 1), (5, 6), (5, 7), (6, 3), (2, 8), (0, 11), (1, 9), (7, 2), (3, 8), (6, 4), (6, 5), (4, 8), (1, 10), (7, 3), (6, 6), (2, 9), (5, 8), (6, 7), (1, 11), (7, 4), (3, 9), (6, 8), (2, 10), (4, 9), (5, 9), (2, 11), (3, 10), (6, 9), (3, 11), (4, 10), (6, 10), (5, 10), (4, 11), (5, 11)],
}

PARTS = [256] * 9 + [384] * 3
SWAPS = 10


def backward(own, seqs, length, seq_n, batch_n, grads_in, values, collective_id):
    (
        n2, resid, cot, fgain, ow, gate, state, entry, rate, vec, inlet, mixed, branch, edge, wr, wi, taps, gw, bw, tok, mgain,
        fg, fu, fd, joined, normed,
    ) = values
    rows, model = n2.shape
    lru, units = gate.shape[1], fd.shape[0]
    width, bw_ = lru // 2, wr.shape[-1]
    per, sub = width // bw_, 4 * bw_
    steps = [("batch", 1 << k) for k in range(batch_n.bit_length() - 1)] + [("seq", 1 << k) for k in range(seq_n.bit_length() - 1)]
    n_steps = len(steps)
    parts, unit = 3, units // 6
    if not own:
        grads_in = []

    def kernel(*refs):
        refs = list(refs)
        cut = lambda n: [refs.pop(0) for _ in range(n)]
        far_in = cut(len(grads_in))
        (
            n2, resid, cot, fgain, ow, gate, state, entry, rate, vec, inlet, mixed, branch, edge, wr, wi, taps, gw, bw, tok, mgain,
            fg, fu, fd, joined, normed,
        ) = cut(26)
        tokens_grad, block_out, totals, gres, low_out, low_far, ggate, ggate_far, lc, q, gb, gb_far, hid, hid_far, ups, ups_far, n2_far, joined_far = cut(18)
        fin, block_total = cut(2) if own else (None, None)
        rate_sum, inlet_sum = (None, None) if own else cut(2)
        low, carry, got, cin, dr, di, gr, gi, gm, ext, head, tail, ahead, fixed, gain_sum, acc, small, gn = cut(18)
        send, recv, swap_send, swap_recv, one, local, s_send, s_recv = cut(8)

        core = core_of()
        seq, bat = lax.axis_index("seq"), lax.axis_index("batch")
        other = (seq, bat + 1 - 2 * core)
        peers = [(flip(seq, bit), bat) if axis == "seq" else (seq, flip(bat, bit)) for axis, bit in steps]
        exchange, blocks = None, None
        if own:
            g0, g1, g2, *bufs, x_send, x_recv = cut(9)
            blocks, *block_bufs, b_send, b_recv = cut(8)
            places = [(ref, row) for row in (0, 256, 512) for ref in (g0, g1)] + [(g2, 0), (g2, 256), (g2, 512), (g0, 0), (g0, 384), (g1, 0)]
            chunks = [(ref, row, part, kind) for (ref, row), part, kind in zip(places, PARTS, KINDS)]
            exchange = Exchange(chunks, bufs, fin, x_send, x_recv)
            exchange.further[6] = BlockSums(blocks, block_bufs, block_total, b_send, b_recv).events()
            blocks[...] = jnp.zeros_like(blocks)
        small[0] = jnp.zeros((16, lru), F32)
        all_peers = [(lax.rem(seq + k, seq_n), bat) for k in range(1, seq_n)] + [peer for peer, step in zip(peers, steps) if step[0] == "batch"]
        greet(all_peers)

        def swap(j, src, dst):
            return pltpu.make_async_remote_copy(
                src_ref=src, dst_ref=dst, send_sem=swap_send.at[j], recv_sem=swap_recv.at[j], device_id=other, device_id_type=MESH
            )

        at = exchange.at if own else (lambda place: None)
        plan = lambda name, steps: spaced(exchange, name, steps) if own else no_pump
        run_feed = lambda p, begin: feed(core, p, n2, cot, fg, fu, fd, hid, ups, gn, begin)
        if own:
            cot_far, normed_far = far_in
            n2_swap, joined_swap = swap(4, n2, n2_far), swap(5, joined, joined_far)
            ups_swaps = [swap(6 + p, ups.at[:, 0, p], ups_far.at[:, p]) for p in range(parts)]
            hid_swap = swap(9, hid, hid_far)
            run_up = lambda p: wgrad_up(core, chunks[2 * p], chunks[2 * p + 1], n2, n2_far, ups.at[:, 1, p], ups_far.at[:, p], plan(f"u{p}", 2))

            def opening():
                def pump():
                    @pl.when(pl.program_id(0) == 0)
                    def _():
                        met(len(all_peers))
                        n2_swap.start()

                return pump

            run_feed(0, opening)
            ups_swaps[0].start()
            joined_swap.start()
            n2_swap.wait()
            ups_swaps[0].wait()
            run_up(0)
            run_feed(1, plan("f1", 2))
            ups_swaps[1].start()
            run_feed(2, plan("f2", 2))
            ups_swaps[2].start()
            hid_swap.start()
            ups_swaps[1].wait()
            run_up(1)
            ups_swaps[2].wait()
            run_up(2)
            joined_swap.wait()
            hid_swap.wait()
            wgrad_down(core, chunks[6:9], hid, hid_far, cot, cot_far, plan("d", 2 * parts))
        else:
            met(len(all_peers))
            for p in range(parts):
                run_feed(p, no_pump)
        norm_back(core, gn, resid, cot, fgain, gres, low, gain_sum)
        at("a4")
        keep = pltpu.make_async_copy(low, low_out, one)
        keep.start()
        low_swap = swap(0, low, low_far)
        low_swap.start()
        turn(
            core, seqs, length, low, ow, gate, state, rate, vec, ggate, lc, q, carry, gm,
            plan("t", 2),
        )
        gate_swap = swap(1, ggate.at[0], ggate_far)
        gate_swap.start()
        arriving = Entry(carry, got, seq_n, send, recv)
        arriving.start()
        keep.wait()
        low_swap.wait()
        if own:
            at("b0")
            exchange.free(0)
            exchange.free(2)
            wgrad(core, chunks[9:10], joined, joined_far, low_out, low_far, False)
            at("b1")
        arriving.finish(cin, True)
        gate_swap.wait()
        at("b2")
        gates_back(
            own, core, seqs, length, lc, q, cin, state, entry, rate, inlet, mixed, branch, edge, wr, wi, taps, vec,
            gb, head, tail, blocks, rate_sum, inlet_sum, small.at[0], dr, di, gr, gi, gm, ext,
            plan("g", 2),
        )

        to_left = pltpu.make_async_remote_copy(
            src_ref=head, dst_ref=ahead, send_sem=swap_send.at[2], recv_sem=swap_recv.at[2],
            device_id=(lax.rem(seq + seq_n - 1, seq_n), bat), device_id_type=MESH,
        )
        to_left.start()
        if own:
            at("c0")
            exchange.free(4)
            wgrad(core, chunks[10:11], normed, normed_far, ggate.at[1], ggate_far, True)
            at("c1")
        to_left.wait()
        weight = (seq < seq_n - 1).astype(F32)
        copies = []
        for i in range(2):
            mine = (1 - i) * (1 - core) + i * core
            for s in range(seqs):
                y = ahead[mine, 8 * s : 8 * s + 8, :] * weight
                t = tail[mine, 16 * s : 16 * s + 16, :]
                grown = jnp.concatenate([jnp.zeros((16, width), F32), y], axis=0)
                for k in range(1, 4):
                    t = t + taps[k : k + 1, pl.ds(pl.multiple_of(mine * width, 128), width)] * grown[k : k + 16]
                fixed[i, 16 * s : 16 * s + 16, :] = t.astype(BF16)
                copy = pltpu.make_async_copy(
                    fixed.at[i, 16 * s : 16 * s + 16], gb.at[i, (s + 1) * length - 16 : (s + 1) * length], local.at[i, s]
                )
                copy.start()
                copies.append(copy)
        for copy in copies:
            copy.wait()
        branch_swap = swap(3, gb.at[0], gb_far)
        branch_swap.start()
        at("c2")
        branch_swap.wait()
        at("c3")
        if own:
            exchange.free(1)
            exchange.free(3)
            wgrad(core, chunks[11:12], normed, normed_far, gb.at[1], gb_far, True)
            at("c4")

        begin = plan("i", 4)
        tile = 128
        acc[...] = jnp.zeros_like(acc)

        def input_grad(gg_ref, gb_ref, gwt, gwm, bwt, bwm, x_ref, gr_ref, out):
            pump = begin()
            d = nt(gg_ref[0], gwt[...]) + nt(gg_ref[1], gwm[...]) + nt(gb_ref[0], bwt[...]) + nt(gb_ref[1], bwm[...])
            x = x_ref[...].astype(F32)
            r = lax.rsqrt(jnp.mean(x * x, axis=-1, keepdims=True) + 1e-06)
            xr, dg = x * r, d * mgain[...]
            out[...] = gr_ref[...] + r * (dg - xr * jnp.mean(dg * xr, axis=-1, keepdims=True))
            acc[...] += jnp.sum(d * xr, axis=0, keepdims=True)
            pump()

        row = pl.BlockSpec((tile, model), lambda i: (i, 0))
        pair = pl.BlockSpec((2, tile, width), lambda i: (0, i, 0))
        side = lambda c: pl.BlockSpec((model, width), lambda i: (0, c), pipeline_mode=pl.Buffered(1))
        pltpu.emit_pipeline(
            input_grad, grid=(rows // tile,), in_specs=[pair, pair, side(1 - core), side(core), side(1 - core), side(core), row, row], out_specs=[row]
        )(ggate, gb, gw, gw, bw, bw, tok, gres, tokens_grad)

        small[0, 8:9, 0:model] = acc[...]
        small[0, 9:10, 0:model] = gain_sum[...]

        def small_step(k):
            return pltpu.make_async_remote_copy(
                src_ref=small.at[0], dst_ref=small.at[k + 1], send_sem=s_send.at[k], recv_sem=s_recv.at[k],
                device_id=peers[k], device_id_type=MESH,
            )

        def small_event(k):
            small_step(k).wait()
            small[0] = small[0] + small[k + 1]
            if k + 1 < n_steps:
                small_step(k + 1).start()

        small_events = [functools.partial(small_event, k) for k in range(n_steps)]
        small_step(0).start()
        if own:
            exchange.further[7] = small_events
        begin_out = plan("o", 4)
        tile_out = 256

        def last(r, *rest):
            pump = begin_out()
            hid_refs, down_refs, out = rest[: 2 * parts], rest[2 * parts : 4 * parts], rest[-1]
            total = r[...]
            for l, w in zip(hid_refs, down_refs):
                total = total + nn(l[0, 0], w[...])
            out[...] = total.astype(BF16)
            pump()

        col = pl.BlockSpec((rows, tile_out), lambda i: (0, i))
        order = [(side, p) for side in range(2) for p in range(parts)]
        hid_spec = lambda side, p: pl.BlockSpec((1, 1, rows, unit), lambda i: (side, p, 0, 0), pipeline_mode=pl.Buffered(1))
        down_spec = lambda half, p: pl.BlockSpec((unit, tile_out), lambda i: (half * parts + p, i))
        pltpu.emit_pipeline(
            last, grid=(model // tile_out,),
            in_specs=[col] + [hid_spec(*o) for o in order] + [down_spec(core if side else 1 - core, p) for side, p in order], out_specs=[col],
        )(resid, *([hid] * 2 * parts), *([fd] * 2 * parts), block_out)
        if own:
            exchange.drain()
        else:
            for event in small_events:
                event()
        totals[...] = small[0]

    f = lambda *shape: jax.ShapeDtypeStruct(shape, F32)
    b = lambda *shape: jax.ShapeDtypeStruct(shape, BF16)
    vm, dma = pltpu.VMEM, lambda *shape: pltpu.SemaphoreType.DMA(shape)
    out_shape = [
        f(rows, model), b(rows, model), f(16, lru),
        f(rows, model), b(rows, model), b(rows, model), b(2, rows, width), b(rows, width), f(rows, lru), f(rows, lru), b(2, rows, width), b(rows, width),
        b(2, parts, rows, unit), b(2, parts, rows, unit), b(2, 2, parts, rows, unit), b(2, parts, rows, unit), b(rows, model), b(rows, lru),
    ]
    out_specs = [ANY, ANY, INSIDE] + [ANY] * 15
    scratch = [
        vm((rows, model), BF16), vm((2, 2, seqs, width), F32), vm((seq_n, 2, 2, seqs, width), F32), vm((2, seqs, width), F32),
        vm((sub, sub), BF16), vm((sub, sub), BF16), vm((rows, width), BF16), vm((rows, width), BF16),
        vm((seqs, length + 8, width), F32), vm((seqs, length + 8, width), F32), vm((2, 8 * seqs, width), F32), vm((2, 16 * seqs, width), F32),
        vm((2, 8 * seqs, width), F32), vm((2, 16 * seqs, width), BF16), vm((1, model), F32), vm((1, model), F32), vm((n_steps + 1, 16, lru), F32), vm((rows, model), F32),
        dma(seq_n), dma(seq_n), dma(SWAPS), dma(SWAPS), pltpu.SemaphoreType.DMA, dma(2, seqs), dma(n_steps), dma(n_steps),
    ]
    if own:
        out_shape += [b(2, 2, sum(PARTS), 128), b(4 * per, bw_, 128)]
        out_specs += [INSIDE, INSIDE]
        scratch += [vm((16, 768, 128), BF16)] * 3 + Exchange.scratch(len(PARTS), sum(PARTS))
        scratch += [vm((4 * per, bw_, 128), BF16)] + BlockSums.scratch(bw_)
    else:
        out_shape += [f(*wr.shape), f(*wi.shape)]
        out_specs += [INSIDE, INSIDE]
    ins = [ANY] * (len(grads_in) + len(values))
    for j in (3, 16, 20):
        ins[len(grads_in) + j] = INSIDE
    return pl.pallas_call(
        kernel,
        in_specs=ins,
        out_specs=out_specs,
        out_shape=out_shape,
        scratch_shapes=scratch,
        compiler_params=pltpu.CompilerParams(collective_id=collective_id, has_side_effects=True, vmem_limit_bytes=60 * 2**20),
        name="backward",
    )(*grads_in, *values)


def lay(sums, totals, blocks, model, lru, units, n):
    shapes = [(model // n, units), (model // n, units), (units // n, model), (lru // n, model), (model // n, lru), (model // n, lru)]
    rows = sums.shape[2]
    count, wide_b = blocks.shape[0] // 2, blocks.shape[1]

    def kernel(v, b, s, rate, inlet, taps, decay, rate_off, inlet_off, conv_off, gain1, gain2, *outs):
        taps[...] = s[0:4, :]
        for j, vector in enumerate((decay, rate_off, inlet_off, conv_off)):
            vector[...] = s[4 + j, :]
        gain1[...] = s[8, 0:model]
        gain2[...] = s[9, 0:model]
        for y in range(2):
            for m, out in enumerate(outs):
                part, wide = out.shape
                for t in range(wide // 256):
                    if m < 2:
                        at, col = t // 2 * 512 + m * 256 + t % 2 * 128, t // 2 * 512 + y * 256 + t % 2 * 128
                    else:
                        at, col = 1536 + [0, 768, 1152, 1536][m - 2] + t * part, y * wide // 2 + t * 128
                    out[:, col : col + 128] = v[0, y, at : at + part, :].astype(F32)
        for j in range(count // 2):
            rate[j] = b[0, j, :, 0:wide_b].astype(F32)
            inlet[j] = b[1, j, :, 0:wide_b].astype(F32)

    block = pl.BlockSpec((count // 2, wide_b, wide_b), lambda i: (i, 0, 0))
    flat = lambda size: (pl.BlockSpec((size,), lambda i: (0,)), jax.ShapeDtypeStruct((size,), F32))
    vectors = [(whole((4, lru)), jax.ShapeDtypeStruct((4, lru), F32))] + [flat(lru)] * 4 + [flat(model)] * 2
    return pl.pallas_call(
        kernel,
        grid=(2,),
        in_specs=[pl.BlockSpec((1, 2, rows, 128), lambda i: (i, 0, 0, 0)), pl.BlockSpec((2, count // 2, wide_b, 128), lambda i: (0, i, 0, 0)), whole(totals.shape)],
        out_specs=[block, block] + [v[0] for v in vectors] + [pl.BlockSpec((part, wide // 2), lambda i: (0, i)) for part, wide in shapes],
        out_shape=[jax.ShapeDtypeStruct((count, wide_b, wide_b), F32)] * 2 + [v[1] for v in vectors] + [jax.ShapeDtypeStruct(shape, F32) for shape in shapes],
        compiler_params=params(),
        name="lay",
    )(sums, blocks.reshape(2, count, wide_b, 128), totals)


def swap(value):
    count = lax.axis_size("batch")
    return lax.ppermute(value, "batch", [(i, i ^ 1) for i in range(count)])


def local(
    tokens, cotangent, gate_weight, branch_weight, out_weight, conv_taps, conv_offset, rate_weight, inlet_weight,
    rate_offset, inlet_offset, decay_param, mixer_gain, feed_gain, feed_gate, feed_up, feed_down,
):
    seqs, length, model = tokens.shape
    lru, units = gate_weight.shape[1], feed_gate.shape[1]
    rows = seqs * length
    seq_n, batch_n = lax.axis_size("seq"), lax.axis_size("batch")
    core = lax.rem(lax.axis_index("batch"), 2)

    tok, cot = tokens.reshape(rows, model), cotangent.reshape(rows, model)
    cot_far = swap(cot)
    none = jnp.zeros_like(conv_offset)
    vec = jnp.stack(
        [conv_offset, rate_offset, inlet_offset, jax.nn.softplus(decay_param), jax.nn.sigmoid(decay_param), none, none, none]
    )
    gain1, gain2 = mixer_gain[None], feed_gain[None]

    normed, gate, branch, edge, mixed, rate, inlet, h, p, entry = front(
        tok, gain1, gate_weight, branch_weight, conv_taps, vec, rate_weight, inlet_weight, seqs, length, seq_n, 0
    )
    normed_far = swap(normed)
    joined, resid, normed_two, state = join(tok, gate, h, p, entry, out_weight, gain2, seqs, length)

    own = (seq_n, batch_n) == (8, 4)
    tokens_grad, out, totals, _, grad_low, _, ggate, _, _, _, gb, _, hid, _, ups, _, _, _, *sums = backward(
        own, seqs, length, seq_n, batch_n, [cot_far, normed_far],
        [
            normed_two, resid, cot, gain2, out_weight, gate, state, entry, rate, vec, inlet, mixed, branch, edge,
            rate_weight, inlet_weight, conv_taps, gate_weight, branch_weight, tok, gain1, feed_gate, feed_up, feed_down, joined, normed,
        ],
        1,
    )
    if own:
        rate_all, inlet_all, *vectors = lay(sums[0], totals, sums[1], model, lru, units, seq_n)
        vectors, (gate_feed_all, up_feed_all, down_all, out_all, gate_all, branch_all) = vectors[:7], vectors[7:]
    else:
        vectors = [totals[0:4], *totals[4:8], totals[8, :model], totals[9, :model]]
        rate_all, inlet_all = lax.psum((sums[0], sums[1]), ("seq", "batch"))

        def full(pair):
            pair = pair if pair.ndim == 4 else pair[:, None]
            pair = jnp.where(core == 0, pair[::-1], pair)
            return pair.transpose(2, 0, 1, 3).reshape(rows, -1)

        def total(left, right):
            return lax.psum(lax.psum_scatter(tn(left, right), "seq", scatter_dimension=0, tiled=True), "batch")

        down_all = total(full(hid), cot)
        gate_feed_all, up_feed_all = total(normed_two, full(ups[0])), total(normed_two, full(ups[1]))
        out_all = total(joined, grad_low)
        gate_all, branch_all = total(normed, full(ggate)), total(normed, full(gb))

    return (
        out.reshape(seqs, length, model), tokens_grad.reshape(seqs, length, model), gate_all, branch_all, out_all,
        vectors[0], vectors[4], rate_all, inlet_all, vectors[2], vectors[3], vectors[1], vectors[5], vectors[6],
        gate_feed_all, up_feed_all, down_all,
    )


def solution(mesh):
    big = P("batch", "seq", None)
    in_specs = (big, big) + (P(),) * 15
    out_specs = (big, big) + (P("seq", None),) * 3 + (P(),) * 9 + (P("seq", None),) * 3
    return jax.shard_map(local, mesh=mesh, in_specs=in_specs, out_specs=out_specs, check_vma=False)
```

```python
import functools
import jax
import jax.numpy as jnp
from jax import lax
from jax.experimental import pallas as pl
from jax.experimental.pallas import tpu as pltpu
from jax.sharding import PartitionSpec as P

F32, BF16 = jnp.float32, jnp.bfloat16
VLIM = 56 * 2**20
GELU_A, GELU_B = 0.7978845608028654, 0.044715


def nn(a, b):
    return lax.dot_general(a, b, (((1,), (0,)), ((), ())), preferred_element_type=F32)


def nt(a, b):
    return lax.dot_general(a, b, (((1,), (1,)), ((), ())), preferred_element_type=F32)


def tn(a, b):
    return lax.dot_general(a, b, (((0,), (0,)), ((), ())), preferred_element_type=F32)


def sigmoid(v):
    return 1.0 / (1.0 + jnp.exp(-v))


def drop(u, decay):
    v = 2.0 * u
    series = 1.0 + v * (1.0 / 7.0)
    for k in (6.0, 5.0, 4.0, 3.0, 2.0):
        series = 1.0 + (v * (1.0 / k)) * series
    return jnp.where(v > -0.35, -v * series, 1.0 - decay * decay)


def gelu_parts(v):
    square = v * v
    inner = jnp.tanh(GELU_A * v * (1.0 + GELU_B * square))
    half = 0.5 + 0.5 * inner
    act = v * half
    slope = half + 0.5 * v * (1.0 - inner * inner) * (GELU_A + 3.0 * GELU_A * GELU_B * square)
    return act, slope


def gelu(v):
    inner = jnp.tanh(GELU_A * v * (1.0 + GELU_B * (v * v)))
    return v * (0.5 + 0.5 * inner)


def spread(dense, blocks, count, width):
    for a in range(count):
        parts = []
        if a > 0:
            parts.append(jnp.zeros((width, a * width), dense.dtype))
        parts.append(blocks[a])
        if a < count - 1:
            parts.append(jnp.zeros((width, (count - 1 - a) * width), dense.dtype))
        dense[a * width : (a + 1) * width, :] = jnp.concatenate(parts, axis=1)


def params(sem=("arbitrary",), **kw):
    return pltpu.CompilerParams(dimension_semantics=sem, vmem_limit_bytes=VLIM, **kw)


def whole(shape):
    return pl.BlockSpec(shape, lambda *_: (0,) * len(shape))


MESH = pl.DeviceIdType.MESH


def greet(peers):
    barrier = pltpu.get_barrier_semaphore()
    for peer in peers:
        pl.semaphore_signal(barrier, inc=1, device_id=peer, device_id_type=MESH)


def met(count):
    pl.semaphore_wait(pltpu.get_barrier_semaphore(), count)


def flip(index, bit):
    return index + bit - 2 * bit * (lax.rem(index // bit, 2))


class Entry:
    def __init__(self, part, got, n, send, recv):
        self.part, self.got, self.n = part, got, n
        self.me = lax.axis_index("seq")
        self.copies = [
            pltpu.make_async_remote_copy(
                src_ref=part, dst_ref=got.at[self.me], send_sem=send.at[k], recv_sem=recv.at[k],
                device_id=(lax.rem(self.me + k, n), lax.axis_index("batch")), device_id_type=MESH,
            )
            for k in range(1, n)
        ]

    def start(self):
        for copy in self.copies:
            copy.start()
        self.got[self.me] = self.part[...]

    def finish(self, out, reverse):
        for copy in self.copies:
            copy.wait()

        def one(k, state):
            j = self.n - 1 - k if reverse else k
            before = (j > self.me) if reverse else (j < self.me)
            return jnp.where(before, self.got[j, :, 0] * state + self.got[j, :, 1], state)

        out[...] = lax.fori_loop(0, self.n, one, jnp.zeros(out.shape, F32))


def front_kernel(
    seqs, length, seq_n, tok, gain, gw, bw, taps, vec, wr, wi,
    normed, gate, branch, edge, mixed, rate, inlet, h, p, entry,
    halo, hn, ext, dr, di, rp, ip, carry, got, state, h_send, h_recv, send, recv,
):
    rows, width = seqs * length, gw.shape[1]
    sub = dr.shape[-1]

    seq, bat = lax.axis_index("seq"), lax.axis_index("batch")

    copies = [
        pltpu.make_async_remote_copy(
            src_ref=tok.at[(s + 1) * length - 16 : (s + 1) * length], dst_ref=halo.at[s], send_sem=h_send.at[s], recv_sem=h_recv.at[s],
            device_id=(lax.rem(seq + 1, seq_n), bat), device_id_type=MESH,
        )
        for s in range(seqs)
    ]

    @pl.when(pl.program_id(0) == 0)
    def _():
        greet([(lax.rem(seq + k, seq_n), bat) for k in range(1, seq_n)])

        def norm(i, _):
            x = tok[pl.ds(i * 32, 32), :].astype(F32)
            r = lax.rsqrt(jnp.mean(x * x, axis=-1, keepdims=True) + 1e-06)
            normed[pl.ds(i * 32, 32), :] = (x * r * gain[...]).astype(BF16)
            return 0

        lax.fori_loop(0, rows // 32, norm, 0)
        met(seq_n - 1)
        for copy in copies:
            copy.start()

    gate[...] = nn(normed[...], gw[...])
    b16 = nn(normed[...], bw[...]).astype(BF16)

    @pl.when(pl.program_id(0) == 0)
    def _():
        for s in range(seqs):
            copies[s].wait()
            x = halo[s].astype(F32)
            r = lax.rsqrt(jnp.mean(x * x, axis=-1, keepdims=True) + 1e-06)
            hn[16 * s : 16 * s + 16, :] = (x * r * gain[...]).astype(BF16)

    e16 = (nn(hn[...], bw[...]) * (seq > 0).astype(F32)).astype(BF16)
    branch[...] = b16
    edge[...] = e16
    e32 = e16.astype(F32)
    for s in range(seqs):
        ext[s, 0:8, :] = e32[16 * s + 8 : 16 * s + 16]
        ext[s, 8 : 8 + length, :] = b16[length * s : length * (s + 1)].astype(F32)

    tap = [taps[k : k + 1, :] for k in range(4)]
    off = vec[0:1, :]
    for s in range(seqs):

        def conv(i, _):
            x = ext[s, pl.ds(pl.multiple_of(i * 32, 32), 40), :]
            total = off + tap[0] * x[8:40]
            for k in range(1, 4):
                total = total + tap[k] * x[8 - k : 40 - k]
            mixed[pl.ds(pl.multiple_of(s * length + i * 32, 32), 32), :] = total.astype(BF16)
            return 0

        lax.fori_loop(0, length // 32, conv, 0)

    for g in range(width // sub):
        cols = slice(g * sub, (g + 1) * sub)
        spread(dr.at[g], [wr[g * 4 + a] for a in range(4)], 4, wr.shape[-1])
        spread(di.at[g], [wi[g * 4 + a] for a in range(4)], 4, wi.shape[-1])
        rp[:, cols] = nn(mixed[:, cols], dr[g])
        ip[:, cols] = nn(mixed[:, cols], di[g])

    ro, io, slope = vec[1:2, :], vec[2:3, :], -8.0 * vec[3:4, :]

    def gates(i, _):
        at = pl.ds(pl.multiple_of(i * 32, 32), 32)
        rt = sigmoid(rp[at, :] + ro)
        it = sigmoid(ip[at, :] + io)
        log_decay = rt * slope
        decay = jnp.exp(log_decay)
        rate[at, :] = rt
        inlet[at, :] = it
        p[at, :] = decay
        h[at, :] = jnp.sqrt(drop(log_decay, decay)) * it * mixed[at, :].astype(F32)
        return 0

    lax.fori_loop(0, rows // 32, gates, 0)

    row = lax.broadcasted_iota(jnp.int32, (8, width), 0)

    def scan(i, last):
        out = []
        for s in range(seqs):
            at = pl.ds(pl.multiple_of(s * length + i * 8, 8), 8)
            a, b = p[at, :], h[at, :]
            for d in (1, 2, 4):
                keep = row >= d
                b = b + a * jnp.where(keep, pltpu.roll(b, d, 0), 0.0)
                a = a * jnp.where(keep, pltpu.roll(a, d, 0), 1.0)
            ap, bp = last[s]
            b = b + a * bp
            a = a * ap
            p[at, :] = a
            h[at, :] = b
            out.append((a[7:8], b[7:8]))
        return tuple(out)

    init = tuple((jnp.ones((1, width), F32), jnp.zeros((1, width), F32)) for _ in range(seqs))
    last = lax.fori_loop(0, length // 8, scan, init)
    for s in range(seqs):
        carry[pl.program_id(0), 0, s : s + 1, :] = last[s][0]
        carry[pl.program_id(0), 1, s : s + 1, :] = last[s][1]

    @pl.when(pl.program_id(0) == 1)
    def _():
        arriving = Entry(carry, got, seq_n, send, recv)
        arriving.start()
        arriving.finish(state, False)
        for g in range(2):
            for s in range(seqs):
                entry[s, :, g * width : (g + 1) * width] = state[g, s : s + 1, :]


def front(tok, gain, gw, bw, taps, vec, wr, wi, seqs, length, seq_n, collective_id):
    rows, model = tok.shape
    lru, bw_ = gw.shape[1], wr.shape[-1]
    width, sub, per = lru // 2, 4 * bw_, lru // 2 // bw_
    col = lambda r: pl.BlockSpec((r, width), lambda j: (0, j))
    blk = pl.BlockSpec((per, bw_, bw_), lambda j: (j, 0, 0))
    f = lambda dt: jax.ShapeDtypeStruct((rows, lru), dt)
    vm, dma = pltpu.VMEM, lambda n: pltpu.SemaphoreType.DMA((n,))
    return pl.pallas_call(
        functools.partial(front_kernel, seqs, length, seq_n),
        grid=(2,),
        in_specs=[
            whole((rows, model)), whole((1, model)),
            pl.BlockSpec((model, width), lambda j: (0, j)), pl.BlockSpec((model, width), lambda j: (0, j)), col(4), col(8), blk, blk,
        ],
        out_specs=[
            whole((rows, model)), col(rows), col(rows), col(16 * seqs), col(rows), col(rows), col(rows), col(rows), col(rows),
            whole((seqs, 1, lru)),
        ],
        out_shape=[
            jax.ShapeDtypeStruct((rows, model), BF16), f(F32), f(BF16),
            jax.ShapeDtypeStruct((16 * seqs, lru), BF16), f(BF16), f(F32), f(F32), f(F32), f(F32),
            jax.ShapeDtypeStruct((seqs, 1, lru), F32),
        ],
        scratch_shapes=[
            vm((seqs, 16, model), BF16), vm((16 * seqs, model), BF16), vm((seqs, 8 + length, width), F32),
            vm((2, sub, sub), BF16), vm((2, sub, sub), BF16), vm((rows, width), F32), vm((rows, width), F32),
            vm((2, 2, seqs, width), F32), vm((seq_n, 2, 2, seqs, width), F32), vm((2, seqs, width), F32),
            dma(seqs), dma(seqs), dma(seq_n), dma(seq_n),
        ],
        compiler_params=params(collective_id=collective_id, has_side_effects=True),
        name="front",
    )(tok, gain, gw, bw, taps, vec, wr, wi)


def join_kernel(tok, gate, h, p, entry, ow, gain, joined, resid, normed, state_ref):
    rows = tok.shape[0]
    ent = entry[0]

    def join(i, _):
        at = pl.ds(pl.multiple_of(i * 16, 16), 16)
        state = h[at, :] + p[at, :] * ent
        state_ref[at, :] = state
        joined[at, :] = (gelu(gate[at, :]) * state).astype(BF16)
        return 0

    lax.fori_loop(0, rows // 16, join, 0)
    resid[...] = nn(joined[...], ow[...])

    def norm(i, _):
        at = pl.ds(pl.multiple_of(i * 32, 32), 32)
        y = tok[at, :].astype(F32) + resid[at, :]
        resid[at, :] = y
        r = lax.rsqrt(jnp.mean(y * y, axis=-1, keepdims=True) + 1e-06)
        normed[at, :] = (y * r * gain[...]).astype(BF16)
        return 0

    lax.fori_loop(0, rows // 32, norm, 0)


def join(tok, gate, h, p, entry, ow, gain, seqs, length):
    rows, model = tok.shape
    lru = gate.shape[1]
    tile = 128
    per = length // tile
    row = lambda w: pl.BlockSpec((tile, w), lambda i: (i, 0))
    return pl.pallas_call(
        join_kernel,
        grid=(rows // tile,),
        in_specs=[row(model), row(lru), row(lru), row(lru), pl.BlockSpec((1, 1, lru), lambda i: (i // per, 0, 0)), whole((lru, model)), whole((1, model))],
        out_specs=[row(lru), row(model), row(model), row(lru)],
        out_shape=[jax.ShapeDtypeStruct((rows, lru), BF16), jax.ShapeDtypeStruct((rows, model), F32), jax.ShapeDtypeStruct((rows, model), BF16), jax.ShapeDtypeStruct((rows, lru), F32)],
        compiler_params=params(),
        name="join",
    )(tok, gate, h, p, entry, ow, gain)


ORDERS = {"A": ("xhyl", "yxhl"), "E": ("xlhy", "yxlh"), "F": ("xylh", "yxlh")}


class Exchange:
    def __init__(self, chunks, bufs, fin, send, recv):
        self.chunks, self.bufs, self.fin, self.sems = chunks, bufs, fin, (send, recv)
        self.first = [sum(c[2] for c in chunks[:q]) for q in range(len(chunks))]
        seq, bat = lax.axis_index("seq"), lax.axis_index("batch")
        core, y = lax.rem(bat, 2), bat // 2
        x, low, high = lax.rem(seq, 2), lax.rem(seq // 2, 2), seq // 4
        bit = {"x": x, "y": y, "l": low, "h": high}
        move = {"x": (1 - 2 * x, 0), "y": (0, 2 - 4 * y), "l": (2 - 4 * low, 0), "h": (4 - 8 * high, 0)}
        pick = lambda a, b: a if a is b else (1 - core) * a + core * b
        self.core, self.y = core, y
        self.other, self.across = (seq, bat + 1 - 2 * core), (seq, bat + 2 - 4 * y)
        self.bits, self.peers = {}, {}
        for kind, (first, second) in ORDERS.items():
            self.bits[kind] = [pick(bit[a], bit[b]) for a, b in zip(first, second)]
            self.peers[kind] = [
                (seq + pick(move[a][0], move[b][0]), bat + pick(move[a][1], move[b][1])) for a, b in zip(first, second)
            ] + [self.across, self.other]
        self.greet = [(seq + move[a][0], bat) for a in "xlh"] + [self.across, self.other]
        self.freed, self.further = set(), {}

    def at(self, place):
        for k, q in PLAN.get(place, ()):
            self.step(k, q)

    def free(self, q):
        self.copy(0, q).wait_send()
        self.freed.add(q)

    def drain(self):
        self.at("drain")
        for q in range(len(self.chunks)):
            for k in range(4):
                if k > 0 or q not in self.freed:
                    self.copy(k, q).wait_send()

    def copy(self, k, q):
        grad, row, part, kind = self.chunks[q]
        size, bits = 8 >> k, self.bits[kind]
        at = slice(self.first[q], self.first[q] + part)
        if k == 0:
            src, dst = grad.at[pl.ds((1 - bits[0]) * 8, 8), row : row + part], self.bufs[0].at[:, at]
        elif k < 4:
            src, dst = self.bufs[k - 1].at[pl.ds((1 - bits[k]) * size, size), at], self.bufs[k].at[:, at]
        elif k == 4:
            src = dst = self.fin.at[self.core, self.y, at]
        else:
            src = dst = self.fin.at[self.core, :, at]
        return pltpu.make_async_remote_copy(
            src_ref=src, dst_ref=dst, send_sem=self.sems[0].at[k, q], recv_sem=self.sems[1].at[k, q],
            device_id=self.peers[kind][k], device_id_type=MESH,
        )

    def add(self, k, q, base, size):
        grad, row, part, kind = self.chunks[q]
        dst, bits = self.bufs[k], self.bits[kind]
        for j in range(size):

            def body(i, _):
                a = pl.ds(pl.multiple_of(self.first[q] + i * 128, 128), 128)
                if k == 0:
                    own = grad[bits[0] * 8 + base + j, pl.ds(pl.multiple_of(row + i * 128, 128), 128), :]
                else:
                    own = self.bufs[k - 1][bits[k] * (8 >> k) + base + j, a, :]
                dst[base + j, a, :] = dst[base + j, a, :] + own
                return 0

            lax.fori_loop(0, part // 128, body, 0)

    def step(self, k, q):
        if k > 5:
            self.further[k][q]()
        elif k < 0:
            self.copy(0, q).start()
        elif k < 3:
            half, bits = 4 >> k, self.bits[self.chunks[q][3]]
            self.copy(k, q).wait_recv()
            self.add(k, q, (1 - bits[k + 1]) * half, half)
            self.copy(k + 1, q).start()
            self.add(k, q, bits[k + 1] * half, half)
        elif k == 3:
            bits = self.bits[self.chunks[q][3]]
            self.copy(3, q).wait_recv()

            def body(i, _):
                a = pl.ds(pl.multiple_of(self.first[q] + i * 128, 128), 128)
                self.fin[self.core, self.y, a, :] = self.bufs[3][0, a, :] + self.bufs[2][bits[3], a, :]
                return 0

            lax.fori_loop(0, self.chunks[q][2] // 128, body, 0)
            self.copy(4, q).start()
        elif k == 4:
            self.copy(4, q).wait()
            self.copy(5, q).start()
        else:
            self.copy(5, q).wait()

    @staticmethod
    def scratch(chunks, rows):
        return [pltpu.VMEM((8 >> k, rows, 128), BF16) for k in range(4)] + [pltpu.SemaphoreType.DMA((6, chunks))] * 2


class BlockSums:
    def __init__(self, value, bufs, out, send, recv):
        self.value, self.bufs, self.out, self.sems = value, bufs, out, (send, recv)
        seq, bat = lax.axis_index("seq"), lax.axis_index("batch")
        core, y = lax.rem(bat, 2), bat // 2
        x, low, high = lax.rem(seq, 2), lax.rem(seq // 2, 2), seq // 4
        self.bits = [core, low, high, x, y]
        self.peers = [(seq, bat + 1 - 2 * core), (seq + 2 - 4 * low, bat), (seq + 4 - 8 * high, bat), (seq + 1 - 2 * x, bat), (seq, bat + 2 - 4 * y)]
        self.base = [0]
        for k in range(5):
            self.base.append(self.base[-1] + self.bits[k] * (16 >> k))

    def halve(self, k):
        size = 16 >> k
        return pltpu.make_async_remote_copy(
            src_ref=self.value.at[pl.ds(self.base[k] + (1 - self.bits[k]) * size, size)], dst_ref=self.bufs[k],
            send_sem=self.sems[0].at[k], recv_sem=self.sems[1].at[k], device_id=self.peers[k], device_id_type=MESH,
        )

    def hand(self, k):
        at = pl.ds(self.base[k + 1], 16 >> k)
        return pltpu.make_async_remote_copy(
            src_ref=self.out.at[at], dst_ref=self.out.at[at],
            send_sem=self.sems[0].at[5 + k], recv_sem=self.sems[1].at[5 + k], device_id=self.peers[k], device_id_type=MESH,
        )

    def events(self):
        def took(k):
            size = 16 >> k
            self.halve(k).wait()

            def body(j, _):
                at = self.base[k + 1] + j
                total = (self.value[at].astype(F32) + self.bufs[k][j].astype(F32)).astype(BF16)
                if k < 4:
                    self.value[at] = total
                else:
                    self.out[at] = total
                return 0

            lax.fori_loop(0, size, body, 0)
            if k < 4:
                self.halve(k + 1).start()
            else:
                self.hand(4).start()

        def got(k):
            self.hand(k).wait()
            if k > 0:
                self.hand(k - 1).start()

        first = [lambda: self.halve(0).start()]
        return first + [functools.partial(took, k) for k in range(5)] + [functools.partial(got, k) for k in range(4, -1, -1)]

    @staticmethod
    def scratch(width):
        return [pltpu.VMEM((16 >> k, width, 128), BF16) for k in range(5)] + [pltpu.SemaphoreType.DMA((10,))] * 2


def core_of():
    return lax.rem(lax.axis_index("batch"), 2)


def group(core):
    i = pl.program_id(0)
    return (1 - i) * (1 - core) + i * core


def put_pieces(chunks, row, acc, core, y, s):
    part, cols = acc.shape
    for t in range(cols // 128):
        at = row[t] if isinstance(row, (list, tuple)) else row + t * part
        base = 0
        for ref, first, rows, kind in chunks:
            low, high = max(at, base), min(at + part, base + rows)
            if low < high:
                ref[place_of(core, s, y, kind), first + low - base : first + high - base, :] = acc[
                    low - at : high - at, t * 128 : (t + 1) * 128
                ].astype(BF16)
            base += rows


def place_of(core, s, y, kind):
    bit = {"x": s % 2, "l": (s // 2) % 2, "h": s // 4, "y": y}
    place = lambda order: sum(bit[a] * (8 >> k) for k, a in enumerate(order))
    first, second = ORDERS[kind]
    return place(first) if first == second else (1 - core) * place(first) + core * place(second)


def wgrad(core, chunks, lhs, lhs_far, rhs, rhs_far, own_columns):
    rows, deep = lhs.shape
    tile = rhs.shape[1] // (2 if own_columns else 4)
    base, part = 0 if own_columns else 2 * core, deep // 8

    def body(a, b, c, d):
        acc = tn(a[...], c[...]) + tn(b[...], d[...])
        for s in range(8):
            put_pieces(chunks, 0, acc[s * part : (s + 1) * part], core, pl.program_id(0), s)

    left = pl.BlockSpec(lhs.shape, lambda y: (0, 0), pipeline_mode=pl.Buffered(1))
    right = pl.BlockSpec((rows, tile), lambda y: (0, base + y))
    pltpu.emit_pipeline(body, grid=(2,), in_specs=[left, left, right, right])(lhs, lhs_far, rhs, rhs_far)


def wgrad_up(core, gate_chunk, up_chunk, lhs, lhs_far, rhs, rhs_far, begin):
    rows, deep = lhs.shape
    tile, part = rhs.shape[2], deep // 8

    def body(a, b, c, d):
        pump = begin()
        acc = tn(a[...], c[0]) + tn(b[...], d[0])
        for j, chunk in enumerate((gate_chunk, up_chunk)):

            @pl.when(pl.program_id(0) == j)
            def _():
                for s in range(8):
                    for y in range(2):
                        put_pieces([chunk], 0, acc[s * part : (s + 1) * part, y * tile // 2 : (y + 1) * tile // 2], core, y, s)

        pump()

    left = pl.BlockSpec(lhs.shape, lambda i: (0, 0), pipeline_mode=pl.Buffered(1))
    right = pl.BlockSpec((1, rows, tile), lambda i: (i, 0, 0))
    pltpu.emit_pipeline(body, grid=(2,), in_specs=[left, left, right, right])(lhs, lhs_far, rhs, rhs_far)


def wgrad_down(core, chunks, hid, hid_far, cot, cot_far, begin):
    _, parts, rows, units = hid.shape
    half_cols = cot.shape[1] // 2
    block = 2 * parts * units // 8

    def body(l, m, c, d):
        pump = begin()
        i = pl.program_id(0)
        acc = tn(l[0, 0], c[...]) + tn(m[0, 0], d[...])
        for side in range(2):
            for p in range(parts):

                @pl.when(i == side * parts + p)
                def _():
                    half = core if side else 1 - core
                    for j in range(units // 128):
                        unit = p * units + j * 128
                        s = 4 * half + unit // block
                        row = unit % block
                        for y in range(2):
                            cut = acc[j * 128 : (j + 1) * 128, y * half_cols // 2 : (y + 1) * half_cols // 2]
                            put_pieces(chunks, [row, block + row], cut, core, y, s)

        pump()

    mine = pl.BlockSpec((1, 1, rows, units), lambda i: (i // parts, i % parts, 0, 0))
    theirs = pl.BlockSpec((1, 1, rows, units), lambda i: (1 - i // parts, i % parts, 0, 0))
    right = pl.BlockSpec((rows, half_cols), lambda i: (0, core), pipeline_mode=pl.Buffered(1))
    pltpu.emit_pipeline(body, grid=(2 * parts,), in_specs=[mine, theirs, right, right])(hid, hid_far, cot, cot_far)


def feed(core, part, n2, cot, fg, fu, fd, hid, ups, acc, begin):
    rows, model = n2.shape
    parts, tile = hid.shape[1], hid.shape[3]
    block = rows // 2

    def body(n2_ref, cot_ref, fg_ref, fu_ref, fd_ref, hid_ref, gg_ref, gu_ref):
        pump = begin()
        for r in range(2):
            at = slice(r * block, (r + 1) * block)
            gate, up = nn(n2_ref[at, :], fg_ref[...]), nn(n2_ref[at, :], fu_ref[...])
            g = nt(cot_ref[at, :], fd_ref[...])
            act, slope = gelu_parts(gate)
            hid_ref[0, 0, at, :] = (act * up).astype(BF16)
            gg_ref[0, 0, at, :] = (g * up * slope).astype(BF16)
            gu_ref[0, 0, at, :] = (g * act).astype(BF16)
        total = nt(gg_ref[0, 0], fg_ref[...]) + nt(gu_ref[0, 0], fu_ref[...])
        if part == 0:

            @pl.when(pl.program_id(0) == 0)
            def _():
                acc[...] = total

            @pl.when(pl.program_id(0) > 0)
            def _():
                acc[...] += total

        else:
            acc[...] += total
        pump()

    unit = lambda i: ((1 - i) * (1 - core) + i * core) * parts + part
    flat = pl.BlockSpec((rows, model), lambda i: (0, 0), pipeline_mode=pl.Buffered(1))
    col = pl.BlockSpec((model, tile), lambda i: (0, unit(i)))
    out = pl.BlockSpec((1, 1, rows, tile), lambda i: (i, part, 0, 0))
    pltpu.emit_pipeline(
        body, grid=(2,), in_specs=[flat, flat, col, col, pl.BlockSpec((tile, model), lambda i: (unit(i), 0))], out_specs=[out, out, out]
    )(n2, cot, fg, fu, fd, hid, ups.at[0], ups.at[1])


def norm_back(core, gn, resid, cot, fgain, gres, low, gain_sum):
    rows, model = gn.shape
    tile = 128
    gain_sum[...] = jnp.zeros_like(gain_sum)

    def body(y_ref, c_ref, out_ref):
        g = fgain[...]

        def norm(i, total):
            at = pl.ds(pl.multiple_of(i * 16, 16), 16)
            place = pl.ds(pl.multiple_of(pl.program_id(0) * tile + i * 16, 16), 16)
            y, d = y_ref[at, :], gn[place, :]
            r = lax.rsqrt(jnp.mean(y * y, axis=-1, keepdims=True) + 1e-06)
            dg, yr = d * g, y * r
            dot = jnp.mean(dg * yr, axis=-1, keepdims=True)
            out = c_ref[at, :].astype(F32) + r * (dg - yr * dot)
            out_ref[at, :] = out
            low[place, :] = out.astype(BF16)
            add = d * yr
            return total + add[0:8] + add[8:16]

        total = lax.fori_loop(0, tile // 16, norm, jnp.zeros((8, model), F32))
        gain_sum[...] += jnp.sum(total, axis=0, keepdims=True)

    row = pl.BlockSpec((tile, model), lambda i: (i, 0))
    pltpu.emit_pipeline(body, grid=(rows // tile,), in_specs=[row, row], out_specs=[row])(resid, cot, gres)


def turn(core, seqs, length, low, ow, gate, state, rate, vec, ggate, lc, q, carry, gj, begin):
    rows, lru = gate.shape
    width = lru // 2

    def body(ow_ref, gate_ref, state_ref, rate_ref, vec_ref, gg_ref, lc_ref, q_ref):
        pump = begin()
        for s in range(seqs):
            gj[s, 0:length, :] = nt(low[s * length : (s + 1) * length, :], ow_ref[...])
        pump()
        slope = -8.0 * vec_ref[3:4, :]
        for s in range(seqs):

            def act(i, _):
                at = pl.ds(pl.multiple_of(s * length + i * 16, 16), 16)
                here = pl.ds(pl.multiple_of(i * 16, 16), 16)
                value, der = gelu_parts(gate_ref[at, :])
                d = gj[s, here, :]
                gg_ref[0, at, :] = (d * state_ref[at, :] * der).astype(BF16)
                gj[s, here, :] = d * value
                return 0

            lax.fori_loop(0, length // 16, act, 0)
            pump()

        row = lax.broadcasted_iota(jnp.int32, (8, width), 0)
        tiles = length // 8

        def scan(k, last):
            i = tiles - 1 - k
            out = []
            for s in range(seqs):
                at = pl.ds(pl.multiple_of(s * length + i * 8, 8), 8)
                g = gj[s, pl.ds(pl.multiple_of(i * 8, 8), 8), :]
                a = jnp.exp(rate_ref[at, :] * slope)
                b = a * g
                for d in (1, 2, 4):
                    keep = row < 8 - d
                    b = b + a * jnp.where(keep, pltpu.roll(b, 8 - d, 0), 0.0)
                    a = a * jnp.where(keep, pltpu.roll(a, 8 - d, 0), 1.0)
                ap, bp = last[s]
                b = b + a * bp
                a = a * ap
                lc_ref[at, :] = g + jnp.where(row < 7, pltpu.roll(b, 7, 0), bp)
                q_ref[at, :] = jnp.where(row < 7, pltpu.roll(a, 7, 0), ap)
                out.append((a[0:1], b[0:1]))
            return tuple(out)

        init = tuple((jnp.ones((1, width), F32), jnp.zeros((1, width), F32)) for _ in range(seqs))
        last = lax.fori_loop(0, tiles, scan, init)
        for s in range(seqs):
            carry[group(core), 0, s : s + 1, :] = last[s][0]
            carry[group(core), 1, s : s + 1, :] = last[s][1]
        pump()

    grp = lambda i: (1 - i) * (1 - core) + i * core
    col = lambda r: pl.BlockSpec((r, width), lambda i: (0, grp(i)))
    pltpu.emit_pipeline(
        body, grid=(2,),
        in_specs=[
            pl.BlockSpec((width, ow.shape[1]), lambda i: (grp(i), 0)), col(rows), col(rows), col(rows), col(8),
        ],
        out_specs=[pl.BlockSpec((1, rows, width), lambda i: (i, 0, 0)), col(rows), col(rows)],
    )(ow, gate, state, rate, vec, ggate, lc, q)


def gates_back(
    own, core, seqs, length, lc, q, cin, states, entry, rate, inlet, mixed, branch, edge, wr, wi, taps, vec,
    gb, head, tail, blocks, rate_sum, inlet_sum, sums_out, dr, di, gr, gi, gm, ext, begin,
):
    rows, lru = lc.shape
    width, bw_ = lru // 2, wr.shape[-1]
    per, sub = width // bw_, dr.shape[-1]

    def body(
        lc_ref, q_ref, state_ref, e_ref, rate_ref, inlet_ref, mixed_ref, branch_ref, edge_ref, wr_ref, wi_ref, taps_ref, vec_ref,
        gb_ref,
    ):
        pump = begin()
        mine = group(core)
        slope = -8.0 * vec_ref[3:4, :]
        zero = jnp.zeros((8, width), F32)
        row = lax.broadcasted_iota(jnp.int32, (16, width), 0)

        sums = (zero, zero, zero)
        for s in range(seqs):
            c_in, ent = cin[mine, s : s + 1, :], e_ref[s]

            def gates(i, carry):
                (before, t0, t1, t2) = carry
                at = pl.ds(pl.multiple_of(s * length + i * 16, 16), 16)
                state = state_ref[at, :]
                prev = jnp.where(row > 0, pltpu.roll(state, 1, 0), before)
                carried = lc_ref[at, :] + q_ref[at, :] * c_in
                rt, it, mx = rate_ref[at, :], inlet_ref[at, :], mixed_ref[at, :].astype(F32)
                log_decay = rt * slope
                decay = jnp.exp(log_decay)
                gap = drop(log_decay, decay)
                inv = lax.rsqrt(gap)
                nf = gap * inv
                im = it * mx
                g_log = carried * decay * (prev - im * decay * inv)
                cn = carried * nf
                g_rt = g_log * slope * (rt * (1.0 - rt))
                g_it = cn * im * (1.0 - it)
                gr[at, :] = g_rt.astype(BF16)
                gi[at, :] = g_it.astype(BF16)
                gm[s, pl.ds(pl.multiple_of(i * 16, 16), 16), :] = cn * it
                lr = g_log * rt
                return (state[15:16], t0 + lr[0:8] + lr[8:16], t1 + g_rt[0:8] + g_rt[8:16], t2 + g_it[0:8] + g_it[8:16])

            _, *sums = lax.fori_loop(0, length // 16, gates, (ent, *sums))
            pump()
        down = lambda v: jnp.sum(v, axis=0, keepdims=True)
        lanes = pl.ds(pl.multiple_of(mine * width, 128), width)
        sums_out[4:5, lanes] = down(sums[0]) * (-8.0 * vec_ref[4:5, :])
        sums_out[5:6, lanes] = down(sums[1])
        sums_out[6:7, lanes] = down(sums[2])

        for g in range(width // sub):
            cols = slice(g * sub, (g + 1) * sub)
            spread(dr, [wr_ref[g * 4 + a] for a in range(4)], 4, bw_)
            spread(di, [wi_ref[g * 4 + a] for a in range(4)], 4, bw_)
            back = nt(gr[:, cols], dr[...]) + nt(gi[:, cols], di[...])
            rs = tn(mixed_ref[:, cols], gr[:, cols])
            is_ = tn(mixed_ref[:, cols], gi[:, cols])
            for a in range(4):
                block = slice(a * bw_, (a + 1) * bw_)
                if own:
                    blocks[mine * per + g * 4 + a, :, 0:bw_] = rs[block, block].astype(BF16)
                    blocks[2 * per + mine * per + g * 4 + a, :, 0:bw_] = is_[block, block].astype(BF16)
                else:
                    rate_sum[mine * per + g * 4 + a] = rs[block, block]
                    inlet_sum[mine * per + g * 4 + a] = is_[block, block]
            for s in range(seqs):
                gm[s, 0:length, cols] += back[s * length : (s + 1) * length]
        pump()

        for s in range(seqs):
            gm[s, length : length + 8, :] = zero
            ext[s, 0:8, :] = edge_ref[16 * s : 16 * s + 16].astype(F32)[8:16]
            ext[s, 8 : 8 + length, :] = branch_ref[s * length : (s + 1) * length].astype(F32)
            head[mine, 8 * s : 8 * s + 8, :] = gm[s, 0:8, :]

        tap = [taps_ref[k : k + 1, :] for k in range(4)]
        acc = (zero,) * 5
        for s in range(seqs):

            def conv(i, acc):
                lo = pl.multiple_of(i * 16, 16)
                y = gm[s, pl.ds(lo, 24), :]
                x = ext[s, pl.ds(lo, 24), :]
                total = tap[0] * y[0:16]
                for k in range(1, 4):
                    total = total + tap[k] * y[k : k + 16]
                gb_ref[0, pl.ds(pl.multiple_of(s * length + i * 16, 16), 16), :] = total.astype(BF16)
                now = y[0:16]
                new = []
                for k in range(4):
                    prod = now * x[8 - k : 24 - k]
                    new.append(acc[k] + prod[0:8] + prod[8:16])
                new.append(acc[4] + now[0:8] + now[8:16])
                return tuple(new)

            acc = lax.fori_loop(0, length // 16, conv, acc)
            y = gm[s, length - 16 : length + 8, :]
            total = tap[0] * y[0:16]
            for k in range(1, 4):
                total = total + tap[k] * y[k : k + 16]
            tail[mine, 16 * s : 16 * s + 16, :] = total
            pump()
        for k in range(4):
            sums_out[k : k + 1, lanes] = down(acc[k])
        sums_out[7:8, lanes] = down(acc[4])

    grp = lambda i: (1 - i) * (1 - core) + i * core
    col = lambda r: pl.BlockSpec((r, width), lambda i: (0, grp(i)))
    blk = pl.BlockSpec((per, bw_, bw_), lambda i: (grp(i), 0, 0))
    pltpu.emit_pipeline(
        body, grid=(2,),
        in_specs=[
            col(rows), col(rows), col(rows), pl.BlockSpec((seqs, 1, width), lambda i: (0, 0, grp(i))),
            col(rows), col(rows), col(rows), col(rows), col(edge.shape[0]), blk, blk, col(4), col(8),
        ],
        out_specs=[pl.BlockSpec((1, rows, width), lambda i: (i, 0, 0))],
    )(lc, q, states, entry, rate, inlet, mixed, branch, edge, wr, wi, taps, vec, gb)


def spaced(exchange, name, steps):
    def begin():
        place = iter(range(64))

        def pump():
            j = next(place)
            for i in range(steps):
                if PLAN.get(f"{name}{i}{j}"):

                    @pl.when(pl.program_id(0) == i)
                    def _():
                        exchange.at(f"{name}{i}{j}")

        return pump

    return begin


def no_pump():
    return lambda: None


ANY = pl.BlockSpec(memory_space=pl.ANY)
INSIDE = pl.BlockSpec(memory_space=pltpu.VMEM)


KINDS = "AFEAFEAFEAFE"
PLAN = {
    "u000": [(-1, 0)],
    "u010": [(-1, 1)],
    "f200": [(0, 0), (0, 1)],
    "u100": [(-1, 2)],
    "u110": [(1, 0), (-1, 3), (1, 1)],
    "u200": [(-1, 4)],
    "d00": [(2, 0), (2, 1)],
    "d40": [(3, 0), (3, 1), (0, 2), (-1, 5)],
    "t00": [(4, 0), (4, 1), (0, 3), (-1, 6)],
    "t01": [(1, 2)],
    "t02": [(5, 0), (5, 1), (0, 4), (-1, 7)],
    "t12": [(2, 2)],
    "b1": [(3, 2), (1, 3), (0, 5), (-1, 8)],
    "b2": [(1, 4)],
    "g01": [(4, 2), (0, 6), (-1, 9)],
    "g02": [(2, 3), (2, 4)],
    "g03": [(5, 2), (0, 7)],
    "g10": [(1, 5)],
    "g11": [(3, 3), (3, 4)],
    "c1": [(-1, 10), (4, 3), (4, 4), (2, 5), (1, 6), (1, 7), (0, 8), (6, 0)],
    "c3": [(5, 3), (5, 4), (6, 1)],
    "c4": [(-1, 11), (3, 5)],
    "i00": [(2, 6), (2, 7), (0, 9)],
    "i10": [(4, 5)],
    "i30": [(5, 5)],
    "o00": [(3, 6), (3, 7), (1, 8), (6, 2)],
    "o10": [(7, 0)],
    "drain": [(4, 6), (4, 7), (0, 10), (7, 1), (5, 6), (5, 7), (6, 3), (2, 8), (0, 11), (1, 9), (7, 2), (3, 8), (6, 4), (6, 5), (4, 8), (1, 10), (7, 3), (6, 6), (2, 9), (5, 8), (6, 7), (1, 11), (7, 4), (3, 9), (6, 8), (2, 10), (4, 9), (5, 9), (2, 11), (3, 10), (6, 9), (3, 11), (4, 10), (6, 10), (5, 10), (4, 11), (5, 11)],
}

PARTS = [256] * 9 + [384] * 3
SWAPS = 10


def backward(own, seqs, length, seq_n, batch_n, grads_in, values, collective_id):
    (
        n2, resid, cot, fgain, ow, gate, state, entry, rate, vec, inlet, mixed, branch, edge, wr, wi, taps, gw, bw, tok, mgain,
        fg, fu, fd, joined, normed,
    ) = values
    rows, model = n2.shape
    lru, units = gate.shape[1], fd.shape[0]
    width, bw_ = lru // 2, wr.shape[-1]
    per, sub = width // bw_, 4 * bw_
    steps = [("batch", 1 << k) for k in range(batch_n.bit_length() - 1)] + [("seq", 1 << k) for k in range(seq_n.bit_length() - 1)]
    n_steps = len(steps)
    parts, unit = 3, units // 6
    if not own:
        grads_in = []

    def kernel(*refs):
        refs = list(refs)
        cut = lambda n: [refs.pop(0) for _ in range(n)]
        far_in = cut(len(grads_in))
        (
            n2, resid, cot, fgain, ow, gate, state, entry, rate, vec, inlet, mixed, branch, edge, wr, wi, taps, gw, bw, tok, mgain,
            fg, fu, fd, joined, normed,
        ) = cut(26)
        tokens_grad, block_out, totals, gres, low_out, low_far, ggate, ggate_far, lc, q, gb, gb_far, hid, hid_far, ups, ups_far, n2_far, joined_far = cut(18)
        fin, block_total = cut(2) if own else (None, None)
        rate_sum, inlet_sum = (None, None) if own else cut(2)
        low, carry, got, cin, dr, di, gr, gi, gm, ext, head, tail, ahead, fixed, gain_sum, acc, small, gn = cut(18)
        send, recv, swap_send, swap_recv, one, local, s_send, s_recv = cut(8)

        core = core_of()
        seq, bat = lax.axis_index("seq"), lax.axis_index("batch")
        other = (seq, bat + 1 - 2 * core)
        peers = [(flip(seq, bit), bat) if axis == "seq" else (seq, flip(bat, bit)) for axis, bit in steps]
        exchange, blocks = None, None
        if own:
            g0, g1, g2, *bufs, x_send, x_recv = cut(9)
            blocks, *block_bufs, b_send, b_recv = cut(8)
            places = [(ref, row) for row in (0, 256, 512) for ref in (g0, g1)] + [(g2, 0), (g2, 256), (g2, 512), (g0, 0), (g0, 384), (g1, 0)]
            chunks = [(ref, row, part, kind) for (ref, row), part, kind in zip(places, PARTS, KINDS)]
            exchange = Exchange(chunks, bufs, fin, x_send, x_recv)
            exchange.further[6] = BlockSums(blocks, block_bufs, block_total, b_send, b_recv).events()
            blocks[...] = jnp.zeros_like(blocks)
        small[0] = jnp.zeros((16, lru), F32)
        all_peers = [(lax.rem(seq + k, seq_n), bat) for k in range(1, seq_n)] + [peer for peer, step in zip(peers, steps) if step[0] == "batch"]
        greet(all_peers)

        def swap(j, src, dst):
            return pltpu.make_async_remote_copy(
                src_ref=src, dst_ref=dst, send_sem=swap_send.at[j], recv_sem=swap_recv.at[j], device_id=other, device_id_type=MESH
            )

        at = exchange.at if own else (lambda place: None)
        plan = lambda name, steps: spaced(exchange, name, steps) if own else no_pump
        run_feed = lambda p, begin: feed(core, p, n2, cot, fg, fu, fd, hid, ups, gn, begin)
        if own:
            cot_far, normed_far = far_in
            n2_swap, joined_swap = swap(4, n2, n2_far), swap(5, joined, joined_far)
            ups_swaps = [swap(6 + p, ups.at[:, 0, p], ups_far.at[:, p]) for p in range(parts)]
            hid_swap = swap(9, hid, hid_far)
            run_up = lambda p: wgrad_up(core, chunks[2 * p], chunks[2 * p + 1], n2, n2_far, ups.at[:, 1, p], ups_far.at[:, p], plan(f"u{p}", 2))

            def opening():
                def pump():
                    @pl.when(pl.program_id(0) == 0)
                    def _():
                        met(len(all_peers))
                        n2_swap.start()

                return pump

            run_feed(0, opening)
            ups_swaps[0].start()
            joined_swap.start()
            n2_swap.wait()
            ups_swaps[0].wait()
            run_up(0)
            run_feed(1, plan("f1", 2))
            ups_swaps[1].start()
            run_feed(2, plan("f2", 2))
            ups_swaps[2].start()
            hid_swap.start()
            ups_swaps[1].wait()
            run_up(1)
            ups_swaps[2].wait()
            run_up(2)
            joined_swap.wait()
            hid_swap.wait()
            wgrad_down(core, chunks[6:9], hid, hid_far, cot, cot_far, plan("d", 2 * parts))
        else:
            met(len(all_peers))
            for p in range(parts):
                run_feed(p, no_pump)
        norm_back(core, gn, resid, cot, fgain, gres, low, gain_sum)
        at("a4")
        keep = pltpu.make_async_copy(low, low_out, one)
        keep.start()
        low_swap = swap(0, low, low_far)
        low_swap.start()
        turn(
            core, seqs, length, low, ow, gate, state, rate, vec, ggate, lc, q, carry, gm,
            plan("t", 2),
        )
        gate_swap = swap(1, ggate.at[0], ggate_far)
        gate_swap.start()
        arriving = Entry(carry, got, seq_n, send, recv)
        arriving.start()
        keep.wait()
        low_swap.wait()
        if own:
            at("b0")
            exchange.free(0)
            exchange.free(2)
            wgrad(core, chunks[9:10], joined, joined_far, low_out, low_far, False)
            at("b1")
        arriving.finish(cin, True)
        gate_swap.wait()
        at("b2")
        gates_back(
            own, core, seqs, length, lc, q, cin, state, entry, rate, inlet, mixed, branch, edge, wr, wi, taps, vec,
            gb, head, tail, blocks, rate_sum, inlet_sum, small.at[0], dr, di, gr, gi, gm, ext,
            plan("g", 2),
        )

        to_left = pltpu.make_async_remote_copy(
            src_ref=head, dst_ref=ahead, send_sem=swap_send.at[2], recv_sem=swap_recv.at[2],
            device_id=(lax.rem(seq + seq_n - 1, seq_n), bat), device_id_type=MESH,
        )
        to_left.start()
        if own:
            at("c0")
            exchange.free(4)
            wgrad(core, chunks[10:11], normed, normed_far, ggate.at[1], ggate_far, True)
            at("c1")
        to_left.wait()
        weight = (seq < seq_n - 1).astype(F32)
        copies = []
        for i in range(2):
            mine = (1 - i) * (1 - core) + i * core
            for s in range(seqs):
                y = ahead[mine, 8 * s : 8 * s + 8, :] * weight
                t = tail[mine, 16 * s : 16 * s + 16, :]
                grown = jnp.concatenate([jnp.zeros((16, width), F32), y], axis=0)
                for k in range(1, 4):
                    t = t + taps[k : k + 1, pl.ds(pl.multiple_of(mine * width, 128), width)] * grown[k : k + 16]
                fixed[i, 16 * s : 16 * s + 16, :] = t.astype(BF16)
                copy = pltpu.make_async_copy(
                    fixed.at[i, 16 * s : 16 * s + 16], gb.at[i, (s + 1) * length - 16 : (s + 1) * length], local.at[i, s]
                )
                copy.start()
                copies.append(copy)
        for copy in copies:
            copy.wait()
        branch_swap = swap(3, gb.at[0], gb_far)
        branch_swap.start()
        at("c2")
        branch_swap.wait()
        at("c3")
        if own:
            exchange.free(1)
            exchange.free(3)
            wgrad(core, chunks[11:12], normed, normed_far, gb.at[1], gb_far, True)
            at("c4")

        begin = plan("i", 4)
        tile = 128
        acc[...] = jnp.zeros_like(acc)

        def input_grad(gg_ref, gb_ref, gwt, gwm, bwt, bwm, x_ref, gr_ref, out):
            pump = begin()
            d = nt(gg_ref[0], gwt[...]) + nt(gg_ref[1], gwm[...]) + nt(gb_ref[0], bwt[...]) + nt(gb_ref[1], bwm[...])
            x = x_ref[...].astype(F32)
            r = lax.rsqrt(jnp.mean(x * x, axis=-1, keepdims=True) + 1e-06)
            xr, dg = x * r, d * mgain[...]
            out[...] = gr_ref[...] + r * (dg - xr * jnp.mean(dg * xr, axis=-1, keepdims=True))
            acc[...] += jnp.sum(d * xr, axis=0, keepdims=True)
            pump()

        row = pl.BlockSpec((tile, model), lambda i: (i, 0))
        pair = pl.BlockSpec((2, tile, width), lambda i: (0, i, 0))
        side = lambda c: pl.BlockSpec((model, width), lambda i: (0, c), pipeline_mode=pl.Buffered(1))
        pltpu.emit_pipeline(
            input_grad, grid=(rows // tile,), in_specs=[pair, pair, side(1 - core), side(core), side(1 - core), side(core), row, row], out_specs=[row]
        )(ggate, gb, gw, gw, bw, bw, tok, gres, tokens_grad)

        small[0, 8:9, 0:model] = acc[...]
        small[0, 9:10, 0:model] = gain_sum[...]

        def small_step(k):
            return pltpu.make_async_remote_copy(
                src_ref=small.at[0], dst_ref=small.at[k + 1], send_sem=s_send.at[k], recv_sem=s_recv.at[k],
                device_id=peers[k], device_id_type=MESH,
            )

        def small_event(k):
            small_step(k).wait()
            small[0] = small[0] + small[k + 1]
            if k + 1 < n_steps:
                small_step(k + 1).start()

        small_events = [functools.partial(small_event, k) for k in range(n_steps)]
        small_step(0).start()
        if own:
            exchange.further[7] = small_events
        begin_out = plan("o", 4)
        tile_out = 256

        def last(r, *rest):
            pump = begin_out()
            hid_refs, down_refs, out = rest[: 2 * parts], rest[2 * parts : 4 * parts], rest[-1]
            total = r[...]
            for l, w in zip(hid_refs, down_refs):
                total = total + nn(l[0, 0], w[...])
            out[...] = total.astype(BF16)
            pump()

        col = pl.BlockSpec((rows, tile_out), lambda i: (0, i))
        order = [(side, p) for side in range(2) for p in range(parts)]
        hid_spec = lambda side, p: pl.BlockSpec((1, 1, rows, unit), lambda i: (side, p, 0, 0), pipeline_mode=pl.Buffered(1))
        down_spec = lambda half, p: pl.BlockSpec((unit, tile_out), lambda i: (half * parts + p, i))
        pltpu.emit_pipeline(
            last, grid=(model // tile_out,),
            in_specs=[col] + [hid_spec(*o) for o in order] + [down_spec(core if side else 1 - core, p) for side, p in order], out_specs=[col],
        )(resid, *([hid] * 2 * parts), *([fd] * 2 * parts), block_out)
        if own:
            exchange.drain()
        else:
            for event in small_events:
                event()
        totals[...] = small[0]

    f = lambda *shape: jax.ShapeDtypeStruct(shape, F32)
    b = lambda *shape: jax.ShapeDtypeStruct(shape, BF16)
    vm, dma = pltpu.VMEM, lambda *shape: pltpu.SemaphoreType.DMA(shape)
    out_shape = [
        f(rows, model), b(rows, model), f(16, lru),
        f(rows, model), b(rows, model), b(rows, model), b(2, rows, width), b(rows, width), f(rows, lru), f(rows, lru), b(2, rows, width), b(rows, width),
        b(2, parts, rows, unit), b(2, parts, rows, unit), b(2, 2, parts, rows, unit), b(2, parts, rows, unit), b(rows, model), b(rows, lru),
    ]
    out_specs = [ANY, ANY, INSIDE] + [ANY] * 15
    scratch = [
        vm((rows, model), BF16), vm((2, 2, seqs, width), F32), vm((seq_n, 2, 2, seqs, width), F32), vm((2, seqs, width), F32),
        vm((sub, sub), BF16), vm((sub, sub), BF16), vm((rows, width), BF16), vm((rows, width), BF16),
        vm((seqs, length + 8, width), F32), vm((seqs, length + 8, width), F32), vm((2, 8 * seqs, width), F32), vm((2, 16 * seqs, width), F32),
        vm((2, 8 * seqs, width), F32), vm((2, 16 * seqs, width), BF16), vm((1, model), F32), vm((1, model), F32), vm((n_steps + 1, 16, lru), F32), vm((rows, model), F32),
        dma(seq_n), dma(seq_n), dma(SWAPS), dma(SWAPS), pltpu.SemaphoreType.DMA, dma(2, seqs), dma(n_steps), dma(n_steps),
    ]
    if own:
        out_shape += [b(2, 2, sum(PARTS), 128), b(4 * per, bw_, 128)]
        out_specs += [INSIDE, INSIDE]
        scratch += [vm((16, 768, 128), BF16)] * 3 + Exchange.scratch(len(PARTS), sum(PARTS))
        scratch += [vm((4 * per, bw_, 128), BF16)] + BlockSums.scratch(bw_)
    else:
        out_shape += [f(*wr.shape), f(*wi.shape)]
        out_specs += [INSIDE, INSIDE]
    ins = [ANY] * (len(grads_in) + len(values))
    for j in (3, 16, 20):
        ins[len(grads_in) + j] = INSIDE
    return pl.pallas_call(
        kernel,
        in_specs=ins,
        out_specs=out_specs,
        out_shape=out_shape,
        scratch_shapes=scratch,
        compiler_params=pltpu.CompilerParams(collective_id=collective_id, has_side_effects=True, vmem_limit_bytes=60 * 2**20),
        name="backward",
    )(*grads_in, *values)


def lay(sums, totals, blocks, model, lru, units, n):
    shapes = [(model // n, units), (model // n, units), (units // n, model), (lru // n, model), (model // n, lru), (model // n, lru)]
    rows = sums.shape[2]
    count, wide_b = blocks.shape[0] // 2, blocks.shape[1]

    def kernel(v, b, s, rate, inlet, taps, decay, rate_off, inlet_off, conv_off, gain1, gain2, *outs):
        taps[...] = s[0:4, :]
        for j, vector in enumerate((decay, rate_off, inlet_off, conv_off)):
            vector[...] = s[4 + j, :]
        gain1[...] = s[8, 0:model]
        gain2[...] = s[9, 0:model]
        for y in range(2):
            for m, out in enumerate(outs):
                part, wide = out.shape
                for t in range(wide // 256):
                    if m < 2:
                        at, col = t // 2 * 512 + m * 256 + t % 2 * 128, t // 2 * 512 + y * 256 + t % 2 * 128
                    else:
                        at, col = 1536 + [0, 768, 1152, 1536][m - 2] + t * part, y * wide // 2 + t * 128
                    out[:, col : col + 128] = v[0, y, at : at + part, :].astype(F32)
        for j in range(count // 2):
            rate[j] = b[0, j, :, 0:wide_b].astype(F32)
            inlet[j] = b[1, j, :, 0:wide_b].astype(F32)

    block = pl.BlockSpec((count // 2, wide_b, wide_b), lambda i: (i, 0, 0))
    flat = lambda size: (pl.BlockSpec((size,), lambda i: (0,)), jax.ShapeDtypeStruct((size,), F32))
    vectors = [(whole((4, lru)), jax.ShapeDtypeStruct((4, lru), F32))] + [flat(lru)] * 4 + [flat(model)] * 2
    return pl.pallas_call(
        kernel,
        grid=(2,),
        in_specs=[pl.BlockSpec((1, 2, rows, 128), lambda i: (i, 0, 0, 0)), pl.BlockSpec((2, count // 2, wide_b, 128), lambda i: (0, i, 0, 0)), whole(totals.shape)],
        out_specs=[block, block] + [v[0] for v in vectors] + [pl.BlockSpec((part, wide // 2), lambda i: (0, i)) for part, wide in shapes],
        out_shape=[jax.ShapeDtypeStruct((count, wide_b, wide_b), F32)] * 2 + [v[1] for v in vectors] + [jax.ShapeDtypeStruct(shape, F32) for shape in shapes],
        compiler_params=params(),
        name="lay",
    )(sums, blocks.reshape(2, count, wide_b, 128), totals)


def swap(value):
    count = lax.axis_size("batch")
    return lax.ppermute(value, "batch", [(i, i ^ 1) for i in range(count)])


def local(
    tokens, cotangent, gate_weight, branch_weight, out_weight, conv_taps, conv_offset, rate_weight, inlet_weight,
    rate_offset, inlet_offset, decay_param, mixer_gain, feed_gain, feed_gate, feed_up, feed_down,
):
    seqs, length, model = tokens.shape
    lru, units = gate_weight.shape[1], feed_gate.shape[1]
    rows = seqs * length
    seq_n, batch_n = lax.axis_size("seq"), lax.axis_size("batch")
    core = lax.rem(lax.axis_index("batch"), 2)

    tok, cot = tokens.reshape(rows, model), cotangent.reshape(rows, model)
    cot_far = swap(cot)
    none = jnp.zeros_like(conv_offset)
    vec = jnp.stack(
        [conv_offset, rate_offset, inlet_offset, jax.nn.softplus(decay_param), jax.nn.sigmoid(decay_param), none, none, none]
    )
    gain1, gain2 = mixer_gain[None], feed_gain[None]

    normed, gate, branch, edge, mixed, rate, inlet, h, p, entry = front(
        tok, gain1, gate_weight, branch_weight, conv_taps, vec, rate_weight, inlet_weight, seqs, length, seq_n, 0
    )
    normed_far = swap(normed)
    joined, resid, normed_two, state = join(tok, gate, h, p, entry, out_weight, gain2, seqs, length)

    own = (seq_n, batch_n) == (8, 4)
    tokens_grad, out, totals, _, grad_low, _, ggate, _, _, _, gb, _, hid, _, ups, _, _, _, *sums = backward(
        own, seqs, length, seq_n, batch_n, [cot_far, normed_far],
        [
            normed_two, resid, cot, gain2, out_weight, gate, state, entry, rate, vec, inlet, mixed, branch, edge,
            rate_weight, inlet_weight, conv_taps, gate_weight, branch_weight, tok, gain1, feed_gate, feed_up, feed_down, joined, normed,
        ],
        1,
    )
    if own:
        rate_all, inlet_all, *vectors = lay(sums[0], totals, sums[1], model, lru, units, seq_n)
        vectors, (gate_feed_all, up_feed_all, down_all, out_all, gate_all, branch_all) = vectors[:7], vectors[7:]
    else:
        vectors = [totals[0:4], *totals[4:8], totals[8, :model], totals[9, :model]]
        rate_all, inlet_all = lax.psum((sums[0], sums[1]), ("seq", "batch"))

        def full(pair):
            pair = pair if pair.ndim == 4 else pair[:, None]
            pair = jnp.where(core == 0, pair[::-1], pair)
            return pair.transpose(2, 0, 1, 3).reshape(rows, -1)

        def total(left, right):
            return lax.psum(lax.psum_scatter(tn(left, right), "seq", scatter_dimension=0, tiled=True), "batch")

        down_all = total(full(hid), cot)
        gate_feed_all, up_feed_all = total(normed_two, full(ups[0])), total(normed_two, full(ups[1]))
        out_all = total(joined, grad_low)
        gate_all, branch_all = total(normed, full(ggate)), total(normed, full(gb))

    return (
        out.reshape(seqs, length, model), tokens_grad.reshape(seqs, length, model), gate_all, branch_all, out_all,
        vectors[0], vectors[4], rate_all, inlet_all, vectors[2], vectors[3], vectors[1], vectors[5], vectors[6],
        gate_feed_all, up_feed_all, down_all,
    )


def solution(mesh):
    big = P("batch", "seq", None)
    in_specs = (big, big) + (P(),) * 15
    out_specs = (big, big) + (P("seq", None),) * 3 + (P(),) * 9 + (P("seq", None),) * 3
    return jax.shard_map(local, mesh=mesh, in_specs=in_specs, out_specs=out_specs, check_vma=False)
```
